32 devices in a mesh: seq: 16 (over z, y, core), row: 2 (over x).
Axes of the slice: x: 2, y: 2, z: 4, core: 2. Of those that a mesh axis runs over, the one named last changes fastest.
Arguments:
- layer_input: bfloat16 [2, 16384, 384], P('row', 'seq'), may hold values from -6 to 6
- segment_ids: int32 [2, 16384], P('row', 'seq'), may hold values from 0 to 63, never falling along the last dimension, each value on 1 to 512 neighbouring positions
- out_grad: bfloat16 [2, 16384, 384], P('row', 'seq'), may hold values from -6 to 6
- weights: float32 [1971840], P(('seq', 'row')), may hold values from -3 to 3
- momentum: float32 [1971840], P(('seq', 'row')), may hold values from -271.529 to 271.529
- average: float32 [1971840], P(('seq', 'row')), may hold values from -3 to 3
Outputs:
- block_output: bfloat16 [2, 16384, 384], P('row', 'seq')
- input_grad: float32 [2, 16384, 384], P('row', 'seq')
- weight_grad: float32 [1971840], P(('seq', 'row'))
- new_momentum: float32 [1971840], P(('seq', 'row'))
- new_average: float32 [1971840], P(('seq', 'row'))
- new_weights: float32 [1971840], P(('seq', 'row'))
- weight_copy: bfloat16 [1971840], P(('seq', 'row'))
The draws below stay inside these ranges and needn't reach their ends.
Inputs may be any that keep to these rules, and one draw needn't show every extreme that they name: `segment_ids`: ids never fall along a row; every document holds 1 to 512 tokens and one of each row holds exactly 512.
All inputs are finite; a program needn't handle non-finite values.
Results may differ from the reference program's by a relative error of at most 0.012.
The reference program's roundings to bfloat16 on the way count: a program that leaves them out, or rounds other values in their place, can miss the bound.
Values may be sent and summed in bfloat16 or wider, within the bound.
A program may use at most 128 MiB of HBM per device.

```python
import math
import jax
import jax.numpy as jnp
import numpy as np
from jax import lax

D = 384
HEADS = 6
HEAD_DIM = 64
FF = 1536
SPAN = 256
LAYERS = 1
QBLOCK = 512
ROWS = 2
SEQLEN = 16384
ALL_TOK = 32768
MAXDOC = 512
DOCS = 64
RAW_PARAMS = 1971840
NPARAM = 1971840


def flat_layout():
    root_width = 1.0 / math.sqrt(D)
    per_layer = [(D * D, root_width, 0.1, 0), (D * D, root_width, 0.1, 0), (D * D, root_width, 0.3, 0), (D * D, 3.0 * root_width, 0.3, 0), (D * FF, root_width, 0.2, 0), (FF * D, 1.5 / math.sqrt(FF), 0.3, 0), (D, 0.3, 0.5, 0), (D, 0.3, 0.5, 0), (D, 0.3, 0.5, 0), (D, 0.3, 0.5, 0), (D, 0.0, 0.5, 1), (D, 0.3, 0.5, 0), (FF, 0.3, 0.3, 0), (D, 0.3, 0.5, 0), (D, 0.0, 0.5, 1), (D, 0.3, 0.5, 0)]
    pieces = []
    for layer_index in range(LAYERS):
        pieces = pieces + per_layer
    pieces = pieces + [(2 * SPAN * D, root_width, 0.01 * math.sqrt(D), 0), (D, 0.0, 0.5, 1), (D, 0.3, 0.5, 0)]
    if NPARAM > RAW_PARAMS:
        pieces = pieces + [(NPARAM - RAW_PARAMS, 0.3, 0.3, 0)]
    return pieces


def spread_values(key, use_grads, gain_width):
    parts_out = []
    for position, (amount, value_scale, grad_scale, gain_flag) in enumerate(flat_layout()):
        sub_key = jax.random.fold_in(key, position)
        bell_curve = jax.random.truncated_normal(sub_key, -3.0, 3.0, (amount,), jnp.float32)
        even_part = jax.random.uniform(jax.random.fold_in(sub_key, 7), (amount,), jnp.float32, -1.0, 1.0)
        blended = bell_curve
        if use_grads:
            values = blended * (grad_scale * math.sqrt(ALL_TOK))
        elif gain_flag:
            values = 1.0 + 0.5 * gain_width * even_part
        else:
            values = blended * value_scale
        parts_out.append(values)
    return jnp.concatenate(parts_out)


def draw_weights(key, part):
    key = jax.random.fold_in(key, 101)
    gain_width = 0.8
    return spread_values(key, False, gain_width)


def draw_momentum(key, part):
    key = jax.random.fold_in(key, 102)
    return spread_values(key, True, 0.8)


def draw_average(key, part):
    key = jax.random.fold_in(key, 103)
    gain_width = 0.8
    return spread_values(key, False, gain_width)


def levels(stream_key, dims, cuts, smallest, top_value):
    def one(axis_at, shards_of):
        heights = jax.random.uniform(jax.random.fold_in(jax.random.fold_in(stream_key, 6), axis_at), (shards_of,), jnp.float32, smallest / len(cuts), top_value / len(cuts))
        return jnp.repeat(jnp.exp(heights), dims[axis_at] // shards_of).reshape((-1,) + (1,) * (len(dims) - axis_at - 1))

    level = one(*cuts[0])
    for cut in cuts[1:]:
        level = level * one(*cut)
    return level


def length_profile(number_of, total, reach, slope):
    loads = [(1 << 20) // math.isqrt(grade ** slope) + 1 for grade in range(2, number_of + 1)]
    rest, counts = total - reach - (number_of - 1), [1] * (number_of - 1)
    while rest > 0:
        movable = [i for i in range(number_of - 1) if counts[i] < reach]
        pool, remaining = sum([loads[i] for i in movable]), rest
        for i in movable:
            addition = min(reach - counts[i], max(1, remaining * loads[i] // pool), rest)
            counts[i] = counts[i] + addition
            rest = rest - addition
    return np.array([reach] + counts)


def ragged_sizes(own_key, count, total, limit, slope):
    if count == 2:
        one = jax.random.randint(own_key, (), max(1, total - limit), min(limit, total - 1) + 1)
        return jnp.stack([one, total - one])
    sizes = jnp.asarray(length_profile(count, total, limit, slope), jnp.int32)
    twos = (count - 1) // 2
    source_of, sink = sizes[1:1 + 2 * twos:2], sizes[2:2 + 2 * twos:2]
    margin = jnp.minimum(source_of - 1, limit - sink)
    moved = jax.random.randint(jax.random.fold_in(own_key, 1), (twos,), 0, 1 << 20) % (margin + 1)
    sizes = sizes.at[1:1 + 2 * twos:2].set(source_of - moved).at[2:2 + 2 * twos:2].set(sink + moved)
    return sizes[jax.random.permutation(jax.random.fold_in(own_key, 2), count)]


def scatter_about(rng, shape, deviation, limit, shards=(), held_as=jnp.bfloat16):
    factor_of = levels(rng, shape, shards, -0.22, 0.18) if shards else 1.0
    result = jax.random.normal(rng, shape, jnp.float32) * deviation * factor_of
    return jnp.minimum(jnp.maximum(result, -limit), limit).astype(held_as)


def setup_inputs(seed: int = 0) -> dict:
    arg_keys = jax.random.split(jax.random.key(seed), 7)
    return {
        "layer_input": scatter_about(arg_keys[0], (ROWS, SEQLEN, D), 1.0, 6.0, ((0, 2), (1, 16))),
        "segment_ids": jax.vmap(lambda own: jnp.searchsorted(jnp.cumsum(ragged_sizes(own, DOCS, SEQLEN, MAXDOC, 1)), jnp.arange(SEQLEN), side="right"))(jax.random.split(arg_keys[1], ROWS)).reshape((ROWS, SEQLEN)).astype(jnp.int32),
        "out_grad": scatter_about(arg_keys[2], (ROWS, SEQLEN, D), 1.0, 6.0, ((0, 2), (1, 16))),
        "weights": draw_weights(jax.random.fold_in(arg_keys[6], 71), 0),
        "momentum": draw_momentum(jax.random.fold_in(arg_keys[6], 71), 0),
        "average": draw_average(jax.random.fold_in(arg_keys[6], 71), 0),
    }


@jax.custom_vjp
def low(v):
    return lax.optimization_barrier(v.astype(jnp.bfloat16)).astype(jnp.float32)

@jax.custom_vjp
def low_back(v):
    return v

def low_keep(v):
    return (low(v), None)

def low_pass(kept, grad):
    return (grad,)

def back_keep(v):
    return (v, None)

def back_low(kept, grad):
    return (low(grad),)
low.defvjp(low_keep, low_pass)
low_back.defvjp(back_keep, back_low)
TOP_PRECISION = lax.Precision.HIGHEST
EPSILON = 1e-07

def layer_pieces():
    return [('query_w', (D, D)), ('key_w', (D, D)), ('value_w', (D, D)), ('output_w', (D, D)), ('up_w', (D, FF)), ('down_w', (FF, D)), ('query_b', (D,)), ('key_b', (D,)), ('value_b', (D,)), ('output_b', (D,)), ('attn_gain', (D,)), ('attn_shift', (D,)), ('up_bias', (FF,)), ('down_bias', (D,)), ('ffn_gain', (D,)), ('ffn_shift', (D,))]

def unpack(flat_params):
    offset = 0
    layers_list = []
    for layer_index in range(LAYERS):
        weights_of = {}
        for piece_name, extent in layer_pieces():
            amount = math.prod(extent)
            weights_of[piece_name] = flat_params[offset:offset + amount].reshape(extent)
            offset += amount
        layers_list.append(weights_of)
    shared = {}
    for piece_name, extent in (('rel_table', (2 * SPAN, D)), ('rel_gain', (D,)), ('rel_shift', (D,))):
        amount = math.prod(extent)
        shared[piece_name] = flat_params[offset:offset + amount].reshape(extent)
        offset += amount
    return (layers_list, shared)

def matmul(left, right):
    return jnp.dot(left, right, precision=TOP_PRECISION, preferred_element_type=jnp.float32)

def rounded(values):
    return low(low_back(values))

def layer_norm(values, gain, shift):
    centered = values - lax.optimization_barrier(jnp.mean(values, axis=-1, keepdims=True))
    variance = lax.optimization_barrier(jnp.mean(centered * centered, axis=-1, keepdims=True))
    return centered * lax.rsqrt(variance + EPSILON) * gain + shift

def sheared_row_shift(matrix):
    leading = matrix.shape[:-2]
    rows_count, width = matrix.shape[-2:]
    padded = jnp.pad(matrix, [(0, 0)] * len(leading) + [(0, 0), (0, rows_count)])
    flattened = padded.reshape(leading + (rows_count * (width + rows_count),))
    flattened = flattened[..., :rows_count * (width + rows_count - 1)]
    return flattened.reshape(leading + (rows_count, width + rows_count - 1))

def attend_block(block_index, query, key_pad, value_pad, seg_pad, position_key_extended, position_query_flipped):
    per_row = SEQLEN // QBLOCK
    row_index = block_index // per_row
    offset = block_index % per_row * QBLOCK
    key_rows = QBLOCK + 2 * SPAN
    zero_index = jnp.zeros((), jnp.int32)
    query_block_rows = lax.dynamic_slice(query, (row_index, offset, zero_index), (1, QBLOCK, D))[0].reshape(QBLOCK, HEADS, HEAD_DIM)
    key_block_rows = lax.dynamic_slice(key_pad, (row_index, offset, zero_index), (1, key_rows, D))[0].reshape(key_rows, HEADS, HEAD_DIM)
    value_blk = lax.dynamic_slice(value_pad, (row_index, offset, zero_index), (1, key_rows, D))[0].reshape(key_rows, HEADS, HEAD_DIM)
    seg_query = lax.dynamic_slice(seg_pad, (row_index, offset + SPAN), (1, QBLOCK))[0]
    seg_key = lax.dynamic_slice(seg_pad, (row_index, offset), (1, key_rows))[0]
    content = jnp.einsum('ahd,bhd->hab', query_block_rows, key_block_rows, precision=TOP_PRECISION)
    target_position = sheared_row_shift(jnp.einsum('igk,ogk->gio', query_block_rows, position_key_extended, precision=TOP_PRECISION)[..., ::-1])
    source_position = sheared_row_shift(jnp.einsum('lxw,gxw->xlg', key_block_rows, position_query_flipped, precision=TOP_PRECISION))
    source_position = jnp.swapaxes(source_position[..., 2 * SPAN:2 * SPAN + QBLOCK], 1, 2)
    scores = low_back(content + target_position + source_position) * (1.0 / math.sqrt(3.0 * HEAD_DIM))
    distance = jnp.arange(key_rows)[None, :] - jnp.arange(QBLOCK)[:, None]
    allowed = (distance >= 0) & (distance <= 2 * SPAN) & (seg_query[:, None] == seg_key[None, :])
    masked = jnp.where(allowed[None], scores, -1e+30)
    top = lax.optimization_barrier(jnp.max(masked, axis=-1, keepdims=True))
    expv = jnp.exp(masked - top)
    probs = low(expv / lax.optimization_barrier(jnp.sum(expv, axis=-1, keepdims=True)))
    context = jnp.einsum('hab,bhd->ahd', probs, value_blk, precision=TOP_PRECISION)
    return context.reshape(QBLOCK, D)

def encoder_layer(hidden, weights_of, pos_low, seg_pad):
    x_low = low(hidden)
    query = rounded(matmul(x_low, weights_of['query_w']) + weights_of['query_b'])
    key = rounded(matmul(x_low, weights_of['key_w']) + weights_of['key_b'])
    value = rounded(matmul(x_low, weights_of['value_w']) + weights_of['value_b'])
    pos_key = low(matmul(pos_low, weights_of['key_w']) + weights_of['key_b'])
    pos_query = low(matmul(pos_low, weights_of['query_w']) + weights_of['query_b'])
    position_key_extended = jnp.concatenate([pos_key, pos_key[-1:]], axis=0).reshape(2 * SPAN + 1, HEADS, HEAD_DIM)
    position_query_flipped = jnp.concatenate([pos_query[-1:], pos_query[::-1]], axis=0).reshape(2 * SPAN + 1, HEADS, HEAD_DIM)
    key_pad = jnp.pad(key, ((0, 0), (SPAN, SPAN), (0, 0)))
    value_pad = jnp.pad(value, ((0, 0), (SPAN, SPAN), (0, 0)))
    block_count = ROWS * SEQLEN // QBLOCK
    block_fn = jax.checkpoint(attend_block)
    contexts = lax.map(lambda block_index: block_fn(block_index, query, key_pad, value_pad, seg_pad, position_key_extended, position_query_flipped), jnp.arange(block_count, dtype=jnp.int32))
    context = rounded(contexts.reshape(ROWS, SEQLEN, D))
    attended = low_back(matmul(context, weights_of['output_w']) + weights_of['output_b'])
    middle = layer_norm(hidden + attended, weights_of['attn_gain'], weights_of['attn_shift'])
    up_proj = low_back(matmul(low(middle), weights_of['up_w']) + weights_of['up_bias'])
    activated = low(jax.nn.gelu(up_proj, approximate=False))
    down_proj = low_back(matmul(activated, weights_of['down_w']) + weights_of['down_bias'])
    return layer_norm(middle + down_proj, weights_of['ffn_gain'], weights_of['ffn_shift'])

def reference(layer_input, segment_ids, out_grad, weights, momentum, average):
    seg_pad = jnp.pad(segment_ids + 1, ((0, 0), (SPAN, SPAN)))

    def forward(inputs, flat_params):
        layers_list, shared = unpack(low(flat_params))
        pos_low = low(layer_norm(shared['rel_table'], shared['rel_gain'], shared['rel_shift']))
        hidden = inputs
        for weights_of in layers_list:
            hidden = encoder_layer(hidden, weights_of, pos_low, seg_pad)
        return hidden
    outputs, pullback = jax.vjp(forward, layer_input.astype(jnp.float32), weights)
    input_grad, weight_grad = pullback(out_grad.astype(jnp.float32))
    rate = 0.1 / math.sqrt(ALL_TOK)
    new_momentum = 0.5 * momentum + weight_grad
    new_weights = weights - rate * (weight_grad + 0.5 * new_momentum)
    new_average = 0.5 * average + 0.5 * new_weights
    return (outputs.astype(jnp.bfloat16), input_grad, weight_grad, new_momentum, new_average, new_weights, new_weights.astype(jnp.bfloat16))
```

```python
import functools
import math

import jax
import jax.numpy as jnp
from jax import lax
from jax.experimental import pallas as pl
from jax.experimental.pallas import tpu as pltpu
from jax.sharding import PartitionSpec as P

D = 384
HEADS = 6
HEAD_DIM = 64
FF = 1536
SPAN = 256
QBLOCK = 512


TOP_PRECISION = lax.Precision.HIGHEST
EPSILON = 1e-07


def with_halo(cells, sides, width):
    for axis, dim in sides:
        count = lax.axis_size(axis)
        ends = count - 1
        head = lax.slice_in_dim(cells, 0, width, axis=dim)
        tail = lax.slice_in_dim(cells, cells.shape[dim] - width, cells.shape[dim], axis=dim)
        cells = jnp.concatenate(
            [
                lax.ppermute(tail, axis, [(i, (i + 1) % count) for i in range(ends)]),
                cells,
                lax.ppermute(head, axis, [((i + 1) % count, i) for i in range(ends)]),
            ],
            axis=dim,
        )
    return cells


def shifted(block, axis, distance):
    devices = range(lax.axis_size(axis))
    route = [(i - distance, i) for i in devices if i - distance in devices]
    return lax.ppermute(block, axis, route)


def layer_pieces():
    return [
        ("query_w", (D, D)),
        ("key_w", (D, D)),
        ("value_w", (D, D)),
        ("output_w", (D, D)),
        ("up_w", (D, FF)),
        ("down_w", (FF, D)),
        ("query_b", (D,)),
        ("key_b", (D,)),
        ("value_b", (D,)),
        ("output_b", (D,)),
        ("attn_gain", (D,)),
        ("attn_shift", (D,)),
        ("up_bias", (FF,)),
        ("down_bias", (D,)),
        ("ffn_gain", (D,)),
        ("ffn_shift", (D,)),
    ]


def shared_pieces():
    return (("rel_table", (2 * SPAN, D)), ("rel_gain", (D,)), ("rel_shift", (D,)))


def unpack(flat_params):
    offset = 0
    weights_of = {}
    for piece_name, extent in layer_pieces():
        amount = math.prod(extent)
        weights_of[piece_name] = flat_params[offset : offset + amount].reshape(extent)
        offset += amount
    layers_list = [weights_of]
    shared = {}
    for piece_name, extent in shared_pieces():
        amount = math.prod(extent)
        shared[piece_name] = flat_params[offset : offset + amount].reshape(extent)
        offset += amount
    return (layers_list, shared)


def pack(layer_grads, shared_grads, total_length):
    pieces_out = []
    for grads_of in layer_grads:
        for piece_name, extent in layer_pieces():
            pieces_out.append(grads_of[piece_name].reshape(-1))
    for piece_name, extent in shared_pieces():
        pieces_out.append(shared_grads[piece_name].reshape(-1))
    used = sum((piece.shape[0] for piece in pieces_out))
    if total_length > used:
        pieces_out.append(jnp.zeros((total_length - used,), jnp.float32))
    return jnp.concatenate(pieces_out)


def layer_norm(values, gain, shift):
    centered = values - jnp.mean(values, axis=-1, keepdims=True)
    variance = jnp.mean(centered * centered, axis=-1, keepdims=True)
    return centered * lax.rsqrt(variance + EPSILON) * gain + shift


def norm_grads(values, gain, shift, upstream):
    outputs, pullback = jax.vjp(layer_norm, values, gain, shift)
    return pullback(upstream)


def gelu_exact(values):
    return jax.nn.gelu(values, approximate=False)


def matmul(left, right):
    return jnp.dot(left, right, preferred_element_type=jnp.float32)


def matmul_tn(left, right):
    return lax.dot_general(
        left, right, (((0,), (0,)), ((), ())), preferred_element_type=jnp.float32
    )


def matmul_nt(left, right):
    return lax.dot_general(
        left, right, (((1,), (1,)), ((), ())), preferred_element_type=jnp.float32
    )


NB = 5
PAIRS = 3
SC = 1.0/math.sqrt(3.0*HEAD_DIM)
LOG2E = 1.4426950408889634
bf=jnp.bfloat16; f32=jnp.float32
NT=(((1,),(1,)),((),())); NN=(((1,),(0,)),((),())); TN=(((0,),(0,)),((),()))
def dot(a,b,d=NN): return lax.dot_general(a,b,d,preferred_element_type=f32)

def head_mask(rows, h):
    lane=lax.broadcasted_iota(jnp.int32,(rows,128),1)
    return (lane<64) if h==0 else (lane>=64)
def keep(x,h):
    return jnp.where(head_mask(x.shape[0],h), x, jnp.zeros_like(x))

def skew(A):
    return jnp.concatenate([pltpu.roll(A[8*g:8*g+8,:512],8*g+1,1,stride=1,stride_axis=0) for g in range(16)],axis=0)


def att_fwd_body(nblk, q_ref,k_ref,v_ref,krt_ref,qrt_ref,segq_ref,segk_ref,ctx_ref,p_ref,x_scr,bias_scr):
    row=lax.broadcasted_iota(jnp.int32,(128,128),0); lane=lax.broadcasted_iota(jnp.int32,(128,128),1)
    eye=(row==lane).astype(bf)
    def mk_bias(t,c):
        off=pl.multiple_of(t*128,128)
        sq=segq_ref[pl.ds(off,128),:]
        for b in range(NB):
            sk=segk_ref[0:1,pl.ds(pl.multiple_of(off+128*b,128),128)]
            ok = sq==sk
            if b==0: ok = ok & (lane>=row)
            if b==NB-1: ok = ok & (lane<=row)
            bias_scr[t,:,128*b:128*b+128]=jnp.where(ok,0.0,-1e30).astype(f32)
        return c
    lax.fori_loop(0,nblk,mk_bias,0)
    def pair(p,c):
        def keyside(J):
            kj=k_ref[p,pl.ds(pl.multiple_of(jnp.minimum(J,nblk+3)*128,128),128),:]
            for h in range(2):
                C=dot(keep(kj,h),qrt_ref[p],NT)
                R=skew(C)
                x_scr[h,J,:,0:128]=jnp.where(lane>row,R[:,:128],C[:,512:]).astype(bf)
                x_scr[h,J,:,128:512]=R[:,128:].astype(bf)
                x_scr[h,J,:,512:640]=R[:,:128].astype(bf)
        def st(J,c):
            keyside(J); return c
        lax.fori_loop(0,5,st,0)
        def qblock(t,c):
            off=pl.multiple_of(t*128,128)
            qt=q_ref[p,pl.ds(off,128),:]
            kw=[k_ref[p,pl.ds(pl.multiple_of(off+128*b,128),128),:] for b in range(NB)]
            vw=v_ref[p,pl.ds(off,640),:]
            ctx=[]
            for h in range(2):
                qm=keep(qt,h)
                A=dot(qm,krt_ref[p],NT)
                R=skew(A)
                lhs=jnp.concatenate([qm,eye],axis=1)
                rhs=jnp.concatenate([jnp.concatenate([kw[b],x_scr[h,t+b,:,128*(4-b):128*(5-b)]],axis=1) for b in range(NB)],axis=0)
                S=dot(lhs,rhs,NT)
                Y=jnp.concatenate([jnp.where(lane>row,R[:,:128],A[:,512:]),R[:,128:],R[:,:128]],axis=1)
                S=S+Y+bias_scr[t]
                m=jnp.max(S,axis=1,keepdims=True)
                e=jnp.exp2((S-m)*(SC*LOG2E))
                s=jnp.sum(e,axis=1,keepdims=True)
                P=(e*(1.0/s)).astype(bf)
                p_ref[p,t,h]=P
                ctx.append(dot(P,vw,NN))
            ctx_ref[p,pl.ds(off,128),:]=jnp.where(lane<64,ctx[0],ctx[1]).astype(bf)
            keyside(c)
            return c+1
        lax.fori_loop(0,nblk,qblock,jnp.int32(5))
        return c
    lax.fori_loop(0,PAIRS,pair,0)

def att_fwd(q,k,v,krt,qrt,segq_b,segk):
    T=q.shape[1]; nblk=T//128
    return pl.pallas_call(functools.partial(att_fwd_body,nblk),
        out_shape=[jax.ShapeDtypeStruct((PAIRS,T,128),bf),jax.ShapeDtypeStruct((PAIRS,nblk,2,128,640),bf)],
        scratch_shapes=[pltpu.VMEM((2,nblk+5,128,640),bf),pltpu.VMEM((nblk,128,640),f32)],
        compiler_params=pltpu.CompilerParams(vmem_limit_bytes=48<<20),
    )(q,k,v,krt,qrt,segq_b,segk)

def unskew(Grev):
    return jnp.concatenate([pltpu.roll(Grev[8*g:8*g+8],384+8*g,1,stride=1,stride_axis=0) for g in range(16)],axis=0)

def unrev(x, J):
    hi=x.astype(bf); lo=(x-hi.astype(f32)).astype(bf)
    y=dot(J,jnp.concatenate([hi,lo],axis=1))
    return y[:,:128]+y[:,128:]

def att_bwd_body(nblk, q_ref,k_ref,v_ref,krt_ref,qrt_ref,dctx_ref,p_ref,dq_ref,dk_ref,dv_ref,dkr_ref,dqr_ref,gt_scr,dvt_scr):
    row=lax.broadcasted_iota(jnp.int32,(128,128),0); lane=lax.broadcasted_iota(jnp.int32,(128,128),1)
    JR=(row+lane==127).astype(bf)
    gt_scr[...]=jnp.zeros(gt_scr.shape,bf)
    zero=jnp.zeros((128,128),bf)
    def pair(p,c):
        dvt_scr[...]=jnp.zeros(dvt_scr.shape,f32)
        dkr_ref[p]=jnp.zeros((128,640),f32)
        dqr_ref[p]=jnp.zeros((128,640),f32)
        def qblock(t,J0):
            off=pl.multiple_of(t*128,128)
            qt=q_ref[p,pl.ds(off,128),:]
            qT=qt.T
            qTr=dot(qT,JR).astype(bf)
            dct=dctx_ref[p,pl.ds(off,128),:]
            dcT=dct.T
            kw=k_ref[p,pl.ds(off,640),:]
            vw=v_ref[p,pl.ds(off,640),:]
            krt=krt_ref[p]
            dq1=[]; dq2=[]
            for h in range(2):
                dp=dot(keep(dct,h),vw,NT)
                Pb=p_ref[p,t,h]
                Pf=Pb.astype(f32)
                w=Pf*dp
                inner=jnp.sum(w,axis=1,keepdims=True)
                G=(w-Pf*inner).astype(bf)
                Gd=jnp.where(lane==row,G[:,:128],zero)
                Gm=jnp.concatenate([jnp.where(lane>row,G[:,:128],G[:,512:]),G[:,128:512]],axis=1)
                Gu=unskew(dot(JR,Gm)).astype(bf)
                dq1.append(dot(jnp.concatenate([G,Gd],axis=1),jnp.concatenate([kw,krt[512:]],axis=0)))
                dq2.append(dot(Gu,krt[:512]))
                hs=slice(64*h,64*h+64)
                dkr_ref[p,hs,0:512]+=dot(qTr[hs],Gu)
                dkr_ref[p,hs,512:640]+=dot(qT[hs],Gd)
                dvt_scr[hs,pl.ds(off,640)]+=dot(dcT[hs],Pb)
                for b in range(NB):
                    gt_scr[h,J0+b,:,128*(4-b):128*(5-b)]=dot(JR,G[:,128*b:128*b+128],NT).astype(bf)
            dq=jnp.where(lane<64,dq1[0],dq1[1])+unrev(jnp.where(lane<64,dq2[0],dq2[1]),JR)
            dq_ref[p,pl.ds(off,128),:]=(SC*dq).astype(bf)
            return J0+1
        lax.fori_loop(0,nblk,qblock,jnp.int32(0))
        def kblock(J,c):
            off=pl.multiple_of(J*128,128)
            kj=k_ref[p,pl.ds(off,128),:]
            kT=kj.T
            kTr=dot(kT,JR).astype(bf)
            qw=jnp.concatenate([q_ref[p,pl.ds(pl.multiple_of(jnp.clip(J-4+w,0,nblk-1)*128,128),128),:] for w in range(NB)],axis=0)
            rhs=jnp.concatenate([qw,qrt_ref[p]],axis=0)
            dks=[]
            for h in range(2):
                GT=gt_scr[h,J]
                Gd=jnp.where(lane+row==127,GT[:,:128],zero)
                Gm=jnp.concatenate([jnp.where(lane+row>127,GT[:,:128],GT[:,512:]),GT[:,128:512]],axis=1).astype(f32)
                Gu=unskew(Gm).astype(bf)
                Gx=jnp.concatenate([Gu,Gd],axis=1)
                dks.append(dot(jnp.concatenate([GT,Gx],axis=1),rhs))
                hs=slice(64*h,64*h+64)
                dqr_ref[p,hs,:]+=dot(kTr[hs],Gx)
            dk_ref[p,pl.ds(off,128),:]=SC*unrev(jnp.where(lane<64,dks[0],dks[1]),JR)
            dv_ref[p,pl.ds(off,128),:]=dvt_scr[:,pl.ds(off,128)].T
            return c
        lax.fori_loop(0,nblk+4,kblock,0)
        dkr_ref[p]=SC*dkr_ref[p]
        dqr_ref[p]=SC*dqr_ref[p]
        return c
    lax.fori_loop(0,PAIRS,pair,0)

def att_bwd(q,k,v,krt,qrt,dctx,P):
    T=q.shape[1]; nblk=T//128; E=T+512
    return pl.pallas_call(functools.partial(att_bwd_body,nblk),
        out_shape=[jax.ShapeDtypeStruct((PAIRS,T,128),bf),jax.ShapeDtypeStruct((PAIRS,E,128),f32),jax.ShapeDtypeStruct((PAIRS,E,128),f32),
          jax.ShapeDtypeStruct((PAIRS,128,640),f32),jax.ShapeDtypeStruct((PAIRS,128,640),f32)],
        scratch_shapes=[pltpu.VMEM((2,nblk+4,128,640),bf),pltpu.VMEM((128,E),f32)],
        compiler_params=pltpu.CompilerParams(vmem_limit_bytes=48<<20),
    )(q,k,v,krt,qrt,dctx,P)


def paired(a):
    return a.reshape(a.shape[0],PAIRS,128).transpose(1,0,2)

def unpaired(a):
    return a.transpose(1,0,2).reshape(a.shape[1],D)

def untable(x):
    x=x.reshape(D,640).T
    y=x[:512][::-1]
    return y.at[511].add(jnp.sum(x[512:],axis=0))


def layer_forward(hidden, weights_of, pos_low, seg_ext):
    x_low = hidden.astype(jnp.bfloat16)
    query_low = (
        matmul(x_low, weights_of["query_w"]) + weights_of["query_b"].astype(jnp.float32)
    ).astype(jnp.bfloat16)
    key_low = (matmul(x_low, weights_of["key_w"]) + weights_of["key_b"].astype(jnp.float32)).astype(
        jnp.bfloat16
    )
    value_low = (
        matmul(x_low, weights_of["value_w"]) + weights_of["value_b"].astype(jnp.float32)
    ).astype(jnp.bfloat16)
    kv_ext = with_halo(jnp.stack([key_low, value_low]), (("seq", 1),), SPAN)
    pos_key = (
        matmul(pos_low, weights_of["key_w"]) + weights_of["key_b"].astype(jnp.float32)
    ).astype(jnp.bfloat16)
    pos_query = (
        matmul(pos_low, weights_of["query_w"]) + weights_of["query_b"].astype(jnp.float32)
    ).astype(jnp.bfloat16)
    key_table = paired(jnp.concatenate([pos_key[::-1], jnp.broadcast_to(pos_key[-1:], (128, D))], axis=0))
    query_table = paired(jnp.concatenate([pos_query[::-1], jnp.broadcast_to(pos_query[-1:], (128, D))], axis=0))
    tokens_here = x_low.shape[0]
    seg_rows = jnp.broadcast_to(seg_ext[SPAN : SPAN + tokens_here, None], (tokens_here, 128))
    qp, kp, vp = paired(query_low), paired(kv_ext[0]), paired(kv_ext[1])
    context, probs = att_fwd(qp, kp, vp, key_table, query_table, seg_rows, seg_ext[None])
    context = unpaired(context)
    context_low = context.astype(jnp.bfloat16)
    first_sum = (
        hidden
        + matmul(context_low, weights_of["output_w"])
        + weights_of["output_b"].astype(jnp.float32)
    )
    middle = layer_norm(
        first_sum,
        weights_of["attn_gain"].astype(jnp.float32),
        weights_of["attn_shift"].astype(jnp.float32),
    )
    middle_low = middle.astype(jnp.bfloat16)
    up_proj = matmul(middle_low, weights_of["up_w"]) + weights_of["up_bias"].astype(jnp.float32)
    act_low = gelu_exact(up_proj).astype(jnp.bfloat16)
    second_sum = (
        middle + matmul(act_low, weights_of["down_w"]) + weights_of["down_bias"].astype(jnp.float32)
    )
    output = layer_norm(
        second_sum,
        weights_of["ffn_gain"].astype(jnp.float32),
        weights_of["ffn_shift"].astype(jnp.float32),
    )
    saved = {
        "x_low": x_low,
        "att": (qp, kp, vp, key_table, query_table),
        "probs": probs,
        "context_low": context_low,
        "first_sum": first_sum,
        "middle_low": middle_low,
        "up_proj": up_proj,
        "act_low": act_low,
        "second_sum": second_sum,
    }
    return (output, saved)


def layer_backward(saved, weights_of, pos_low, seg_ext, grad_out):
    grads_of = {}
    tokens_here = saved["x_low"].shape[0]
    second_grad, grads_of["ffn_gain"], grads_of["ffn_shift"] = norm_grads(
        saved["second_sum"],
        weights_of["ffn_gain"].astype(jnp.float32),
        weights_of["ffn_shift"].astype(jnp.float32),
        grad_out,
    )
    down_grad = second_grad.astype(jnp.bfloat16)
    grads_of["down_w"] = matmul_tn(saved["act_low"], down_grad)
    grads_of["down_bias"] = jnp.sum(down_grad.astype(jnp.float32), axis=0)
    act_grad = matmul_nt(down_grad, weights_of["down_w"])
    up_grad = jax.vjp(gelu_exact, saved["up_proj"])[1](act_grad)[0].astype(jnp.bfloat16)
    grads_of["up_w"] = matmul_tn(saved["middle_low"], up_grad)
    grads_of["up_bias"] = jnp.sum(up_grad.astype(jnp.float32), axis=0)
    middle_grad = second_grad + matmul_nt(up_grad, weights_of["up_w"])
    first_grad, grads_of["attn_gain"], grads_of["attn_shift"] = norm_grads(
        saved["first_sum"],
        weights_of["attn_gain"].astype(jnp.float32),
        weights_of["attn_shift"].astype(jnp.float32),
        middle_grad,
    )
    attn_grad = first_grad.astype(jnp.bfloat16)
    grads_of["output_w"] = matmul_tn(saved["context_low"], attn_grad)
    grads_of["output_b"] = jnp.sum(attn_grad.astype(jnp.float32), axis=0)
    context_grad = matmul_nt(attn_grad, weights_of["output_w"]).astype(jnp.bfloat16)
    dquery, dkey_ext, dvalue_ext, dkr, dqr = att_bwd(*saved["att"], paired(context_grad), saved["probs"])
    dquery, dkey_ext, dvalue_ext = unpaired(dquery), unpaired(dkey_ext), unpaired(dvalue_ext)
    dpos_key, dpos_query = untable(dkr), untable(dqr)
    left_rim = jnp.stack([dkey_ext[:SPAN], dvalue_ext[:SPAN]])
    right_rim = jnp.stack([dkey_ext[SPAN + tokens_here :], dvalue_ext[SPAN + tokens_here :]])
    from_next = shifted(left_rim.astype(jnp.bfloat16), "seq", -1).astype(left_rim.dtype)
    from_prev = shifted(right_rim.astype(jnp.bfloat16), "seq", 1).astype(right_rim.dtype)
    head_pad = ((0, tokens_here - SPAN), (0, 0))
    tail_pad = ((tokens_here - SPAN, 0), (0, 0))
    dkey = (
        dkey_ext[SPAN : SPAN + tokens_here]
        + jnp.pad(from_prev[0], head_pad)
        + jnp.pad(from_next[0], tail_pad)
    )
    dvalue = (
        dvalue_ext[SPAN : SPAN + tokens_here]
        + jnp.pad(from_prev[1], head_pad)
        + jnp.pad(from_next[1], tail_pad)
    )
    dquery_low = dquery.astype(jnp.bfloat16)
    dkey_low = dkey.astype(jnp.bfloat16)
    dvalue_low = dvalue.astype(jnp.bfloat16)
    pos_wide = pos_low.astype(jnp.float32)
    key_wide = weights_of["key_w"].astype(jnp.float32)
    query_wide = weights_of["query_w"].astype(jnp.float32)
    x_low = saved["x_low"]
    grads_of["query_w"] = matmul_tn(x_low, dquery_low) + jnp.dot(
        pos_wide.T, dpos_query, precision=TOP_PRECISION
    )
    grads_of["key_w"] = matmul_tn(x_low, dkey_low) + jnp.dot(
        pos_wide.T, dpos_key, precision=TOP_PRECISION
    )
    grads_of["value_w"] = matmul_tn(x_low, dvalue_low)
    grads_of["query_b"] = jnp.sum(dquery_low.astype(jnp.float32), axis=0) + jnp.sum(
        dpos_query, axis=0
    )
    grads_of["key_b"] = jnp.sum(dkey_low.astype(jnp.float32), axis=0) + jnp.sum(dpos_key, axis=0)
    grads_of["value_b"] = jnp.sum(dvalue_low.astype(jnp.float32), axis=0)
    dpos = jnp.dot(dpos_key, key_wide.T, precision=TOP_PRECISION) + jnp.dot(
        dpos_query, query_wide.T, precision=TOP_PRECISION
    )
    grad_in = (
        first_grad
        + matmul_nt(dquery_low, weights_of["query_w"])
        + matmul_nt(dkey_low, weights_of["key_w"])
        + matmul_nt(dvalue_low, weights_of["value_w"])
    )
    return (grad_in, grads_of, dpos)


def on_device(layer_input, segment_ids, out_grad, weights, momentum, average):
    tokens_here = layer_input.shape[1]
    hidden = layer_input[0].astype(jnp.float32)
    seg_ext = with_halo(segment_ids[0] + 1, (("seq", 0),), SPAN)
    weights_low = weights.astype(jnp.bfloat16)
    gathered = lax.all_gather(weights_low, ("seq", "row"), axis=0, tiled=True)
    total_length = gathered.shape[0]
    layers_list, shared = unpack(gathered)
    table_wide = shared["rel_table"].astype(jnp.float32)
    table_gain = shared["rel_gain"].astype(jnp.float32)
    table_shift = shared["rel_shift"].astype(jnp.float32)
    pos_low = layer_norm(table_wide, table_gain, table_shift).astype(jnp.bfloat16)
    saved_list = []
    for weights_of in layers_list:
        hidden, saved = layer_forward(hidden, weights_of, pos_low, seg_ext)
        saved_list.append(saved)
    block_output = hidden.astype(jnp.bfloat16)
    regathered = lax.all_gather(weights_low, ("seq", "row"), axis=0, tiled=True)
    back_layers, unused_shared = unpack(regathered)
    grad_hidden = out_grad[0].astype(jnp.float32)
    grad_hidden, grads_of, dpos = layer_backward(
        saved_list[0], back_layers[0], pos_low, seg_ext, grad_hidden
    )
    grads_reversed = [grads_of]
    shared_grads = {}
    shared_grads["rel_table"], shared_grads["rel_gain"], shared_grads["rel_shift"] = norm_grads(
        table_wide, table_gain, table_shift, dpos
    )
    grad_flat = pack(grads_reversed[::-1], shared_grads, total_length)
    weight_grad = lax.psum_scatter(grad_flat, ("seq", "row"), scatter_dimension=0, tiled=True)
    all_tokens = tokens_here * lax.axis_size("seq") * layer_input.shape[0] * lax.axis_size("row")
    rate = 0.1 / math.sqrt(all_tokens)
    new_momentum = 0.5 * momentum + weight_grad
    new_weights = weights - rate * (weight_grad + 0.5 * new_momentum)
    new_average = 0.5 * average + 0.5 * new_weights
    return (
        block_output[None],
        grad_hidden[None],
        weight_grad,
        new_momentum,
        new_average,
        new_weights,
        new_weights.astype(jnp.bfloat16),
    )


def solution(mesh):
    placed = (
        P("row", "seq", None),
        P("row", "seq"),
        P("row", "seq", None),
        P(("seq", "row")),
        P(("seq", "row")),
        P(("seq", "row")),
    )
    return jax.shard_map(
        on_device,
        mesh=mesh,
        in_specs=placed,
        out_specs=(
            P("row", "seq", None),
            P("row", "seq", None),
            P(("seq", "row")),
            P(("seq", "row")),
            P(("seq", "row")),
            P(("seq", "row")),
            P(("seq", "row")),
        ),
        check_vma=False,
    )
```

```python
import functools
import itertools
import math

import jax
import jax.numpy as jnp
from jax import lax
from jax.experimental import pallas as pl
from jax.experimental.pallas import tpu as pltpu
from jax.sharding import PartitionSpec as P

D = 384
HEADS = 6
HEAD_DIM = 64
FF = 1536
SPAN = 256
QBLOCK = 512


TOP_PRECISION = lax.Precision.HIGHEST
EPSILON = 1e-07


def with_halo(cells, sides, width):
    for axis, dim in sides:
        count = lax.axis_size(axis)
        ends = count - 1
        head = lax.slice_in_dim(cells, 0, width, axis=dim)
        tail = lax.slice_in_dim(cells, cells.shape[dim] - width, cells.shape[dim], axis=dim)
        cells = jnp.concatenate(
            [
                lax.ppermute(tail, axis, [(i, (i + 1) % count) for i in range(ends)]),
                cells,
                lax.ppermute(head, axis, [((i + 1) % count, i) for i in range(ends)]),
            ],
            axis=dim,
        )
    return cells


def shifted(block, axis, distance):
    devices = range(lax.axis_size(axis))
    route = [(i - distance, i) for i in devices if i - distance in devices]
    return lax.ppermute(block, axis, route)


def layer_pieces():
    return [
        ("query_w", (D, D)),
        ("key_w", (D, D)),
        ("value_w", (D, D)),
        ("output_w", (D, D)),
        ("up_w", (D, FF)),
        ("down_w", (FF, D)),
        ("query_b", (D,)),
        ("key_b", (D,)),
        ("value_b", (D,)),
        ("output_b", (D,)),
        ("attn_gain", (D,)),
        ("attn_shift", (D,)),
        ("up_bias", (FF,)),
        ("down_bias", (D,)),
        ("ffn_gain", (D,)),
        ("ffn_shift", (D,)),
    ]


def shared_pieces():
    return (("rel_table", (2 * SPAN, D)), ("rel_gain", (D,)), ("rel_shift", (D,)))


def layer_norm(values, gain, shift):
    centered = values - jnp.mean(values, axis=-1, keepdims=True)
    variance = jnp.mean(centered * centered, axis=-1, keepdims=True)
    return centered * lax.rsqrt(variance + EPSILON) * gain + shift


def norm_grads(values, gain, shift, upstream):
    outputs, pullback = jax.vjp(layer_norm, values, gain, shift)
    return pullback(upstream)


def gelu_exact(values):
    return jax.nn.gelu(values, approximate=False)


def matmul(left, right):
    return jnp.dot(left, right, preferred_element_type=jnp.float32)


def matmul_tn(left, right):
    return lax.dot_general(
        left, right, (((0,), (0,)), ((), ())), preferred_element_type=jnp.float32
    )


def matmul_nt(left, right):
    return lax.dot_general(
        left, right, (((1,), (1,)), ((), ())), preferred_element_type=jnp.float32
    )


NB = 5
PAIRS = 3
SC = 1.0/math.sqrt(3.0*HEAD_DIM)
LOG2E = 1.4426950408889634
bf=jnp.bfloat16; f32=jnp.float32
NT=(((1,),(1,)),((),())); NN=(((1,),(0,)),((),())); TN=(((0,),(0,)),((),()))
def dot(a,b,d=NN): return lax.dot_general(a,b,d,preferred_element_type=f32)

def head_mask(rows, h):
    lane=lax.broadcasted_iota(jnp.int32,(rows,128),1)
    return (lane<64) if h==0 else (lane>=64)
def keep(x,h):
    return jnp.where(head_mask(x.shape[0],h), x, jnp.zeros_like(x))

def skew(A):
    return jnp.concatenate([pltpu.roll(A[8*g:8*g+8,:512],8*g+1,1,stride=1,stride_axis=0) for g in range(16)],axis=0)


def att_fwd_body(nblk, q_ref,k_ref,v_ref,krt_ref,qrt_ref,segq_ref,segk_ref,ctx_ref,p_ref,x_scr,bias_scr):
    row=lax.broadcasted_iota(jnp.int32,(128,128),0); lane=lax.broadcasted_iota(jnp.int32,(128,128),1)
    eye=(row==lane).astype(bf)
    def mk_bias(t,c):
        off=pl.multiple_of(t*128,128)
        sq=segq_ref[pl.ds(off,128),:]
        for b in range(NB):
            sk=segk_ref[0:1,pl.ds(pl.multiple_of(off+128*b,128),128)]
            ok = sq==sk
            if b==0: ok = ok & (lane>=row)
            if b==NB-1: ok = ok & (lane<=row)
            bias_scr[t,:,128*b:128*b+128]=jnp.where(ok,0.0,-1e30).astype(f32)
        return c
    lax.fori_loop(0,nblk,mk_bias,0)
    def pair(p,c):
        def keyside(J):
            kj=k_ref[p,pl.ds(pl.multiple_of(jnp.minimum(J,nblk+3)*128,128),128),:]
            for h in range(2):
                C=dot(keep(kj,h),qrt_ref[p],NT)
                R=skew(C)
                x_scr[h,J,:,0:128]=jnp.where(lane>row,R[:,:128],C[:,512:]).astype(bf)
                x_scr[h,J,:,128:512]=R[:,128:].astype(bf)
                x_scr[h,J,:,512:640]=R[:,:128].astype(bf)
        def st(J,c):
            keyside(J); return c
        lax.fori_loop(0,5,st,0)
        def qblock(t,c):
            off=pl.multiple_of(t*128,128)
            qt=q_ref[p,pl.ds(off,128),:]
            kw=[k_ref[p,pl.ds(pl.multiple_of(off+128*b,128),128),:] for b in range(NB)]
            vw=v_ref[p,pl.ds(off,640),:]
            ctx=[]
            for h in range(2):
                qm=keep(qt,h)
                A=dot(qm,krt_ref[p],NT)
                R=skew(A)
                lhs=jnp.concatenate([qm,eye],axis=1)
                rhs=jnp.concatenate([jnp.concatenate([kw[b],x_scr[h,t+b,:,128*(4-b):128*(5-b)]],axis=1) for b in range(NB)],axis=0)
                S=dot(lhs,rhs,NT)
                Y=jnp.concatenate([jnp.where(lane>row,R[:,:128],A[:,512:]),R[:,128:],R[:,:128]],axis=1)
                S=S+Y+bias_scr[t]
                m=jnp.max(S,axis=1,keepdims=True)
                e=jnp.exp2((S-m)*(SC*LOG2E))
                s=jnp.sum(e,axis=1,keepdims=True)
                P=(e*(1.0/s)).astype(bf)
                p_ref[p,t,h]=P
                ctx.append(dot(P,vw,NN))
            ctx_ref[p,pl.ds(off,128),:]=jnp.where(lane<64,ctx[0],ctx[1]).astype(bf)
            keyside(c)
            return c+1
        lax.fori_loop(0,nblk,qblock,jnp.int32(5))
        return c
    lax.fori_loop(0,PAIRS,pair,0)

def att_fwd(q,k,v,krt,qrt,segq_b,segk):
    T=q.shape[1]; nblk=T//128
    return pl.pallas_call(functools.partial(att_fwd_body,nblk),
        out_shape=[jax.ShapeDtypeStruct((PAIRS,T,128),bf),jax.ShapeDtypeStruct((PAIRS,nblk,2,128,640),bf)],
        scratch_shapes=[pltpu.VMEM((2,nblk+5,128,640),bf),pltpu.VMEM((nblk,128,640),f32)],
        compiler_params=pltpu.CompilerParams(vmem_limit_bytes=48<<20),
    )(q,k,v,krt,qrt,segq_b,segk)

def unskew(Grev):
    return jnp.concatenate([pltpu.roll(Grev[8*g:8*g+8],384+8*g,1,stride=1,stride_axis=0) for g in range(16)],axis=0)

def unrev(x, J):
    hi=x.astype(bf); lo=(x-hi.astype(f32)).astype(bf)
    y=dot(J,jnp.concatenate([hi,lo],axis=1))
    return y[:,:128]+y[:,128:]

def att_bwd_body(nblk, q_ref,k_ref,v_ref,krt_ref,qrt_ref,dctx_ref,p_ref,dq_ref,dk_ref,dv_ref,dkr_ref,dqr_ref,gt_scr,dvt_scr):
    row=lax.broadcasted_iota(jnp.int32,(128,128),0); lane=lax.broadcasted_iota(jnp.int32,(128,128),1)
    JR=(row+lane==127).astype(bf)
    gt_scr[...]=jnp.zeros(gt_scr.shape,bf)
    zero=jnp.zeros((128,128),bf)
    def pair(p,c):
        dvt_scr[...]=jnp.zeros(dvt_scr.shape,f32)
        dkr_ref[p]=jnp.zeros((128,640),f32)
        dqr_ref[p]=jnp.zeros((128,640),f32)
        def qblock(t,J0):
            off=pl.multiple_of(t*128,128)
            qt=q_ref[p,pl.ds(off,128),:]
            qT=qt.T
            qTr=dot(qT,JR).astype(bf)
            dct=dctx_ref[p,pl.ds(off,128),:]
            dcT=dct.T
            kw=k_ref[p,pl.ds(off,640),:]
            vw=v_ref[p,pl.ds(off,640),:]
            krt=krt_ref[p]
            dq1=[]; dq2=[]
            for h in range(2):
                dp=dot(keep(dct,h),vw,NT)
                Pb=p_ref[p,t,h]
                Pf=Pb.astype(f32)
                w=Pf*dp
                inner=jnp.sum(w,axis=1,keepdims=True)
                G=(w-Pf*inner).astype(bf)
                Gd=jnp.where(lane==row,G[:,:128],zero)
                Gm=jnp.concatenate([jnp.where(lane>row,G[:,:128],G[:,512:]),G[:,128:512]],axis=1)
                Gu=unskew(dot(JR,Gm)).astype(bf)
                dq1.append(dot(jnp.concatenate([G,Gd],axis=1),jnp.concatenate([kw,krt[512:]],axis=0)))
                dq2.append(dot(Gu,krt[:512]))
                hs=slice(64*h,64*h+64)
                dkr_ref[p,hs,0:512]+=dot(qTr[hs],Gu)
                dkr_ref[p,hs,512:640]+=dot(qT[hs],Gd)
                dvt_scr[hs,pl.ds(off,640)]+=dot(dcT[hs],Pb)
                for b in range(NB):
                    gt_scr[h,J0+b,:,128*(4-b):128*(5-b)]=dot(JR,G[:,128*b:128*b+128],NT).astype(bf)
            dq=jnp.where(lane<64,dq1[0],dq1[1])+unrev(jnp.where(lane<64,dq2[0],dq2[1]),JR)
            dq_ref[p,pl.ds(off,128),:]=(SC*dq).astype(bf)
            return J0+1
        lax.fori_loop(0,nblk,qblock,jnp.int32(0))
        def kblock(J,c):
            off=pl.multiple_of(J*128,128)
            kj=k_ref[p,pl.ds(off,128),:]
            kT=kj.T
            kTr=dot(kT,JR).astype(bf)
            qw=jnp.concatenate([q_ref[p,pl.ds(pl.multiple_of(jnp.clip(J-4+w,0,nblk-1)*128,128),128),:] for w in range(NB)],axis=0)
            rhs=jnp.concatenate([qw,qrt_ref[p]],axis=0)
            dks=[]
            for h in range(2):
                GT=gt_scr[h,J]
                Gd=jnp.where(lane+row==127,GT[:,:128],zero)
                Gm=jnp.concatenate([jnp.where(lane+row>127,GT[:,:128],GT[:,512:]),GT[:,128:512]],axis=1).astype(f32)
                Gu=unskew(Gm).astype(bf)
                Gx=jnp.concatenate([Gu,Gd],axis=1)
                dks.append(dot(jnp.concatenate([GT,Gx],axis=1),rhs))
                hs=slice(64*h,64*h+64)
                dqr_ref[p,hs,:]+=dot(kTr[hs],Gx)
            dk_ref[p,pl.ds(off,128),:]=SC*unrev(jnp.where(lane<64,dks[0],dks[1]),JR)
            dv_ref[p,pl.ds(off,128),:]=dvt_scr[:,pl.ds(off,128)].T
            return c
        lax.fori_loop(0,nblk+4,kblock,0)
        dkr_ref[p]=SC*dkr_ref[p]
        dqr_ref[p]=SC*dqr_ref[p]
        return c
    lax.fori_loop(0,PAIRS,pair,0)

def att_bwd(q,k,v,krt,qrt,dctx,P):
    T=q.shape[1]; nblk=T//128; E=T+512
    return pl.pallas_call(functools.partial(att_bwd_body,nblk),
        out_shape=[jax.ShapeDtypeStruct((PAIRS,T,128),bf),jax.ShapeDtypeStruct((PAIRS,E,128),f32),jax.ShapeDtypeStruct((PAIRS,E,128),f32),
          jax.ShapeDtypeStruct((PAIRS,128,640),f32),jax.ShapeDtypeStruct((PAIRS,128,640),f32)],
        scratch_shapes=[pltpu.VMEM((2,nblk+4,128,640),bf),pltpu.VMEM((128,E),f32)],
        compiler_params=pltpu.CompilerParams(vmem_limit_bytes=48<<20),
    )(q,k,v,krt,qrt,dctx,P)


MESH = pl.DeviceIdType.MESH
GROUP = 2048


class Grid:
    def __init__(self, seq, row):
        half = seq // 2
        wide = 1
        while wide * wide * 4 <= half:
            wide *= 2
        self.size = {"z": half // wide, "y": wide, "x": row}
        self.seq, self.row, self.count = seq, row, seq * row

    def here(self):
        s, x = lax.axis_index("seq"), lax.axis_index("row")
        y_size = self.size["y"]
        return {"z": s // (2 * y_size), "y": (s // 2) % y_size, "c": s % 2, "x": x}

    def seq_of(self, p):
        return (p["z"] * self.size["y"] + p["y"]) * 2 + p["c"]

    def flat(self, p):
        return self.seq_of(p) * self.row + p["x"]

    def device(self, p):
        return {"seq": self.seq_of(p), "row": p["x"]}

    def plane(self, p):
        return (p["z"] * self.size["y"] + p["y"]) * self.row + p["x"]

    def offsets(self, order):
        choices = []
        for axis in order:
            n = self.size[axis]
            if n == 2:
                choices.append([0, "f"])
            else:
                choices.append([0] + [sign * d for d in range(1, n) for sign in (-1, 1)])
        hops = lambda off: sum(1 if o == "f" else abs(o) for o in off)
        return sorted(itertools.product(*choices), key=hops)


def both(conds):
    out = None
    for cond in conds:
        if cond is not None:
            out = cond if out is None else jnp.logical_and(out, cond)
    return out


def guarded(cond, fn):
    if cond is None:
        fn()
    else:
        pl.when(cond)(fn)


def source_of(grid, p, order, off):
    o, conds = dict(p), []
    for axis, d in zip(order, off):
        if d == "f":
            o[axis] = 1 - p[axis]
        elif d != 0:
            o[axis] = p[axis] + d
            conds.append(p[axis] + d >= 0 if d < 0 else p[axis] + d < grid.size[axis])
    return o, both(conds)


def parent_of(grid, p, order, off):
    last = max((i for i, d in enumerate(off) if d != 0), default=None)
    if last is None:
        return None, None
    q, axis, d = dict(p), order[last], off[last]
    if d == "f":
        q[axis] = 1 - p[axis]
        return q, axis + "0"
    q[axis] = p[axis] + (1 if d > 0 else -1)
    return q, axis + ("+" if d > 0 else "-")


def children_of(grid, p, order, off):
    last = max((i for i, d in enumerate(off) if d != 0), default=None)
    found = []
    if last is not None and off[last] != "f":
        axis, away = order[last], (-1 if off[last] > 0 else 1)
        q = dict(p)
        q[axis] = p[axis] + away
        found.append((axis + ("+" if away > 0 else "-"), q, p[axis] > 0 if away < 0 else p[axis] < grid.size[axis] - 1))
    for axis in order[0 if last is None else last + 1 :]:
        if grid.size[axis] == 2:
            q = dict(p)
            q[axis] = 1 - p[axis]
            found.append((axis + "0", q, None))
        elif grid.size[axis] > 2:
            for sign in (1, -1):
                q = dict(p)
                q[axis] = p[axis] + sign
                found.append((axis + ("+" if sign > 0 else "-"), q, p[axis] > 0 if sign < 0 else p[axis] < grid.size[axis] - 1))
    return found


def neighbours_of(grid, p):
    found = []
    for axis in ("z", "y", "x"):
        found += children_of(grid, p, (axis,), (0,))
    sibling = dict(p)
    sibling["c"] = 1 - p["c"]
    found.append(("c0", sibling, None))
    return found


def enter(grid, p, extra=()):
    sem = pltpu.get_barrier_semaphore()
    total = jnp.int32(0)
    for name, q, cond in neighbours_of(grid, p) + list(extra):
        guarded(cond, lambda q=q: pl.semaphore_signal(sem, inc=1, device_id=grid.device(q), device_id_type=MESH))
        total = total + (1 if cond is None else cond.astype(jnp.int32))
    pl.semaphore_wait(sem, total)


def orders_of(groups):
    return (("z", "y", "x"), ("x", "z", "y")) if groups >= 8 else (("z", "y", "x"),)


def spans(groups):
    if groups < 8:
        return ((0, 16 * groups),)
    first = (groups * 20 + 16) // 32
    return ((0, 16 * first), (16 * first, 16 * (groups - first)))


class Gather:
    def __init__(self, grid, p, slots, send_sem, recv_sem, groups):
        self.grid, self.p, self.slots = grid, p, slots
        self.send_sem, self.recv_sem, self.groups = send_sem, recv_sem, groups
        self.sends, self.used = [], 0

    def copy(self, part, k, q, index):
        start, rows = spans(self.groups)[part]
        block = self.slots.at[k, pl.ds(start, rows), :]
        return pltpu.make_async_remote_copy(
            src_ref=block, dst_ref=block, send_sem=self.send_sem.at[index], recv_sem=self.recv_sem.at[part, k],
            device_id=self.grid.device(q), device_id_type=MESH)

    def arrived(self, part, k):
        start, rows = spans(self.groups)[part]
        block = self.slots.at[k, pl.ds(start, rows), :]
        pltpu.make_async_remote_copy(
            src_ref=block, dst_ref=block, send_sem=self.send_sem.at[0], recv_sem=self.recv_sem.at[part, k],
            device_id=self.grid.device(self.p), device_id_type=MESH).wait_recv()

    def run(self):
        grid, p = self.grid, self.p
        steps = []
        for part, order in enumerate(orders_of(self.groups)):
            for off in grid.offsets(order):
                steps.append((sum(1 if o == "f" else abs(o) for o in off), part, order, off))
        steps.sort(key=lambda item: item[:2])
        sibling = dict(p)
        sibling["c"] = 1 - p["c"]
        finish = []
        for hops, part, order, off in steps:
            o, cond = source_of(grid, p, order, off)
            k = grid.flat(o)
            targets = children_of(grid, p, order, off) + [("c0", sibling, None)]
            indices = [self.used + i for i in range(len(targets))]
            self.used += len(targets)

            def step(part=part, k=k, targets=targets, indices=indices, own=hops == 0):
                if not own:
                    self.arrived(part, k)
                for (name, q, when), index in zip(targets, indices):
                    guarded(when, lambda q=q, index=index: self.copy(part, k, q, index).start())

            guarded(cond, step)

            def end(part=part, k=k, targets=targets, indices=indices):
                for (name, q, when), index in zip(targets, indices):
                    guarded(when, lambda q=q, index=index: self.copy(part, k, q, index).wait_send())

            finish.append((cond, end))
        for part, order in enumerate(orders_of(self.groups)):
            for off in grid.offsets(order):
                o, cond = source_of(grid, sibling, order, off)
                guarded(cond, lambda part=part, k=grid.flat(o): self.arrived(part, k))
        for cond, end in finish:
            guarded(cond, end)

def count_sends(grid, groups):
    fake = {"z": jnp.int32(0), "y": jnp.int32(0), "x": jnp.int32(0), "c": jnp.int32(0)}
    return sum(len(children_of(grid, fake, order, off)) + 1 for order in orders_of(groups) for off in grid.offsets(order))


OPPOSITE = {"+": "-", "-": "+", "0": "0"}


def direction_names(grid):
    names = ["c0"]
    for axis in ("z", "y", "x"):
        if grid.size[axis] == 2:
            names.append(axis + "0")
        elif grid.size[axis] > 2:
            names += [axis + "+", axis + "-"]
    return names


class Scatter:
    def __init__(self, grid, p, flat, first_row, kids, outgoing, total, send_sem, recv_sem, groups):
        self.grid, self.p, self.flat, self.first_row = grid, p, flat, first_row
        self.kids, self.outgoing, self.total = kids, outgoing, total
        self.send_sem, self.recv_sem, self.groups = send_sem, recv_sem, groups
        self.names = direction_names(grid)

    def incoming(self, part, name, place):
        start, rows = spans(self.groups)[part]
        return self.kids.at[self.names.index(name), place, pl.ds(start, rows), :]

    def transfer(self, source, part, name, place, q, send):
        return pltpu.make_async_remote_copy(
            src_ref=source, dst_ref=self.incoming(part, name, place), send_sem=self.send_sem.at[send],
            recv_sem=self.recv_sem.at[part, self.names.index(name), place], device_id=self.grid.device(q), device_id_type=MESH)

    def arrived(self, part, name, place):
        block = self.incoming(part, name, place)
        pltpu.make_async_remote_copy(
            src_ref=block, dst_ref=block, send_sem=self.send_sem.at[0],
            recv_sem=self.recv_sem.at[part, self.names.index(name), place],
            device_id=self.grid.device(self.p), device_id_type=MESH).wait_recv()

    def run(self, result):
        grid, p = self.grid, self.p
        sibling = dict(p)
        sibling["c"] = 1 - p["c"]
        steps = []
        for part, order in enumerate(orders_of(self.groups)):
            for off in grid.offsets(order):
                steps.append((-sum(1 if o == "f" else abs(o) for o in off), part, order, off))
        steps.sort(key=lambda item: item[:2])
        used, finish = 0, []
        for hops, part, order, off in steps:
            o, cond = source_of(grid, sibling, order, off)
            start, rows = spans(self.groups)[part]

            def give(part=part, o=o, index=used, start=start, rows=rows):
                block = self.flat.at[pl.ds(pl.multiple_of(self.first_row(grid.flat(o)) + start, 16), rows), :]
                return self.transfer(block, part, "c0", grid.plane(o), sibling, index)

            guarded(cond, lambda give=give: give().start())
            finish.append((cond, lambda give=give: give().wait_send()))
            used += 1
        for hops, part, order, off in steps:
            o, cond = source_of(grid, p, order, off)
            place, k = grid.plane(o), grid.flat(o)
            start, rows = spans(self.groups)[part]
            kids = children_of(grid, p, order, off)
            parent, side = parent_of(grid, p, order, off)

            def push(part=part, place=place, parent=parent, side=side, index=used, start=start, rows=rows):
                block = self.outgoing.at[place, pl.ds(start, rows), :]
                return self.transfer(block, part, side[0] + OPPOSITE[side[1]], place, parent, index)

            def step(part=part, place=place, k=k, kids=kids, parent=parent, start=start, rows=rows, push=push):
                self.arrived(part, "c0", place)
                mine = self.flat[pl.ds(pl.multiple_of(self.first_row(k) + start, 16), rows), :].astype(f32)
                self.total[0:rows, :] = mine + self.incoming(part, "c0", place)[...].astype(f32)
                for name, q, when in kids:

                    def add(name=name):
                        self.arrived(part, name, place)
                        self.total[0:rows, :] += self.incoming(part, name, place)[...].astype(f32)

                    guarded(when, add)
                if parent is None:
                    result[pl.ds(start, rows), :] = self.total[0:rows, :]
                else:
                    self.outgoing[place, pl.ds(start, rows), :] = self.total[0:rows, :].astype(bf)
                    push().start()

            guarded(cond, step)
            if parent is not None:
                finish.append((cond, lambda push=push: push().wait_send()))
                used += 1
        for cond, end in finish:
            guarded(cond, end)


def scatter_sends(grid, groups):
    return 2 * sum(len(grid.offsets(order)) for order in orders_of(groups))


def shard_groups(shard, count):
    first = [shard * k // GROUP for k in range(count)]
    groups = max(-(-shard * (k + 1) // GROUP) - first[k] for k in range(count))
    return first, max(groups, 2)


def flat_rows(shard, count):
    first, groups = shard_groups(shard, count)
    return 16 * (first[-1] + groups)


def matrix_rows():
    place, at = {}, 0
    for name, extent in tuple(layer_pieces()) + shared_pieces():
        if len(extent) == 2:
            place[name] = (at // 128, extent[0], extent[1] // 128)
        else:
            place[name] = (at // 128, 1, extent[0] // 128)
        at += math.prod(extent)
    return place


MATRICES = ("query_w", "key_w", "value_w", "output_w", "up_w", "down_w", "rel_table")
VECTORS = ("query_b", "key_b", "value_b", "output_b", "attn_gain", "attn_shift", "up_bias", "down_bias", "ffn_gain", "ffn_shift", "rel_gain", "rel_shift")


def vector_rows():
    place, at = {}, 0
    for name in VECTORS:
        wide = matrix_rows()[name][2]
        place[name] = (at, wide)
        at += wide
    return place, -(-at // 8) * 8


def gather_kernel(grid, shard, slot_ref, *refs):
    outs, vec_ref = refs[: len(MATRICES)], refs[len(MATRICES)]
    slots, wide, local_sem, send_sem, recv_sem = refs[len(MATRICES) + 1 :]
    p = grid.here()
    first, groups = shard_groups(shard, grid.count)
    enter(grid, p)
    own = pltpu.make_async_copy(slot_ref, slots.at[grid.flat(p)], local_sem)
    own.start()
    own.wait()
    Gather(grid, p, slots, send_sem, recv_sem, groups).run()
    last = shard * grid.count
    for k in range(grid.count):
        low, high = shard * k // GROUP, -(-shard * (k + 1) // GROUP)
        shared = k + 1 < grid.count and shard * (k + 1) % GROUP != 0
        begin = low + (1 if k > 0 and shard * k % GROUP != 0 else 0)
        end = high - (1 if shared else 0)
        if end > begin:
            wide[16 * begin : 16 * end, :] = slots[k, 16 * (begin - low) : 16 * (end - low), :].astype(f32)
        if shared:
            wide[16 * end : 16 * high, :] = slots[k, 16 * (end - low) : 16 * (high - low), :].astype(f32) + slots[k + 1, 0:16, :].astype(f32)
    place = matrix_rows()
    for name, out in zip(MATRICES, outs):
        base, rows, pieces = place[name]
        for c in range(pieces):
            out[:, 128 * c : 128 * c + 128] = wide[pl.ds(base + c, rows, stride=pieces), :].astype(bf)
    vec_at, vec_total = vector_rows()
    vec_ref[...] = jnp.zeros((vec_total, 128), f32)
    for name in VECTORS:
        base, _, pieces = place[name]
        vec_ref[vec_at[name][0] : vec_at[name][0] + pieces, :] = wide[base : base + pieces, :]


def gather_params(grid, shard, slot):
    _, groups = shard_groups(shard, grid.count)
    place = matrix_rows()
    vmem = pl.BlockSpec(memory_space=pltpu.VMEM)
    total = flat_rows(shard, grid.count)
    return pl.pallas_call(
        functools.partial(gather_kernel, grid, shard),
        out_shape=[jax.ShapeDtypeStruct((place[name][1], 128 * place[name][2]), bf) for name in MATRICES]
        + [jax.ShapeDtypeStruct((vector_rows()[1], 128), f32)],
        in_specs=[vmem],
        out_specs=[vmem] * (len(MATRICES) + 1),
        scratch_shapes=[
            pltpu.VMEM((grid.count, 16 * groups, 128), bf),
            pltpu.VMEM((total, 128), f32),
            pltpu.SemaphoreType.DMA,
            pltpu.SemaphoreType.DMA((count_sends(grid, groups),)),
            pltpu.SemaphoreType.DMA((len(orders_of(groups)), grid.count)),
        ],
        compiler_params=pltpu.CompilerParams(collective_id=0, has_side_effects=True, vmem_limit_bytes=48 << 20),
    )(slot)


def scatter_kernel(grid, shard, *refs):
    grads, vec_ref = refs[: len(MATRICES)], refs[len(MATRICES)]
    out_ref, wide, flat, kids, outgoing, total, send_sem, recv_sem = refs[len(MATRICES) + 1 :]
    p = grid.here()
    _, groups = shard_groups(shard, grid.count)
    place = matrix_rows()
    used = sum(math.prod(extent) for _, extent in tuple(layer_pieces()) + shared_pieces()) // 128
    wide[used - used % 8 :, :] = jnp.zeros((wide.shape[0] - used + used % 8, 128), f32)
    for name, ref in zip(MATRICES, grads):
        base, rows, pieces = place[name]
        for c in range(pieces):
            wide[pl.ds(base + c, rows, stride=pieces), :] = ref[:, 128 * c : 128 * c + 128]
    vec_at, _ = vector_rows()
    for name in VECTORS:
        base, _, pieces = place[name]
        wide[base : base + pieces, :] = vec_ref[vec_at[name][0] : vec_at[name][0] + pieces, :]
    flat[...] = wide[...].astype(bf)
    enter(grid, p)
    Scatter(grid, p, flat, lambda k: (k * shard // GROUP) * 16, kids, outgoing, total, send_sem, recv_sem, groups).run(out_ref)


def scatter_grads(grid, shard, grads, vec):
    _, groups = shard_groups(shard, grid.count)
    rows = flat_rows(shard, grid.count)
    vmem = pl.BlockSpec(memory_space=pltpu.VMEM)
    names, half = len(direction_names(grid)), grid.count // 2
    return pl.pallas_call(
        functools.partial(scatter_kernel, grid, shard),
        out_shape=jax.ShapeDtypeStruct((16 * groups, 128), f32),
        in_specs=[vmem] * (len(MATRICES) + 1),
        out_specs=vmem,
        scratch_shapes=[
            pltpu.VMEM((rows, 128), f32),
            pltpu.VMEM((rows, 128), bf),
            pltpu.VMEM((names, half, 16 * groups, 128), bf),
            pltpu.VMEM((half, 16 * groups, 128), bf),
            pltpu.VMEM((16 * groups, 128), f32),
            pltpu.SemaphoreType.DMA((scatter_sends(grid, groups),)),
            pltpu.SemaphoreType.DMA((len(orders_of(groups)), names, half)),
        ],
        compiler_params=pltpu.CompilerParams(collective_id=1, has_side_effects=True, vmem_limit_bytes=56 << 20),
    )(*grads, vec)


def vectors_of(vec):
    place, _ = vector_rows()
    return {name: vec[at : at + wide].reshape(-1) for name, (at, wide) in place.items()}


def paired(a):
    return a.reshape(a.shape[0],PAIRS,128).transpose(1,0,2)

def unpaired(a):
    return a.transpose(1,0,2).reshape(a.shape[1],D)

def untable(x):
    x=x.reshape(D,640).T
    y=x[:512][::-1]
    return y.at[511].add(jnp.sum(x[512:],axis=0))


def layer_forward(hidden, weights_of, pos_low, seg_ext):
    x_low = hidden.astype(jnp.bfloat16)
    query_low = (
        matmul(x_low, weights_of["query_w"]) + weights_of["query_b"].astype(jnp.float32)
    ).astype(jnp.bfloat16)
    key_low = (matmul(x_low, weights_of["key_w"]) + weights_of["key_b"].astype(jnp.float32)).astype(
        jnp.bfloat16
    )
    value_low = (
        matmul(x_low, weights_of["value_w"]) + weights_of["value_b"].astype(jnp.float32)
    ).astype(jnp.bfloat16)
    kv_ext = with_halo(jnp.stack([key_low, value_low]), (("seq", 1),), SPAN)
    pos_key = (
        matmul(pos_low, weights_of["key_w"]) + weights_of["key_b"].astype(jnp.float32)
    ).astype(jnp.bfloat16)
    pos_query = (
        matmul(pos_low, weights_of["query_w"]) + weights_of["query_b"].astype(jnp.float32)
    ).astype(jnp.bfloat16)
    key_table = paired(jnp.concatenate([pos_key[::-1], jnp.broadcast_to(pos_key[-1:], (128, D))], axis=0))
    query_table = paired(jnp.concatenate([pos_query[::-1], jnp.broadcast_to(pos_query[-1:], (128, D))], axis=0))
    tokens_here = x_low.shape[0]
    seg_rows = jnp.broadcast_to(seg_ext[SPAN : SPAN + tokens_here, None], (tokens_here, 128))
    qp, kp, vp = paired(query_low), paired(kv_ext[0]), paired(kv_ext[1])
    context, probs = att_fwd(qp, kp, vp, key_table, query_table, seg_rows, seg_ext[None])
    context = unpaired(context)
    context_low = context.astype(jnp.bfloat16)
    first_sum = (
        hidden
        + matmul(context_low, weights_of["output_w"])
        + weights_of["output_b"].astype(jnp.float32)
    )
    middle = layer_norm(
        first_sum,
        weights_of["attn_gain"].astype(jnp.float32),
        weights_of["attn_shift"].astype(jnp.float32),
    )
    middle_low = middle.astype(jnp.bfloat16)
    up_proj = matmul(middle_low, weights_of["up_w"]) + weights_of["up_bias"].astype(jnp.float32)
    act_low = gelu_exact(up_proj).astype(jnp.bfloat16)
    second_sum = (
        middle + matmul(act_low, weights_of["down_w"]) + weights_of["down_bias"].astype(jnp.float32)
    )
    output = layer_norm(
        second_sum,
        weights_of["ffn_gain"].astype(jnp.float32),
        weights_of["ffn_shift"].astype(jnp.float32),
    )
    saved = {
        "x_low": x_low,
        "att": (qp, kp, vp, key_table, query_table),
        "probs": probs,
        "context_low": context_low,
        "first_sum": first_sum,
        "middle_low": middle_low,
        "up_proj": up_proj,
        "act_low": act_low,
        "second_sum": second_sum,
    }
    return (output, saved)


def layer_backward(saved, weights_of, pos_low, seg_ext, grad_out):
    grads_of = {}
    tokens_here = saved["x_low"].shape[0]
    second_grad, grads_of["ffn_gain"], grads_of["ffn_shift"] = norm_grads(
        saved["second_sum"],
        weights_of["ffn_gain"].astype(jnp.float32),
        weights_of["ffn_shift"].astype(jnp.float32),
        grad_out,
    )
    down_grad = second_grad.astype(jnp.bfloat16)
    grads_of["down_w"] = matmul_tn(saved["act_low"], down_grad)
    grads_of["down_bias"] = jnp.sum(down_grad.astype(jnp.float32), axis=0)
    act_grad = matmul_nt(down_grad, weights_of["down_w"])
    up_grad = jax.vjp(gelu_exact, saved["up_proj"])[1](act_grad)[0].astype(jnp.bfloat16)
    grads_of["up_w"] = matmul_tn(saved["middle_low"], up_grad)
    grads_of["up_bias"] = jnp.sum(up_grad.astype(jnp.float32), axis=0)
    middle_grad = second_grad + matmul_nt(up_grad, weights_of["up_w"])
    first_grad, grads_of["attn_gain"], grads_of["attn_shift"] = norm_grads(
        saved["first_sum"],
        weights_of["attn_gain"].astype(jnp.float32),
        weights_of["attn_shift"].astype(jnp.float32),
        middle_grad,
    )
    attn_grad = first_grad.astype(jnp.bfloat16)
    grads_of["output_w"] = matmul_tn(saved["context_low"], attn_grad)
    grads_of["output_b"] = jnp.sum(attn_grad.astype(jnp.float32), axis=0)
    context_grad = matmul_nt(attn_grad, weights_of["output_w"]).astype(jnp.bfloat16)
    dquery, dkey_ext, dvalue_ext, dkr, dqr = att_bwd(*saved["att"], paired(context_grad), saved["probs"])
    dquery, dkey_ext, dvalue_ext = unpaired(dquery), unpaired(dkey_ext), unpaired(dvalue_ext)
    dpos_key, dpos_query = untable(dkr), untable(dqr)
    left_rim = jnp.stack([dkey_ext[:SPAN], dvalue_ext[:SPAN]])
    right_rim = jnp.stack([dkey_ext[SPAN + tokens_here :], dvalue_ext[SPAN + tokens_here :]])
    from_next = shifted(left_rim.astype(jnp.bfloat16), "seq", -1).astype(left_rim.dtype)
    from_prev = shifted(right_rim.astype(jnp.bfloat16), "seq", 1).astype(right_rim.dtype)
    head_pad = ((0, tokens_here - SPAN), (0, 0))
    tail_pad = ((tokens_here - SPAN, 0), (0, 0))
    dkey = (
        dkey_ext[SPAN : SPAN + tokens_here]
        + jnp.pad(from_prev[0], head_pad)
        + jnp.pad(from_next[0], tail_pad)
    )
    dvalue = (
        dvalue_ext[SPAN : SPAN + tokens_here]
        + jnp.pad(from_prev[1], head_pad)
        + jnp.pad(from_next[1], tail_pad)
    )
    dquery_low = dquery.astype(jnp.bfloat16)
    dkey_low = dkey.astype(jnp.bfloat16)
    dvalue_low = dvalue.astype(jnp.bfloat16)
    pos_wide = pos_low.astype(jnp.float32)
    key_wide = weights_of["key_w"].astype(jnp.float32)
    query_wide = weights_of["query_w"].astype(jnp.float32)
    x_low = saved["x_low"]
    grads_of["query_w"] = matmul_tn(x_low, dquery_low) + jnp.dot(
        pos_wide.T, dpos_query, precision=TOP_PRECISION
    )
    grads_of["key_w"] = matmul_tn(x_low, dkey_low) + jnp.dot(
        pos_wide.T, dpos_key, precision=TOP_PRECISION
    )
    grads_of["value_w"] = matmul_tn(x_low, dvalue_low)
    grads_of["query_b"] = jnp.sum(dquery_low.astype(jnp.float32), axis=0) + jnp.sum(
        dpos_query, axis=0
    )
    grads_of["key_b"] = jnp.sum(dkey_low.astype(jnp.float32), axis=0) + jnp.sum(dpos_key, axis=0)
    grads_of["value_b"] = jnp.sum(dvalue_low.astype(jnp.float32), axis=0)
    dpos = jnp.dot(dpos_key, key_wide.T, precision=TOP_PRECISION) + jnp.dot(
        dpos_query, query_wide.T, precision=TOP_PRECISION
    )
    grad_in = (
        first_grad
        + matmul_nt(dquery_low, weights_of["query_w"])
        + matmul_nt(dkey_low, weights_of["key_w"])
        + matmul_nt(dvalue_low, weights_of["value_w"])
    )
    return (grad_in, grads_of, dpos)


def on_device(layer_input, segment_ids, out_grad, weights, momentum, average):
    tokens_here = layer_input.shape[1]
    hidden = layer_input[0].astype(jnp.float32)
    seg_ext = with_halo(segment_ids[0] + 1, (("seq", 0),), SPAN)
    grid = Grid(lax.axis_size("seq"), lax.axis_size("row"))
    shard = weights.shape[0]
    _, groups = shard_groups(shard, grid.count)
    own_rank = lax.axis_index("seq") * grid.row + lax.axis_index("row")
    shift = own_rank * shard % GROUP
    slot = lax.dynamic_update_slice(jnp.zeros((GROUP * groups,), bf), weights.astype(bf), (shift,)).reshape(16 * groups, 128)
    *matrices, vec = gather_params(grid, shard, slot)
    weights_of = dict(zip(MATRICES, matrices)) | vectors_of(vec)
    shared = weights_of
    layers_list = [weights_of]
    table_wide = shared["rel_table"].astype(jnp.float32)
    table_gain = shared["rel_gain"].astype(jnp.float32)
    table_shift = shared["rel_shift"].astype(jnp.float32)
    pos_low = layer_norm(table_wide, table_gain, table_shift).astype(jnp.bfloat16)
    saved_list = []
    for weights_of in layers_list:
        hidden, saved = layer_forward(hidden, weights_of, pos_low, seg_ext)
        saved_list.append(saved)
    block_output = hidden.astype(jnp.bfloat16)
    back_layers = layers_list
    grad_hidden = out_grad[0].astype(jnp.float32)
    grad_hidden, grads_of, dpos = layer_backward(
        saved_list[0], back_layers[0], pos_low, seg_ext, grad_hidden
    )
    grads_reversed = [grads_of]
    shared_grads = {}
    shared_grads["rel_table"], shared_grads["rel_gain"], shared_grads["rel_shift"] = norm_grads(
        table_wide, table_gain, table_shift, dpos
    )
    grads_of.update(shared_grads)
    vec_at, vec_total = vector_rows()
    vec_grad = jnp.concatenate([grads_of[name].reshape(-1) for name in VECTORS])
    vec_grad = jnp.pad(vec_grad, (0, 128 * vec_total - vec_grad.shape[0])).reshape(vec_total, 128)
    summed = scatter_grads(grid, shard, [grads_of[name] for name in MATRICES], vec_grad)
    weight_grad = lax.dynamic_slice(summed.reshape(-1), (shift,), (shard,))
    all_tokens = tokens_here * lax.axis_size("seq") * layer_input.shape[0] * lax.axis_size("row")
    rate = 0.1 / math.sqrt(all_tokens)
    new_momentum = 0.5 * momentum + weight_grad
    new_weights = weights - rate * (weight_grad + 0.5 * new_momentum)
    new_average = 0.5 * average + 0.5 * new_weights
    return (
        block_output[None],
        grad_hidden[None],
        weight_grad,
        new_momentum,
        new_average,
        new_weights,
        new_weights.astype(jnp.bfloat16),
    )


def solution(mesh):
    placed = (
        P("row", "seq", None),
        P("row", "seq"),
        P("row", "seq", None),
        P(("seq", "row")),
        P(("seq", "row")),
        P(("seq", "row")),
    )
    return jax.shard_map(
        on_device,
        mesh=mesh,
        in_specs=placed,
        out_specs=(
            P("row", "seq", None),
            P("row", "seq", None),
            P(("seq", "row")),
            P(("seq", "row")),
            P(("seq", "row")),
            P(("seq", "row")),
            P(("seq", "row")),
        ),
        check_vma=False,
    )
```

```python
import functools
import itertools
import math

import jax
import jax.numpy as jnp
from jax import lax
from jax.experimental import pallas as pl
from jax.experimental.pallas import tpu as pltpu
from jax.sharding import PartitionSpec as P

D = 384
HEADS = 6
HEAD_DIM = 64
FF = 1536
SPAN = 256
PAIRS = HEADS // 2
NB = 5
EPSILON = 1e-07
bf = jnp.bfloat16
f32 = jnp.float32


MESH = pl.DeviceIdType.MESH
GROUP = 2048


class Grid:
    def __init__(self, seq, row):
        half = seq // 2
        wide = 1
        while wide * wide * 4 <= half:
            wide *= 2
        self.size = {"z": half // wide, "y": wide, "x": row}
        self.seq, self.row, self.count = seq, row, seq * row

    def here(self):
        s, x = lax.axis_index("seq"), lax.axis_index("row")
        y_size = self.size["y"]
        return {"z": s // (2 * y_size), "y": (s // 2) % y_size, "c": s % 2, "x": x}

    def seq_of(self, p):
        return (p["z"] * self.size["y"] + p["y"]) * 2 + p["c"]

    def flat(self, p):
        return self.seq_of(p) * self.row + p["x"]

    def device(self, p):
        return {"seq": self.seq_of(p), "row": p["x"]}

    def plane(self, p):
        return (p["z"] * self.size["y"] + p["y"]) * self.row + p["x"]

    def offsets(self, order):
        choices = []
        for axis in order:
            n = self.size[axis]
            if n == 2:
                choices.append([0, "f"])
            else:
                choices.append([0] + [sign * d for d in range(1, n) for sign in (-1, 1)])
        hops = lambda off: sum(1 if o == "f" else abs(o) for o in off)
        return sorted(itertools.product(*choices), key=hops)


def both(conds):
    out = None
    for cond in conds:
        if cond is not None:
            out = cond if out is None else jnp.logical_and(out, cond)
    return out


def guarded(cond, fn):
    if cond is None:
        fn()
    else:
        pl.when(cond)(fn)


def source_of(grid, p, order, off):
    o, conds = dict(p), []
    for axis, d in zip(order, off):
        if d == "f":
            o[axis] = 1 - p[axis]
        elif d != 0:
            o[axis] = p[axis] + d
            conds.append(p[axis] + d >= 0 if d < 0 else p[axis] + d < grid.size[axis])
    return o, both(conds)


def parent_of(grid, p, order, off):
    last = max((i for i, d in enumerate(off) if d != 0), default=None)
    if last is None:
        return None, None
    q, axis, d = dict(p), order[last], off[last]
    if d == "f":
        q[axis] = 1 - p[axis]
        return q, axis + "0"
    q[axis] = p[axis] + (1 if d > 0 else -1)
    return q, axis + ("+" if d > 0 else "-")


def children_of(grid, p, order, off):
    last = max((i for i, d in enumerate(off) if d != 0), default=None)
    found = []
    if last is not None and off[last] != "f":
        axis, away = order[last], (-1 if off[last] > 0 else 1)
        q = dict(p)
        q[axis] = p[axis] + away
        found.append((axis + ("+" if away > 0 else "-"), q, p[axis] > 0 if away < 0 else p[axis] < grid.size[axis] - 1))
    for axis in order[0 if last is None else last + 1 :]:
        if grid.size[axis] == 2:
            q = dict(p)
            q[axis] = 1 - p[axis]
            found.append((axis + "0", q, None))
        elif grid.size[axis] > 2:
            for sign in (1, -1):
                q = dict(p)
                q[axis] = p[axis] + sign
                found.append((axis + ("+" if sign > 0 else "-"), q, p[axis] > 0 if sign < 0 else p[axis] < grid.size[axis] - 1))
    return found


def neighbours_of(grid, p):
    found = []
    for axis in ("z", "y", "x"):
        found += children_of(grid, p, (axis,), (0,))
    sibling = dict(p)
    sibling["c"] = 1 - p["c"]
    found.append(("c0", sibling, None))
    return found


def enter(grid, p, extra=()):
    sem = pltpu.get_barrier_semaphore()
    total = jnp.int32(0)
    for name, q, cond in neighbours_of(grid, p) + list(extra):
        guarded(cond, lambda q=q: pl.semaphore_signal(sem, inc=1, device_id=grid.device(q), device_id_type=MESH))
        total = total + (1 if cond is None else cond.astype(jnp.int32))
    pl.semaphore_wait(sem, total)


def orders_of(groups):
    return (("z", "y", "x"), ("x", "z", "y")) if groups >= 8 else (("z", "y", "x"),)


def spans(groups):
    if groups < 8:
        return ((0, 16 * groups),)
    first = (groups * 20 + 16) // 32
    return ((0, 16 * first), (16 * first, 16 * (groups - first)))


class Gather:
    def __init__(self, grid, p, slots, send_sem, recv_sem, groups):
        self.grid, self.p, self.slots = grid, p, slots
        self.send_sem, self.recv_sem, self.groups = send_sem, recv_sem, groups
        self.sends, self.used = [], 0

    def copy(self, part, k, q, index):
        start, rows = spans(self.groups)[part]
        block = self.slots.at[k, pl.ds(start, rows), :]
        return pltpu.make_async_remote_copy(
            src_ref=block, dst_ref=block, send_sem=self.send_sem.at[index], recv_sem=self.recv_sem.at[part, k],
            device_id=self.grid.device(q), device_id_type=MESH)

    def arrived(self, part, k):
        start, rows = spans(self.groups)[part]
        block = self.slots.at[k, pl.ds(start, rows), :]
        pltpu.make_async_remote_copy(
            src_ref=block, dst_ref=block, send_sem=self.send_sem.at[0], recv_sem=self.recv_sem.at[part, k],
            device_id=self.grid.device(self.p), device_id_type=MESH).wait_recv()

    def run(self):
        grid, p = self.grid, self.p
        steps = []
        for part, order in enumerate(orders_of(self.groups)):
            for off in grid.offsets(order):
                steps.append((sum(1 if o == "f" else abs(o) for o in off), part, order, off))
        steps.sort(key=lambda item: item[:2])
        sibling = dict(p)
        sibling["c"] = 1 - p["c"]
        finish = []
        for hops, part, order, off in steps:
            o, cond = source_of(grid, p, order, off)
            k = grid.flat(o)
            targets = children_of(grid, p, order, off) + [("c0", sibling, None)]
            indices = [self.used + i for i in range(len(targets))]
            self.used += len(targets)

            def step(part=part, k=k, targets=targets, indices=indices, own=hops == 0):
                if not own:
                    self.arrived(part, k)
                for (name, q, when), index in zip(targets, indices):
                    guarded(when, lambda q=q, index=index: self.copy(part, k, q, index).start())

            guarded(cond, step)

            def end(part=part, k=k, targets=targets, indices=indices):
                for (name, q, when), index in zip(targets, indices):
                    guarded(when, lambda q=q, index=index: self.copy(part, k, q, index).wait_send())

            finish.append((cond, end))
        for part, order in enumerate(orders_of(self.groups)):
            for off in grid.offsets(order):
                o, cond = source_of(grid, sibling, order, off)
                guarded(cond, lambda part=part, k=grid.flat(o): self.arrived(part, k))
        for cond, end in finish:
            guarded(cond, end)

def count_sends(grid, groups):
    fake = {"z": jnp.int32(0), "y": jnp.int32(0), "x": jnp.int32(0), "c": jnp.int32(0)}
    return sum(len(children_of(grid, fake, order, off)) + 1 for order in orders_of(groups) for off in grid.offsets(order))


OPPOSITE = {"+": "-", "-": "+", "0": "0"}


def direction_names(grid):
    names = ["c0"]
    for axis in ("z", "y", "x"):
        if grid.size[axis] == 2:
            names.append(axis + "0")
        elif grid.size[axis] > 2:
            names += [axis + "+", axis + "-"]
    return names


class Scatter:
    def __init__(self, grid, p, flat, first_row, kids, outgoing, total, send_sem, recv_sem, groups):
        self.grid, self.p, self.flat, self.first_row = grid, p, flat, first_row
        self.kids, self.outgoing, self.total = kids, outgoing, total
        self.send_sem, self.recv_sem, self.groups = send_sem, recv_sem, groups
        self.names = direction_names(grid)

    def incoming(self, part, name, place):
        start, rows = spans(self.groups)[part]
        return self.kids.at[self.names.index(name), place, pl.ds(start, rows), :]

    def transfer(self, source, part, name, place, q, send):
        return pltpu.make_async_remote_copy(
            src_ref=source, dst_ref=self.incoming(part, name, place), send_sem=self.send_sem.at[send],
            recv_sem=self.recv_sem.at[part, self.names.index(name), place], device_id=self.grid.device(q), device_id_type=MESH)

    def arrived(self, part, name, place):
        block = self.incoming(part, name, place)
        pltpu.make_async_remote_copy(
            src_ref=block, dst_ref=block, send_sem=self.send_sem.at[0],
            recv_sem=self.recv_sem.at[part, self.names.index(name), place],
            device_id=self.grid.device(self.p), device_id_type=MESH).wait_recv()

    def run(self, result):
        grid, p = self.grid, self.p
        sibling = dict(p)
        sibling["c"] = 1 - p["c"]
        steps = []
        for part, order in enumerate(orders_of(self.groups)):
            for off in grid.offsets(order):
                steps.append((-sum(1 if o == "f" else abs(o) for o in off), part, order, off))
        steps.sort(key=lambda item: item[:2])
        used, finish = 0, []
        for hops, part, order, off in steps:
            o, cond = source_of(grid, sibling, order, off)
            start, rows = spans(self.groups)[part]

            def give(part=part, o=o, index=used, start=start, rows=rows):
                block = self.flat.at[pl.ds(pl.multiple_of(self.first_row(grid.flat(o)) + start, 16), rows), :]
                return self.transfer(block, part, "c0", grid.plane(o), sibling, index)

            guarded(cond, lambda give=give: give().start())
            finish.append((cond, lambda give=give: give().wait_send()))
            used += 1
        for hops, part, order, off in steps:
            o, cond = source_of(grid, p, order, off)
            place, k = grid.plane(o), grid.flat(o)
            start, rows = spans(self.groups)[part]
            kids = children_of(grid, p, order, off)
            parent, side = parent_of(grid, p, order, off)

            def push(part=part, place=place, parent=parent, side=side, index=used, start=start, rows=rows):
                block = self.outgoing.at[place, pl.ds(start, rows), :]
                return self.transfer(block, part, side[0] + OPPOSITE[side[1]], place, parent, index)

            def step(part=part, place=place, k=k, kids=kids, parent=parent, start=start, rows=rows, push=push):
                self.arrived(part, "c0", place)
                mine = self.flat[pl.ds(pl.multiple_of(self.first_row(k) + start, 16), rows), :].astype(f32)
                self.total[0:rows, :] = mine + self.incoming(part, "c0", place)[...].astype(f32)
                for name, q, when in kids:

                    def add(name=name):
                        self.arrived(part, name, place)
                        self.total[0:rows, :] += self.incoming(part, name, place)[...].astype(f32)

                    guarded(when, add)
                if parent is None:
                    result[pl.ds(start, rows), :] = self.total[0:rows, :]
                else:
                    self.outgoing[place, pl.ds(start, rows), :] = self.total[0:rows, :].astype(bf)
                    push().start()

            guarded(cond, step)
            if parent is not None:
                finish.append((cond, lambda push=push: push().wait_send()))
                used += 1
        for cond, end in finish:
            guarded(cond, end)


def scatter_sends(grid, groups):
    return 2 * sum(len(grid.offsets(order)) for order in orders_of(groups))


def shard_groups(shard, count):
    first = [shard * k // GROUP for k in range(count)]
    groups = max(-(-shard * (k + 1) // GROUP) - first[k] for k in range(count))
    return first, max(groups, 2)


def flat_rows(shard, count):
    first, groups = shard_groups(shard, count)
    return 16 * (first[-1] + groups)


def layer_pieces():
    square, vector_of = (D, D), (D,)
    return (
        ("query_w", square), ("key_w", square), ("value_w", square), ("output_w", square), ("up_w", (D, FF)), ("down_w", (FF, D)),
        ("query_b", vector_of), ("key_b", vector_of), ("value_b", vector_of), ("output_b", vector_of), ("attn_gain", vector_of),
        ("attn_shift", vector_of), ("up_bias", (FF,)), ("down_bias", vector_of), ("ffn_gain", vector_of), ("ffn_shift", vector_of),
        ("rel_table", (2 * SPAN, D)), ("rel_gain", vector_of), ("rel_shift", vector_of),
    )


def matrix_rows():
    place, at = {}, 0
    for name, extent in layer_pieces():
        if len(extent) == 2:
            place[name] = (at // 128, extent[0], extent[1] // 128)
        else:
            place[name] = (at // 128, 1, extent[0] // 128)
        at += math.prod(extent)
    return place


MATRICES = ("query_w", "key_w", "value_w", "output_w", "up_w", "down_w", "rel_table")
VECTORS = tuple(name for name, extent in layer_pieces() if len(extent) == 1)
FEED_FIRST = matrix_rows()["output_w"][0]
FEED_ROWS = matrix_rows()["query_b"][0] - FEED_FIRST
USED_ROWS = sum(rows * pieces for _, rows, pieces in matrix_rows().values())


def vector_rows():
    place, at = {}, 0
    for name in VECTORS:
        wide = matrix_rows()[name][2]
        place[name] = (at, wide)
        at += wide
    return place, -(-at // 8) * 8


SC = 1.0/math.sqrt(3.0*HEAD_DIM)
LOG2E = 1.4426950408889634
NT=(((1,),(1,)),((),())); NN=(((1,),(0,)),((),())); TN=(((0,),(0,)),((),()))
def dot(a,b,d=NN): return lax.dot_general(a,b,d,preferred_element_type=f32)

def head_mask(rows, h):
    lane=lax.broadcasted_iota(jnp.int32,(rows,128),1)
    return (lane<64) if h==0 else (lane>=64)
def keep(x,h):
    return jnp.where(head_mask(x.shape[0],h), x, jnp.zeros_like(x))

def skew(A):
    return jnp.concatenate([pltpu.roll(A[8*g:8*g+8,:512],8*g+1,1,stride=1,stride_axis=0) for g in range(16)],axis=0)


def att_fwd_body(nblk, q_ref,k_ref,v_ref,krt_ref,qrt_ref,seg_ref,ctx_ref,p_ref,x_scr,bias_scr):
    row=lax.broadcasted_iota(jnp.int32,(128,128),0); lane=lax.broadcasted_iota(jnp.int32,(128,128),1)
    eye=(row==lane).astype(bf)
    def mk_bias(t,c):
        off=pl.multiple_of(t*128,128)
        sq=jnp.broadcast_to(seg_ref[0:1,pl.ds(pl.multiple_of(off+SPAN,128),128)],(128,128)).astype(f32).T
        for b in range(NB):
            sk=seg_ref[0:1,pl.ds(pl.multiple_of(off+128*b,128),128)].astype(f32)
            ok = sq==sk
            if b==0: ok = ok & (lane>=row)
            if b==NB-1: ok = ok & (lane<=row)
            bias_scr[t,:,128*b:128*b+128]=jnp.where(ok,0.0,-1e30).astype(f32)
        return c
    lax.fori_loop(0,nblk,mk_bias,0)
    def pair(p,c):
        def keyside(J):
            kj=k_ref[p,pl.ds(pl.multiple_of(jnp.minimum(J,nblk+3)*128,128),128),:]
            for h in range(2):
                C=dot(keep(kj,h),qrt_ref[p],NT)
                R=skew(C)
                x_scr[h,J,:,0:128]=jnp.where(lane>row,R[:,:128],C[:,512:]).astype(bf)
                x_scr[h,J,:,128:512]=R[:,128:].astype(bf)
                x_scr[h,J,:,512:640]=R[:,:128].astype(bf)
        def st(J,c):
            keyside(J); return c
        lax.fori_loop(0,5,st,0)
        def qblock(t,c):
            off=pl.multiple_of(t*128,128)
            qt=q_ref[p,pl.ds(off,128),:]
            kw=[k_ref[p,pl.ds(pl.multiple_of(off+128*b,128),128),:] for b in range(NB)]
            vw=v_ref[p,pl.ds(off,640),:]
            ctx=[]
            for h in range(2):
                qm=keep(qt,h)
                A=dot(qm,krt_ref[p],NT)
                R=skew(A)
                lhs=jnp.concatenate([qm,eye],axis=1)
                rhs=jnp.concatenate([jnp.concatenate([kw[b],x_scr[h,t+b,:,128*(4-b):128*(5-b)]],axis=1) for b in range(NB)],axis=0)
                S=dot(lhs,rhs,NT)
                Y=jnp.concatenate([jnp.where(lane>row,R[:,:128],A[:,512:]),R[:,128:],R[:,:128]],axis=1)
                S=S+Y+bias_scr[t]
                m=jnp.max(S,axis=1,keepdims=True)
                e=jnp.exp2((S-m)*(SC*LOG2E))
                s=jnp.sum(e,axis=1,keepdims=True)
                P=(e*(1.0/s)).astype(bf)
                p_ref[p,t,h]=P
                ctx.append(dot(P,vw,NN))
            ctx_ref[p,pl.ds(off,128),:]=jnp.where(lane<64,ctx[0],ctx[1]).astype(bf)
            keyside(c)
            return c+1
        lax.fori_loop(0,nblk,qblock,jnp.int32(5))
        return c
    lax.fori_loop(0,PAIRS,pair,0)

def unskew(Grev):
    return jnp.concatenate([pltpu.roll(Grev[8*g:8*g+8],384+8*g,1,stride=1,stride_axis=0) for g in range(16)],axis=0)

def unrev(x, J):
    hi=x.astype(bf); lo=(x-hi.astype(f32)).astype(bf)
    y=dot(J,jnp.concatenate([hi,lo],axis=1))
    return y[:,:128]+y[:,128:]

def att_bwd_body(nblk, q_ref,k_ref,v_ref,krt_ref,qrt_ref,dctx_ref,p_ref,dq_ref,dk_ref,dv_ref,dkr_ref,dqr_ref,gt_scr,dvt_scr):
    row=lax.broadcasted_iota(jnp.int32,(128,128),0); lane=lax.broadcasted_iota(jnp.int32,(128,128),1)
    JR=(row+lane==127).astype(bf)
    gt_scr[...]=jnp.zeros(gt_scr.shape,bf)
    zero=jnp.zeros((128,128),bf)
    def pair(p,c):
        dvt_scr[...]=jnp.zeros(dvt_scr.shape,f32)
        dkr_ref[p]=jnp.zeros((128,640),f32)
        dqr_ref[p]=jnp.zeros((128,640),f32)
        def qblock(t,J0):
            off=pl.multiple_of(t*128,128)
            qt=q_ref[p,pl.ds(off,128),:]
            qT=qt.T
            qTr=dot(qT,JR).astype(bf)
            dct=dctx_ref[p,pl.ds(off,128),:]
            dcT=dct.T
            kw=k_ref[p,pl.ds(off,640),:]
            vw=v_ref[p,pl.ds(off,640),:]
            krt=krt_ref[p]
            dq1=[]; dq2=[]
            for h in range(2):
                dp=dot(keep(dct,h),vw,NT)
                Pb=p_ref[p,t,h]
                Pf=Pb.astype(f32)
                w=Pf*dp
                inner=jnp.sum(w,axis=1,keepdims=True)
                G=(w-Pf*inner).astype(bf)
                Gd=jnp.where(lane==row,G[:,:128],zero)
                Gm=jnp.concatenate([jnp.where(lane>row,G[:,:128],G[:,512:]),G[:,128:512]],axis=1)
                Gu=unskew(dot(JR,Gm)).astype(bf)
                dq1.append(dot(jnp.concatenate([G,Gd],axis=1),jnp.concatenate([kw,krt[512:]],axis=0)))
                dq2.append(dot(Gu,krt[:512]))
                hs=slice(64*h,64*h+64)
                dkr_ref[p,hs,0:512]+=dot(qTr[hs],Gu)
                dkr_ref[p,hs,512:640]+=dot(qT[hs],Gd)
                dvt_scr[hs,pl.ds(off,640)]+=dot(dcT[hs],Pb)
                for b in range(NB):
                    gt_scr[h,J0+b,:,128*(4-b):128*(5-b)]=dot(JR,G[:,128*b:128*b+128],NT).astype(bf)
            dq=jnp.where(lane<64,dq1[0],dq1[1])+unrev(jnp.where(lane<64,dq2[0],dq2[1]),JR)
            dq_ref[p,pl.ds(off,128),:]=(SC*dq).astype(bf)
            return J0+1
        lax.fori_loop(0,nblk,qblock,jnp.int32(0))
        def kblock(J,c):
            off=pl.multiple_of(J*128,128)
            kj=k_ref[p,pl.ds(off,128),:]
            kT=kj.T
            kTr=dot(kT,JR).astype(bf)
            qw=jnp.concatenate([q_ref[p,pl.ds(pl.multiple_of(jnp.clip(J-4+w,0,nblk-1)*128,128),128),:] for w in range(NB)],axis=0)
            rhs=jnp.concatenate([qw,qrt_ref[p]],axis=0)
            dks=[]
            for h in range(2):
                GT=gt_scr[h,J]
                Gd=jnp.where(lane+row==127,GT[:,:128],zero)
                Gm=jnp.concatenate([jnp.where(lane+row>127,GT[:,:128],GT[:,512:]),GT[:,128:512]],axis=1).astype(f32)
                Gu=unskew(Gm).astype(bf)
                Gx=jnp.concatenate([Gu,Gd],axis=1)
                dks.append(dot(jnp.concatenate([GT,Gx],axis=1),rhs))
                hs=slice(64*h,64*h+64)
                dqr_ref[p,hs,:]+=dot(kTr[hs],Gx)
            dk_ref[p,pl.ds(off,128),:]=SC*unrev(jnp.where(lane<64,dks[0],dks[1]),JR)
            dv_ref[p,pl.ds(off,128),:]=dvt_scr[:,pl.ds(off,128)].T
            return c
        lax.fori_loop(0,nblk+4,kblock,0)
        dkr_ref[p]=SC*dkr_ref[p]
        dqr_ref[p]=SC*dqr_ref[p]
        return c
    lax.fori_loop(0,PAIRS,pair,0)

def att_bwd(q,k,v,krt,qrt,dctx,P):
    T=q.shape[1]; nblk=T//128; E=T+512
    return pl.pallas_call(functools.partial(att_bwd_body,nblk),
        out_shape=[jax.ShapeDtypeStruct((PAIRS,T,128),bf),jax.ShapeDtypeStruct((PAIRS,E,128),f32),jax.ShapeDtypeStruct((PAIRS,E,128),f32),
          jax.ShapeDtypeStruct((PAIRS,128,640),f32),jax.ShapeDtypeStruct((PAIRS,128,640),f32)],
        scratch_shapes=[pltpu.VMEM((2,nblk+4,128,640),bf),pltpu.VMEM((128,E),f32)],
        compiler_params=pltpu.CompilerParams(vmem_limit_bytes=48<<20),
    )(q,k,v,krt,qrt,dctx,P)


def vector(vec_ref, name):
    at, wide = vector_rows()[0][name]
    return jnp.concatenate([vec_ref[at + i : at + i + 1, :] for i in range(wide)], axis=1)


def put_vector(vec_ref, name, value):
    at, wide = vector_rows()[0][name]
    for i in range(wide):
        vec_ref[at + i : at + i + 1, :] = value[:, 128 * i : 128 * i + 128]


def add_vector(vec_ref, name, value):
    at, wide = vector_rows()[0][name]
    for i in range(wide):
        vec_ref[at + i : at + i + 1, :] += value[:, 128 * i : 128 * i + 128]


def normalized(values):
    centered = values - jnp.mean(values, axis=1, keepdims=True)
    inverse = lax.rsqrt(jnp.mean(centered * centered, axis=1, keepdims=True) + EPSILON)
    return centered * inverse, inverse


def norm_back(upstream, gain, unit, inverse):
    scaled = upstream * gain
    mean = jnp.mean(scaled, axis=1, keepdims=True)
    along = jnp.mean(scaled * unit, axis=1, keepdims=True)
    return inverse * (scaled - mean - unit * along)


def column_sum(values):
    return jnp.sum(values, axis=0, keepdims=True)


def reversal():
    row = lax.broadcasted_iota(jnp.int32, (128, 128), 0)
    lane = lax.broadcasted_iota(jnp.int32, (128, 128), 1)
    return (row + lane == 127).astype(bf)


def reversed_rows(values, JR):
    blocks = values.shape[0] // 128
    return jnp.concatenate([dot(JR, values[128 * b : 128 * b + 128]).astype(bf) for b in reversed(range(blocks))], axis=0)


def project_body(x_ref, query_w, key_w, value_w, table_ref, vec_ref, q_ref, k_ref, v_ref, krt_ref, qrt_ref, pos_ref):
    tokens = q_ref.shape[1]
    JR = reversal()
    unit, _ = normalized(table_ref[...].astype(f32))
    pos = (unit * vector(vec_ref, "rel_gain") + vector(vec_ref, "rel_shift")).astype(bf)
    pos_rev = reversed_rows(pos, JR)
    pos_ref[...] = pos_rev
    for w, b, out in ((key_w, "key_b", krt_ref), (query_w, "query_b", qrt_ref)):
        table = (dot(pos_rev, w[...]) + vector(vec_ref, b)).astype(bf)
        for p in range(PAIRS):
            out[p, 0:512, :] = table[:, 128 * p : 128 * p + 128]
            out[p, 512:640, :] = jnp.broadcast_to(table[0:1, 128 * p : 128 * p + 128], (128, 128))

    bias = {name: vector(vec_ref, name) for name in ("query_b", "key_b", "value_b")}

    def chunk(i, carry):
        rows = pl.ds(pl.multiple_of(i * 256, 256), 256)
        x = x_ref[rows, :]
        for w, b, out in ((key_w, "key_b", k_ref), (value_w, "value_b", v_ref)):
            y = (dot(x, w[...]) + bias[b]).astype(bf)
            for p in range(PAIRS):
                out[p, rows, :] = y[:, 128 * p : 128 * p + 128]
        return carry

    lax.fori_loop(0, x_ref.shape[0] // 256, chunk, 0)

    def own(i, carry):
        rows = pl.ds(pl.multiple_of(i * 256, 256), 256)
        x = x_ref[pl.ds(pl.multiple_of(i * 256 + SPAN, 256), 256), :]
        y = (dot(x, query_w[...]) + bias["query_b"]).astype(bf)
        for p in range(PAIRS):
            q_ref[p, rows, :] = y[:, 128 * p : 128 * p + 128]
        return carry

    lax.fori_loop(0, tokens // 256, own, 0)


SQRT_HALF = 0.7071067811865476
PHI_SCALE = 0.3989422804014327


def gelu_and_slope(u):
    cdf = 0.5 + 0.5 * lax.erf(u * SQRT_HALF)
    return u * cdf, cdf + u * (PHI_SCALE * jnp.exp(-0.5 * u * u))


def feed_body(x_ref, ctx_ref, og_ref, output_w, up_w, down_w, vec_ref, out_ref, dz1_ref, dctx_ref, wide, dvec_ref,
              ml_scr, dup_scr, act_scr, ddown_scr, dattn_scr, slope_scr):
    tokens = out_ref.shape[0]
    dvec_ref[...] = jnp.zeros(dvec_ref.shape, f32)
    vecs = {name: vector(vec_ref, name) for name in ("output_b", "attn_gain", "attn_shift", "up_bias", "down_bias", "ffn_gain", "ffn_shift")}
    C = 256

    def chunk(i, carry):
        rows = pl.ds(pl.multiple_of(i * C, C), C)
        h = x_ref[pl.ds(pl.multiple_of(i * C + SPAN, C), C), :].astype(f32)
        z1 = h + dot(jnp.concatenate([ctx_ref[p, rows, :] for p in range(PAIRS)], axis=1), output_w[...]) + vecs["output_b"]
        unit1, inv1 = normalized(z1)
        mid = unit1 * vecs["attn_gain"] + vecs["attn_shift"]
        ml = mid.astype(bf)
        ml_scr[rows, :] = ml
        z2 = mid + vecs["down_bias"]
        for f in range(FF // 256):
            cols = slice(256 * f, 256 * f + 256)
            up = dot(ml, up_w[:, cols]) + vecs["up_bias"][:, cols]
            act, slope = gelu_and_slope(up)
            act_scr[rows, cols] = act.astype(bf)
            slope_scr[:, cols] = slope
        z2 = z2 + dot(act_scr[rows, :], down_w[...])
        unit2, inv2 = normalized(z2)
        out_ref[rows, :] = (unit2 * vecs["ffn_gain"] + vecs["ffn_shift"]).astype(bf)
        dh = og_ref[rows, :].astype(f32)
        add_vector(dvec_ref, "ffn_gain", column_sum(dh * unit2))
        add_vector(dvec_ref, "ffn_shift", column_sum(dh))
        dz2 = norm_back(dh, vecs["ffn_gain"], unit2, inv2)
        ddown = dz2.astype(bf)
        ddown_scr[rows, :] = ddown
        add_vector(dvec_ref, "down_bias", column_sum(ddown.astype(f32)))
        for f in range(FF // 256):
            cols = slice(256 * f, 256 * f + 256)
            dup = (dot(ddown, down_w[cols, :], NT) * slope_scr[:, cols]).astype(bf)
            dup_scr[rows, cols] = dup
        add_vector(dvec_ref, "up_bias", column_sum(dup_scr[rows, :].astype(f32)))
        dmid = dz2 + dot(dup_scr[rows, :], up_w[...], NT)
        add_vector(dvec_ref, "attn_gain", column_sum(dmid * unit1))
        add_vector(dvec_ref, "attn_shift", column_sum(dmid))
        dz1 = norm_back(dmid, vecs["attn_gain"], unit1, inv1)
        dz1_ref[rows, :] = dz1
        dattn = dz1.astype(bf)
        dattn_scr[rows, :] = dattn
        add_vector(dvec_ref, "output_b", column_sum(dattn.astype(f32)))
        dctx = dot(dattn, output_w[...], NT).astype(bf)
        for p in range(PAIRS):
            dctx_ref[p, rows, :] = dctx[:, 128 * p : 128 * p + 128]
        return carry

    lax.fori_loop(0, tokens // C, chunk, 0)
    place = matrix_rows()

    def put(name, first, rows, value):
        base, _, pieces = place[name]
        for c in range(value.shape[1] // 128):
            wide[pl.ds(base - FEED_FIRST + pieces * first[0] + first[1] + c, rows, stride=pieces), :] = value[:, 128 * c : 128 * c + 128]

    ctx = jnp.concatenate([ctx_ref[p] for p in range(PAIRS)], axis=1)
    put("output_w", (0, 0), D, dot(ctx, dattn_scr[...], TN))
    for f in range(FF // 256):
        cols = slice(256 * f, 256 * f + 256)
        put("up_w", (0, 2 * f), D, dot(ml_scr[...], dup_scr[:, cols], TN))
        put("down_w", (256 * f, 0), 256, dot(act_scr[:, cols], ddown_scr[...], TN))


def split(values):
    high = values.astype(bf)
    return high, (values - high.astype(f32)).astype(bf)


def dot2(left, right, dims=NN):
    if left.dtype == f32:
        return sum(dot(part, right, dims) for part in split(left))
    return sum(dot(left, part, dims) for part in split(right))


def tail_local(dq_ref, x_ref, dz1_ref, query_w, dx_ref, dwq_ref, dvec_ref):
    tokens = dx_ref.shape[0]
    dq = jnp.concatenate([dq_ref[p] for p in range(PAIRS)], axis=1)
    dx_ref[...] = dz1_ref[...] + dot(dq, query_w[...], NT)
    dwq_ref[...] = dot(x_ref[SPAN : SPAN + tokens, :], dq, TN)
    put_vector(dvec_ref, "query_b", column_sum(dq.astype(f32)))


def tail_table(dkr_ref, dqr_ref, pos_ref, table_ref, vec_ref, query_w, key_w, dwq_ref, dwk_ref, dtable_ref, dvec_ref):
    JR = reversal()
    first = lax.broadcasted_iota(jnp.int32, (512, 384), 0) == 0
    dpos = None
    for ref, w, dw, name in ((dkr_ref, key_w, dwk_ref, "key_b"), (dqr_ref, query_w, dwq_ref, "query_b")):
        halves = jnp.concatenate([ref[p].T for p in range(PAIRS)], axis=1)
        tab = halves[:512] + jnp.where(first, column_sum(halves[512:]), 0.0)
        if name == "key_b":
            dw[...] = dot2(pos_ref[...], tab, TN)
            put_vector(dvec_ref, name, column_sum(tab))
        else:
            dw[...] += dot2(pos_ref[...], tab, TN)
            add_vector(dvec_ref, name, column_sum(tab))
        part = dot2(tab, w[...], NT)
        dpos = part if dpos is None else dpos + part
    unit, inverse = normalized(jnp.concatenate([dot(JR, table_ref[128 * b : 128 * b + 128, :]) for b in reversed(range(4))], axis=0))
    put_vector(dvec_ref, "rel_gain", column_sum(dpos * unit))
    put_vector(dvec_ref, "rel_shift", column_sum(dpos))
    dpos = norm_back(dpos, vector(vec_ref, "rel_gain"), unit, inverse).astype(bf)
    for b in range(4):
        dtable_ref[128 * b : 128 * b + 128, :] = dot(JR, dpos[128 * (3 - b) : 128 * (4 - b)])


def tail_keys(dk_ref, dv_ref, halo_ref, x_ref, key_w, value_w, dx_ref, dwk_ref, dwv_ref, dvec_ref):
    tokens = dx_ref.shape[0]
    x = x_ref[SPAN : SPAN + tokens, :]
    for which, (ref, w, dw, name) in enumerate(((dk_ref, key_w, dwk_ref, "key_b"), (dv_ref, value_w, dwv_ref, "value_b"))):
        pieces = []
        for p in range(PAIRS):
            own = ref[p, SPAN : SPAN + tokens, :]
            edge = [halo_ref[side, which, p].astype(f32) for side in (0, 1)]
            pieces.append(jnp.concatenate([own[:SPAN] + edge[0], own[SPAN : tokens - SPAN], own[tokens - SPAN :] + edge[1]], axis=0).astype(bf))
        d = jnp.concatenate(pieces, axis=1)
        dx_ref[...] += dot(d, w[...], NT)
        if name == "key_b":
            dw[...] += dot(x, d, TN)
            add_vector(dvec_ref, name, column_sum(d.astype(f32)))
        else:
            dw[...] = dot(x, d, TN)
            put_vector(dvec_ref, name, column_sum(d.astype(f32)))


def beside(grid, step):
    return {"seq": lax.axis_index("seq") + step, "row": lax.axis_index("row")}


def seq_edges(grid):
    s = lax.axis_index("seq")
    return s > 0, s < grid.seq - 1


def enter_all(grid, p):
    sem = pltpu.get_barrier_semaphore()
    total = jnp.int32(0)
    before, after = seq_edges(grid)
    targets = [(grid.device(q), cond) for _, q, cond in neighbours_of(grid, p)]
    targets += [(beside(grid, -1), before), (beside(grid, 1), after)]
    for device, cond in targets:
        guarded(cond, lambda device=device: pl.semaphore_signal(sem, inc=1, device_id=device, device_id_type=MESH))
        total = total + (1 if cond is None else cond.astype(jnp.int32))
    pl.semaphore_wait(sem, total)


def remote(source, target, send_sem, recv_sem, device):
    return pltpu.make_async_remote_copy(
        src_ref=source, dst_ref=target, send_sem=send_sem, recv_sem=recv_sem, device_id=device, device_id_type=MESH)


def assemble(grid, shard, slots, wide):
    for k in range(grid.count):
        low, high = shard * k // GROUP, -(-shard * (k + 1) // GROUP)
        shared = k + 1 < grid.count and shard * (k + 1) % GROUP != 0
        begin = low + (1 if k > 0 and shard * k % GROUP != 0 else 0)
        end = high - (1 if shared else 0)
        if end > begin:
            wide[16 * begin : 16 * end, :] = slots[k, 16 * (begin - low) : 16 * (end - low), :].astype(f32)
        if shared:
            wide[16 * end : 16 * high, :] = slots[k, 16 * (end - low) : 16 * (high - low), :].astype(f32) + slots[k + 1, 0:16, :].astype(f32)


def unpack(wide, outs, vec_ref):
    place = matrix_rows()
    for name, out in zip(MATRICES, outs):
        base, rows, pieces = place[name]
        for c in range(pieces):
            out[:, 128 * c : 128 * c + 128] = wide[pl.ds(base + c, rows, stride=pieces), :].astype(bf)
    vec_at, vec_total = vector_rows()
    vec_ref[...] = jnp.zeros((vec_total, 128), f32)
    for name in VECTORS:
        base, _, pieces = place[name]
        vec_ref[vec_at[name][0] : vec_at[name][0] + pieces, :] = wide[base : base + pieces, :]


def gather_kernel(grid, shard, slot_ref, x_ref, seg_ref, *refs):
    many = len(MATRICES)
    outs, (vec_ref, x_ext, seg_ext) = refs[:many], refs[many : many + 3]
    slots, wide, local_sem, send_sem, recv_sem, halo_send, halo_recv = refs[many + 3 :]
    p = grid.here()
    tokens = x_ref.shape[0]
    _, groups = shard_groups(shard, grid.count)
    before, after = seq_edges(grid)
    own = pltpu.make_async_copy(slot_ref, slots.at[grid.flat(p)], local_sem)
    own.start()
    enter_all(grid, p)
    own.wait()

    def halo_copies(side):
        step = -1 if side == 0 else 1
        take = pl.ds(0, SPAN) if side == 0 else pl.ds(tokens - SPAN, SPAN)
        land = pl.ds(tokens + SPAN, SPAN) if side == 0 else pl.ds(0, SPAN)
        return [
            remote(x_ref.at[take, :], x_ext.at[land, :], halo_send.at[side, 0], halo_recv.at[side, 0], beside(grid, step)),
            remote(seg_ref.at[:, take], seg_ext.at[:, land], halo_send.at[side, 1], halo_recv.at[side, 1], beside(grid, step)),
        ]

    def start(side):
        for copy in halo_copies(side):
            copy.start()

    pl.when(before)(lambda: start(0))
    pl.when(after)(lambda: start(1))

    def clear(rows):
        x_ext[rows, :] = jnp.zeros((SPAN, D), bf)
        seg_ext[:, rows] = jnp.zeros((8, SPAN), jnp.int32)

    pl.when(jnp.logical_not(before))(lambda: clear(pl.ds(0, SPAN)))
    pl.when(jnp.logical_not(after))(lambda: clear(pl.ds(tokens + SPAN, SPAN)))
    x_ext[SPAN : SPAN + tokens, :] = x_ref[...]
    seg_ext[:, SPAN : SPAN + tokens] = seg_ref[...]
    Gather(grid, p, slots, send_sem, recv_sem, groups).run()
    assemble(grid, shard, slots, wide)
    unpack(wide, outs, vec_ref)

    def end(side):
        for copy in halo_copies(side):
            copy.wait_send()

    def landed(side):
        for copy in halo_copies(side):
            copy.wait_recv()

    pl.when(before)(lambda: end(0))
    pl.when(after)(lambda: end(1))
    pl.when(after)(lambda: landed(0))
    pl.when(before)(lambda: landed(1))


VMEM = pl.BlockSpec(memory_space=pltpu.VMEM)


def matrix_shapes(dtype):
    return [jax.ShapeDtypeStruct((matrix_rows()[name][1], 128 * matrix_rows()[name][2]), dtype) for name in MATRICES]


def gather_params(grid, shard, slot, x, seg):
    _, groups = shard_groups(shard, grid.count)
    tokens = x.shape[0]
    total = flat_rows(shard, grid.count)
    return pl.pallas_call(
        functools.partial(gather_kernel, grid, shard),
        out_shape=matrix_shapes(bf)
        + [
            jax.ShapeDtypeStruct((vector_rows()[1], 128), f32),
            jax.ShapeDtypeStruct((tokens + 2 * SPAN, D), bf),
            jax.ShapeDtypeStruct((8, tokens + 2 * SPAN), jnp.int32),
        ],
        in_specs=[VMEM] * 3,
        out_specs=[VMEM] * (len(MATRICES) + 3),
        scratch_shapes=[
            pltpu.VMEM((grid.count, 16 * groups, 128), bf),
            pltpu.VMEM((total, 128), f32),
            pltpu.SemaphoreType.DMA,
            pltpu.SemaphoreType.DMA((count_sends(grid, groups),)),
            pltpu.SemaphoreType.DMA((len(orders_of(groups)), grid.count)),
            pltpu.SemaphoreType.DMA((2, 2)),
            pltpu.SemaphoreType.DMA((2, 2)),
        ],
        compiler_params=pltpu.CompilerParams(collective_id=0, has_side_effects=True, vmem_limit_bytes=48 << 20),
    )(slot, x, seg)


def forward_kernel(x_ref, seg_ref, query_w, key_w, value_w, table_ref, vec_ref, q_ref, k_ref, v_ref, krt_ref, qrt_ref, pos_ref, ctx_ref, p_ref, x_scr, bias_scr):
    project_body(x_ref, query_w, key_w, value_w, table_ref, vec_ref, q_ref, k_ref, v_ref, krt_ref, qrt_ref, pos_ref)
    att_fwd_body(q_ref.shape[1] // 128, q_ref, k_ref, v_ref, krt_ref, qrt_ref, seg_ref, ctx_ref, p_ref, x_scr, bias_scr)


def forward(x_ext, seg_ext, query_w, key_w, value_w, table, vec):
    E = x_ext.shape[0]
    T = E - 2 * SPAN
    blocks = T // 128
    shape = jax.ShapeDtypeStruct
    return pl.pallas_call(
        forward_kernel,
        out_shape=[
            shape((PAIRS, T, 128), bf), shape((PAIRS, E, 128), bf), shape((PAIRS, E, 128), bf), shape((PAIRS, 640, 128), bf),
            shape((PAIRS, 640, 128), bf), shape((512, D), bf), shape((PAIRS, T, 128), bf), shape((PAIRS, blocks, 2, 128, 640), bf),
        ],
        in_specs=[VMEM] * 7,
        out_specs=[VMEM] * 8,
        scratch_shapes=[pltpu.VMEM((2, blocks + 5, 128, 640), bf), pltpu.VMEM((blocks, 128, 640), f32)],
        compiler_params=pltpu.CompilerParams(vmem_limit_bytes=56 << 20),
    )(x_ext, seg_ext, query_w, key_w, value_w, table, vec)


def feed_kernel(x_ref, ctx_ref, og_ref, output_w, up_w, down_w, vec_ref, out_ref, dz1_ref, dctx_ref, dflat_ref, dvec_ref, ml, dup, act, ddown, dattn, slope, wide):
    feed_body(x_ref, ctx_ref, og_ref, output_w, up_w, down_w, vec_ref, out_ref, dz1_ref, dctx_ref, wide, dvec_ref, ml, dup, act, ddown, dattn, slope)
    dflat_ref[...] = wide[...].astype(bf)


def feed(x_ext, ctx, out_grad, output_w, up_w, down_w, vec):
    T = out_grad.shape[0]
    shape = jax.ShapeDtypeStruct
    return pl.pallas_call(
        feed_kernel,
        out_shape=[shape((T, D), bf), shape((T, D), f32), shape((PAIRS, T, 128), bf), shape((FEED_ROWS, 128), bf), shape(vec.shape, f32)],
        in_specs=[VMEM] * 7,
        out_specs=[VMEM] * 5,
        scratch_shapes=[
            pltpu.VMEM((T, D), bf), pltpu.VMEM((T, FF), bf), pltpu.VMEM((T, FF), bf), pltpu.VMEM((T, D), bf), pltpu.VMEM((T, D), bf),
            pltpu.VMEM((256, FF), f32), pltpu.VMEM((FEED_ROWS, 128), f32),
        ],
        compiler_params=pltpu.CompilerParams(vmem_limit_bytes=56 << 20),
    )(x_ext, ctx, out_grad, output_w, up_w, down_w, vec)


def tail_kernel(grid, shard, dq_ref, dk_ref, dv_ref, dkr_ref, dqr_ref, dz1_ref, x_ref, pos_ref, table_ref, vec_ref, query_w, key_w, value_w, dflat_ref, dvec_in,
                dx_ref, sum_ref, dvec_ref, dwq, dwk, dwv, dtable, wide, flat, kids, outgoing, total, halo_out, halo_in, send_sem, recv_sem, halo_send, halo_recv):
    p = grid.here()
    tokens = dx_ref.shape[0]
    _, groups = shard_groups(shard, grid.count)
    before, after = seq_edges(grid)
    enter_all(grid, p)
    rims = (pl.ds(0, SPAN), pl.ds(tokens + SPAN, SPAN))
    for side in (0, 1):
        for which, ref in ((0, dk_ref), (1, dv_ref)):
            halo_out[side, which] = ref[:, rims[side], :].astype(bf)

    def halo_copy(side):
        return remote(halo_out.at[side], halo_in.at[1 - side], halo_send.at[side], halo_recv.at[1 - side], beside(grid, -1 if side == 0 else 1))

    pl.when(before)(lambda: halo_copy(0).start())
    pl.when(after)(lambda: halo_copy(1).start())

    def clear(side):
        halo_in[side] = jnp.zeros(halo_in.shape[1:], bf)

    pl.when(jnp.logical_not(before))(lambda: clear(0))
    pl.when(jnp.logical_not(after))(lambda: clear(1))
    dvec_ref[...] = dvec_in[...]
    tail_local(dq_ref, x_ref, dz1_ref, query_w, dx_ref, dwq, dvec_ref)
    tail_table(dkr_ref, dqr_ref, pos_ref, table_ref, vec_ref, query_w, key_w, dwq, dwk, dtable, dvec_ref)
    pl.when(before)(lambda: halo_copy(0).wait_send())
    pl.when(after)(lambda: halo_copy(1).wait_send())
    pl.when(before)(lambda: halo_copy(1).wait_recv())
    pl.when(after)(lambda: halo_copy(0).wait_recv())
    tail_keys(dk_ref, dv_ref, halo_in, x_ref, key_w, value_w, dx_ref, dwk, dwv, dvec_ref)
    place = matrix_rows()
    rest = flat.shape[0] - FEED_FIRST - FEED_ROWS
    wide[FEED_FIRST:, :] = jnp.zeros((rest, 128), f32)
    moved = lambda row: row if row < FEED_FIRST else row - FEED_ROWS
    for name, ref in (("query_w", dwq), ("key_w", dwk), ("value_w", dwv), ("rel_table", dtable)):
        base, rows, pieces = place[name]
        for c in range(pieces):
            wide[pl.ds(moved(base) + c, rows, stride=pieces), :] = ref[:, 128 * c : 128 * c + 128]
    vec_at, _ = vector_rows()
    for name in VECTORS:
        base, _, pieces = place[name]
        wide[moved(base) : moved(base) + pieces, :] = dvec_ref[vec_at[name][0] : vec_at[name][0] + pieces, :]
    flat[0:FEED_FIRST, :] = wide[0:FEED_FIRST, :].astype(bf)
    flat[FEED_FIRST : FEED_FIRST + FEED_ROWS, :] = dflat_ref[...]
    flat[FEED_FIRST + FEED_ROWS :, :] = wide[FEED_FIRST:, :].astype(bf)
    Scatter(grid, p, flat, lambda k: (k * shard // GROUP) * 16, kids, outgoing, total, send_sem, recv_sem, groups).run(sum_ref)


def tail(grid, shard, *args):
    _, groups = shard_groups(shard, grid.count)
    rows = flat_rows(shard, grid.count)
    tokens = args[5].shape[0]
    names, half = len(direction_names(grid)), grid.count // 2
    shape = jax.ShapeDtypeStruct
    dx, summed, _ = pl.pallas_call(
        functools.partial(tail_kernel, grid, shard),
        out_shape=[shape((tokens, D), f32), shape((16 * groups, 128), f32), shape((vector_rows()[1], 128), f32)],
        in_specs=[VMEM] * 15,
        out_specs=[VMEM] * 3,
        scratch_shapes=[
            pltpu.VMEM((D, D), f32), pltpu.VMEM((D, D), f32), pltpu.VMEM((D, D), f32), pltpu.VMEM((2 * SPAN, D), f32),
            pltpu.VMEM((rows - FEED_ROWS, 128), f32),
            pltpu.VMEM((rows, 128), bf),
            pltpu.VMEM((names, half, 16 * groups, 128), bf),
            pltpu.VMEM((half, 16 * groups, 128), bf),
            pltpu.VMEM((16 * groups, 128), f32),
            pltpu.VMEM((2, 2, PAIRS, SPAN, 128), bf),
            pltpu.VMEM((2, 2, PAIRS, SPAN, 128), bf),
            pltpu.SemaphoreType.DMA((scatter_sends(grid, groups),)),
            pltpu.SemaphoreType.DMA((len(orders_of(groups)), names, half)),
            pltpu.SemaphoreType.DMA((2,)),
            pltpu.SemaphoreType.DMA((2,)),
        ],
        compiler_params=pltpu.CompilerParams(collective_id=1, has_side_effects=True, vmem_limit_bytes=60 << 20),
    )(*args)
    return dx, summed


def on_device(layer_input, segment_ids, out_grad, weights, momentum, average):
    tokens_here = layer_input.shape[1]
    grid = Grid(lax.axis_size("seq"), lax.axis_size("row"))
    shard = weights.shape[0]
    _, groups = shard_groups(shard, grid.count)
    shift = (lax.axis_index("seq") * grid.row + lax.axis_index("row")) * shard % GROUP
    slot = lax.dynamic_update_slice(jnp.zeros((GROUP * groups,), bf), weights.astype(bf), (shift,)).reshape(16 * groups, 128)
    seg = jnp.broadcast_to(segment_ids + 1, (8, tokens_here))
    *matrices, vec, x_ext, seg_ext = gather_params(grid, shard, slot, layer_input[0], seg)
    query_w, key_w, value_w, output_w, up_w, down_w, table = matrices
    q, k, v, krt, qrt, pos, ctx, probs = forward(x_ext, seg_ext, query_w, key_w, value_w, table, vec)
    block_output, dz1, dctx, dflat, dvec = feed(x_ext, ctx, out_grad[0], output_w, up_w, down_w, vec)
    dq, dk, dv, dkr, dqr = att_bwd(q, k, v, krt, qrt, dctx, probs)
    dx, summed = tail(grid, shard, dq, dk, dv, dkr, dqr, dz1, x_ext, pos, table, vec, query_w, key_w, value_w, dflat, dvec)
    weight_grad = lax.dynamic_slice(summed.reshape(-1), (shift,), (shard,))
    all_tokens = tokens_here * grid.seq * layer_input.shape[0] * grid.row
    rate = 0.1 / math.sqrt(all_tokens)
    new_momentum = 0.5 * momentum + weight_grad
    new_weights = weights - rate * (weight_grad + 0.5 * new_momentum)
    new_average = 0.5 * average + 0.5 * new_weights
    return (
        block_output[None],
        dx[None],
        weight_grad,
        new_momentum,
        new_average,
        new_weights,
        new_weights.astype(jnp.bfloat16),
    )


def solution(mesh):
    flat = P(("seq", "row"))
    tokens = P("row", "seq", None)
    return jax.shard_map(
        on_device,
        mesh=mesh,
        in_specs=(tokens, P("row", "seq"), tokens, flat, flat, flat),
        out_specs=(tokens, tokens, flat, flat, flat, flat, flat),
        check_vma=False,
    )
```

```python
import functools
import itertools
import math

import jax
import jax.numpy as jnp
from jax import lax
from jax.experimental import pallas as pl
from jax.experimental.pallas import tpu as pltpu
from jax.sharding import PartitionSpec as P

D = 384
HEADS = 6
HEAD_DIM = 64
FF = 1536
SPAN = 256
PAIRS = HEADS // 2
NB = 5
EPSILON = 1e-07
bf = jnp.bfloat16
f32 = jnp.float32


MESH = pl.DeviceIdType.MESH
GROUP = 2048


class Grid:
    def __init__(self, seq, row):
        half = seq // 2
        wide = 1
        while wide * wide * 4 <= half:
            wide *= 2
        self.size = {"z": half // wide, "y": wide, "x": row}
        self.seq, self.row, self.count = seq, row, seq * row

    def here(self):
        s, x = lax.axis_index("seq"), lax.axis_index("row")
        y_size = self.size["y"]
        return {"z": s // (2 * y_size), "y": (s // 2) % y_size, "c": s % 2, "x": x}

    def seq_of(self, p):
        return (p["z"] * self.size["y"] + p["y"]) * 2 + p["c"]

    def flat(self, p):
        return self.seq_of(p) * self.row + p["x"]

    def device(self, p):
        return {"seq": self.seq_of(p), "row": p["x"]}

    def plane(self, p):
        return (p["z"] * self.size["y"] + p["y"]) * self.row + p["x"]

    def offsets(self, order):
        choices = []
        for axis in order:
            n = self.size[axis]
            if n == 2:
                choices.append([0, "f"])
            else:
                choices.append([0] + [sign * d for d in range(1, n) for sign in (-1, 1)])
        hops = lambda off: sum(1 if o == "f" else abs(o) for o in off)
        return sorted(itertools.product(*choices), key=hops)


def both(conds):
    out = None
    for cond in conds:
        if cond is not None:
            out = cond if out is None else jnp.logical_and(out, cond)
    return out


def guarded(cond, fn):
    if cond is None:
        fn()
    else:
        pl.when(cond)(fn)


def source_of(grid, p, order, off):
    o, conds = dict(p), []
    for axis, d in zip(order, off):
        if d == "f":
            o[axis] = 1 - p[axis]
        elif d != 0:
            o[axis] = p[axis] + d
            conds.append(p[axis] + d >= 0 if d < 0 else p[axis] + d < grid.size[axis])
    return o, both(conds)


def parent_of(grid, p, order, off):
    last = max((i for i, d in enumerate(off) if d != 0), default=None)
    if last is None:
        return None, None
    q, axis, d = dict(p), order[last], off[last]
    if d == "f":
        q[axis] = 1 - p[axis]
        return q, axis + "0"
    q[axis] = p[axis] + (1 if d > 0 else -1)
    return q, axis + ("+" if d > 0 else "-")


def children_of(grid, p, order, off):
    last = max((i for i, d in enumerate(off) if d != 0), default=None)
    found = []
    if last is not None and off[last] != "f":
        axis, away = order[last], (-1 if off[last] > 0 else 1)
        q = dict(p)
        q[axis] = p[axis] + away
        found.append((axis + ("+" if away > 0 else "-"), q, p[axis] > 0 if away < 0 else p[axis] < grid.size[axis] - 1))
    for axis in order[0 if last is None else last + 1 :]:
        if grid.size[axis] == 2:
            q = dict(p)
            q[axis] = 1 - p[axis]
            found.append((axis + "0", q, None))
        elif grid.size[axis] > 2:
            for sign in (1, -1):
                q = dict(p)
                q[axis] = p[axis] + sign
                found.append((axis + ("+" if sign > 0 else "-"), q, p[axis] > 0 if sign < 0 else p[axis] < grid.size[axis] - 1))
    return found


def neighbours_of(grid, p):
    found = []
    for axis in ("z", "y", "x"):
        found += children_of(grid, p, (axis,), (0,))
    sibling = dict(p)
    sibling["c"] = 1 - p["c"]
    found.append(("c0", sibling, None))
    return found


def enter(grid, p, extra=()):
    sem = pltpu.get_barrier_semaphore()
    total = jnp.int32(0)
    for name, q, cond in neighbours_of(grid, p) + list(extra):
        guarded(cond, lambda q=q: pl.semaphore_signal(sem, inc=1, device_id=grid.device(q), device_id_type=MESH))
        total = total + (1 if cond is None else cond.astype(jnp.int32))
    pl.semaphore_wait(sem, total)


def orders_of(groups):
    return (("z", "y", "x"), ("x", "z", "y")) if groups >= 8 else (("z", "y", "x"),)


def spans(groups):
    if groups < 8:
        return ((0, 16 * groups),)
    first = (groups * 20 + 16) // 32
    return ((0, 16 * first), (16 * first, 16 * (groups - first)))


class Gather:
    def __init__(self, grid, p, slots, send_sem, recv_sem, groups):
        self.grid, self.p, self.slots = grid, p, slots
        self.send_sem, self.recv_sem, self.groups = send_sem, recv_sem, groups
        self.sends, self.used = [], 0

    def copy(self, part, k, q, index):
        start, rows = spans(self.groups)[part]
        block = self.slots.at[k, pl.ds(start, rows), :]
        return pltpu.make_async_remote_copy(
            src_ref=block, dst_ref=block, send_sem=self.send_sem.at[index], recv_sem=self.recv_sem.at[part, k],
            device_id=self.grid.device(q), device_id_type=MESH)

    def arrived(self, part, k):
        start, rows = spans(self.groups)[part]
        block = self.slots.at[k, pl.ds(start, rows), :]
        pltpu.make_async_remote_copy(
            src_ref=block, dst_ref=block, send_sem=self.send_sem.at[0], recv_sem=self.recv_sem.at[part, k],
            device_id=self.grid.device(self.p), device_id_type=MESH).wait_recv()

    def run(self):
        grid, p = self.grid, self.p
        steps = []
        for part, order in enumerate(orders_of(self.groups)):
            for off in grid.offsets(order):
                steps.append((sum(1 if o == "f" else abs(o) for o in off), part, order, off))
        steps.sort(key=lambda item: item[:2])
        sibling = dict(p)
        sibling["c"] = 1 - p["c"]
        finish = []
        for hops, part, order, off in steps:
            o, cond = source_of(grid, p, order, off)
            k = grid.flat(o)
            targets = children_of(grid, p, order, off) + [("c0", sibling, None)]
            indices = [self.used + i for i in range(len(targets))]
            self.used += len(targets)

            def step(part=part, k=k, targets=targets, indices=indices, own=hops == 0):
                if not own:
                    self.arrived(part, k)
                for (name, q, when), index in zip(targets, indices):
                    guarded(when, lambda q=q, index=index: self.copy(part, k, q, index).start())

            guarded(cond, step)

            def end(part=part, k=k, targets=targets, indices=indices):
                for (name, q, when), index in zip(targets, indices):
                    guarded(when, lambda q=q, index=index: self.copy(part, k, q, index).wait_send())

            finish.append((cond, end))
        for part, order in enumerate(orders_of(self.groups)):
            for off in grid.offsets(order):
                o, cond = source_of(grid, sibling, order, off)
                guarded(cond, lambda part=part, k=grid.flat(o): self.arrived(part, k))
        for cond, end in finish:
            guarded(cond, end)

def count_sends(grid, groups):
    fake = {"z": jnp.int32(0), "y": jnp.int32(0), "x": jnp.int32(0), "c": jnp.int32(0)}
    return sum(len(children_of(grid, fake, order, off)) + 1 for order in orders_of(groups) for off in grid.offsets(order))


OPPOSITE = {"+": "-", "-": "+", "0": "0"}


def direction_names(grid):
    names = ["c0"]
    for axis in ("z", "y", "x"):
        if grid.size[axis] == 2:
            names.append(axis + "0")
        elif grid.size[axis] > 2:
            names += [axis + "+", axis + "-"]
    return names


class Scatter:
    def __init__(self, grid, p, flat, first_row, kids, outgoing, total, send_sem, recv_sem, groups):
        self.grid, self.p, self.flat, self.first_row = grid, p, flat, first_row
        self.kids, self.outgoing, self.total = kids, outgoing, total
        self.send_sem, self.recv_sem, self.groups = send_sem, recv_sem, groups
        self.names = direction_names(grid)

    def incoming(self, part, name, place):
        start, rows = spans(self.groups)[part]
        return self.kids.at[self.names.index(name), place, pl.ds(start, rows), :]

    def transfer(self, source, part, name, place, q, send):
        return pltpu.make_async_remote_copy(
            src_ref=source, dst_ref=self.incoming(part, name, place), send_sem=self.send_sem.at[send],
            recv_sem=self.recv_sem.at[part, self.names.index(name), place], device_id=self.grid.device(q), device_id_type=MESH)

    def arrived(self, part, name, place):
        block = self.incoming(part, name, place)
        pltpu.make_async_remote_copy(
            src_ref=block, dst_ref=block, send_sem=self.send_sem.at[0],
            recv_sem=self.recv_sem.at[part, self.names.index(name), place],
            device_id=self.grid.device(self.p), device_id_type=MESH).wait_recv()

    def run(self, result):
        grid, p = self.grid, self.p
        sibling = dict(p)
        sibling["c"] = 1 - p["c"]
        steps = []
        for part, order in enumerate(orders_of(self.groups)):
            for off in grid.offsets(order):
                steps.append((-sum(1 if o == "f" else abs(o) for o in off), part, order, off))
        steps.sort(key=lambda item: item[:2])
        used, finish = 0, []
        for hops, part, order, off in steps:
            o, cond = source_of(grid, sibling, order, off)
            start, rows = spans(self.groups)[part]

            def give(part=part, o=o, index=used, start=start, rows=rows):
                block = self.flat.at[pl.ds(pl.multiple_of(self.first_row(grid.flat(o)) + start, 16), rows), :]
                return self.transfer(block, part, "c0", grid.plane(o), sibling, index)

            guarded(cond, lambda give=give: give().start())
            finish.append((cond, lambda give=give: give().wait_send()))
            used += 1
        for hops, part, order, off in steps:
            o, cond = source_of(grid, p, order, off)
            place, k = grid.plane(o), grid.flat(o)
            start, rows = spans(self.groups)[part]
            kids = children_of(grid, p, order, off)
            parent, side = parent_of(grid, p, order, off)

            def push(part=part, place=place, parent=parent, side=side, index=used, start=start, rows=rows):
                block = self.outgoing.at[place, pl.ds(start, rows), :]
                return self.transfer(block, part, side[0] + OPPOSITE[side[1]], place, parent, index)

            def step(part=part, place=place, k=k, kids=kids, parent=parent, start=start, rows=rows, push=push):
                self.arrived(part, "c0", place)
                mine = self.flat[pl.ds(pl.multiple_of(self.first_row(k) + start, 16), rows), :].astype(f32)
                self.total[0:rows, :] = mine + self.incoming(part, "c0", place)[...].astype(f32)
                for name, q, when in kids:

                    def add(name=name):
                        self.arrived(part, name, place)
                        self.total[0:rows, :] += self.incoming(part, name, place)[...].astype(f32)

                    guarded(when, add)
                if parent is None:
                    result[pl.ds(start, rows), :] = self.total[0:rows, :]
                else:
                    self.outgoing[place, pl.ds(start, rows), :] = self.total[0:rows, :].astype(bf)
                    push().start()

            guarded(cond, step)
            if parent is not None:
                finish.append((cond, lambda push=push: push().wait_send()))
                used += 1
        for cond, end in finish:
            guarded(cond, end)


def scatter_sends(grid, groups):
    return 2 * sum(len(grid.offsets(order)) for order in orders_of(groups))


def shard_groups(shard, count):
    first = [shard * k // GROUP for k in range(count)]
    groups = max(-(-shard * (k + 1) // GROUP) - first[k] for k in range(count))
    return first, max(groups, 2)


def flat_rows(shard, count):
    first, groups = shard_groups(shard, count)
    return 16 * (first[-1] + groups)


def layer_pieces():
    square, vector_of = (D, D), (D,)
    return (
        ("query_w", square), ("key_w", square), ("value_w", square), ("output_w", square), ("up_w", (D, FF)), ("down_w", (FF, D)),
        ("query_b", vector_of), ("key_b", vector_of), ("value_b", vector_of), ("output_b", vector_of), ("attn_gain", vector_of),
        ("attn_shift", vector_of), ("up_bias", (FF,)), ("down_bias", vector_of), ("ffn_gain", vector_of), ("ffn_shift", vector_of),
        ("rel_table", (2 * SPAN, D)), ("rel_gain", vector_of), ("rel_shift", vector_of),
    )


def matrix_rows():
    place, at = {}, 0
    for name, extent in layer_pieces():
        if len(extent) == 2:
            place[name] = (at // 128, extent[0], extent[1] // 128)
        else:
            place[name] = (at // 128, 1, extent[0] // 128)
        at += math.prod(extent)
    return place


MATRICES = ("query_w", "key_w", "value_w", "output_w", "up_w", "down_w", "rel_table")
VECTORS = tuple(name for name, extent in layer_pieces() if len(extent) == 1)
FEED_FIRST = matrix_rows()["output_w"][0]
FEED_ROWS = matrix_rows()["query_b"][0] - FEED_FIRST
USED_ROWS = sum(rows * pieces for _, rows, pieces in matrix_rows().values())


def vector_rows():
    place, at = {}, 0
    for name in VECTORS:
        wide = matrix_rows()[name][2]
        place[name] = (at, wide)
        at += wide
    return place, -(-at // 8) * 8


SC = 1.0 / math.sqrt(3.0 * HEAD_DIM)
LOG2E = 1.4426950408889634
NT = (((1,), (1,)), ((), ()))
NN = (((1,), (0,)), ((), ()))
TN = (((0,), (0,)), ((), ()))


def dot(a, b, dims=NN):
    return lax.dot_general(a, b, dims, preferred_element_type=f32)


def iotas(rows, lanes):
    return lax.broadcasted_iota(jnp.int32, (rows, lanes), 0), lax.broadcasted_iota(jnp.int32, (rows, lanes), 1)


def tile(i):
    return pl.ds(pl.multiple_of(i * 128, 128), 128)


def window(i):
    return pl.ds(pl.multiple_of(i * 128, 128), NB * 128)


def wide_diagonal(columns):
    zero = jnp.zeros((64, 128), columns.dtype)
    return jnp.concatenate([jnp.concatenate([columns[:64], zero], axis=1), jnp.concatenate([zero, columns[64:]], axis=1)], axis=0)


def tall_diagonal(rows):
    lane = iotas(128, 128)[1]
    zero = jnp.zeros_like(rows)
    return jnp.concatenate([jnp.where(lane < 64, rows, zero), jnp.where(lane >= 64, rows, zero)], axis=0)


def own_heads(wide):
    return jnp.concatenate([wide[:64, :128], wide[64:, 128:]], axis=0)


def turn_rows(values, back):
    size = values.shape[0]
    lane = iotas(*values.shape)[1]
    for step in (64, 32, 16, 8, 4, 2, 1):
        moved = pltpu.roll(values, size - step if back else step, 0)
        values = jnp.where(lane & step != 0, moved, values)
    return values


def turn_lanes(values, first):
    return jnp.concatenate([pltpu.roll(values[8 * g : 8 * g + 8, :512], first + 8 * g, 1, stride=1, stride_axis=0) for g in range(16)], axis=0)


def stream_rows(load, up, fine):
    row, lane = iotas(8, 128)
    inner = [(step, lane & step != 0, row < step if not up else row >= 8 - step) for step in fine]
    masks = [lane & step != 0 for step in (8, 16, 32, 64)]
    turned = [None for _ in inner]
    past = [[] for _ in masks]
    extra = 15 + len(inner)
    order = list(range(64 - extra, 64)) + list(range(64)) if not up else list(reversed(list(range(64)) + list(range(extra))))
    for n, i in enumerate(order):
        value = load(i)
        for level, (step, mask, edge) in enumerate(inner):
            now = pltpu.roll(value, step if not up else 8 - step, 0)
            if turned[level] is not None:
                value = jnp.where(mask, jnp.where(edge, turned[level], now), value)
            turned[level] = now
        for level, mask in enumerate(masks):
            past[level].append(value)
            if len(past[level]) > 1 << level:
                value = jnp.where(mask, past[level].pop(0), value)
        if n >= extra:
            yield i, value


def att_fwd_body(nblk, qT_ref, k_ref, vT_ref, krt_ref, qrtT_ref, seg_ref, ctx_ref, p_ref, inv_ref, x_scr, bias_scr, s0, s1, z0, z1, t0, t1, m0, m1):
    row, lane = iotas(128, 128)
    lane2 = iotas(128, 256)[1]
    lane512 = iotas(512, 256)[1]
    items, keys = PAIRS * nblk, nblk + 4

    def mk_bias(t, carry):
        sq = seg_ref[0:1, tile(t + 2)].astype(f32)
        for b in range(NB):
            sk = jnp.broadcast_to(seg_ref[0:1, tile(t + b)], (128, 128)).astype(f32).T
            ok = sk == sq
            if b == 0:
                ok = ok & (row >= lane)
            if b == NB - 1:
                ok = ok & (row <= lane)
            bias_scr[t, 128 * b : 128 * b + 128, :] = jnp.where(ok, 0.0, -1e30).astype(f32)
        return carry

    lax.fori_loop(0, nblk, mk_bias, 0)

    def keyside(p, J, slot):
        C = dot(tall_diagonal(k_ref[p, tile(J), :]), qrtT_ref[p])
        for h in range(2):
            Ch = C[128 * h : 128 * h + 128]
            R = turn_lanes(Ch, 0)
            x_scr[slot, h, :, 0:128] = jnp.where(lane > row, R[:, :128], Ch[:, 512:]).astype(bf)
            x_scr[slot, h, :, 128:512] = R[:, 128:].astype(bf)
            x_scr[slot, h, :, 512:640] = R[:, :128].astype(bf)

    def start(J, carry):
        keyside(0, J, J)
        return carry

    lax.fori_loop(0, keys, start, 0)

    def scores(n, s_scr, z_scr, t_scr, m_scr):
        n = jnp.minimum(n, items - 1)
        p, t = n // nblk, n % nblk
        base = (p % 2) * keys + t
        Q2 = wide_diagonal(qT_ref[p, :, tile(t)])
        odd = lane2 % 2 == 1
        zero = jnp.zeros_like(Q2)
        table = krt_ref[p]
        moved = krt_ref[PAIRS + p]
        Z = dot(jnp.concatenate([table, moved], axis=1), jnp.concatenate([jnp.where(odd, zero, Q2), jnp.where(odd, Q2, zero)], axis=0))
        ends = jnp.where(odd[:1], Z[2:3], Z[1:2])
        z_scr[...] = Z
        s_scr[...] = dot(k_ref[p, window(t), :], Q2)
        for h in range(2):
            cols = slice(128 * h, 128 * h + 128)

            def load(i):
                return z_scr[8 * i : 8 * i + 8, cols]

            end = ends[:, cols]
            top = None
            held = None
            for i, y in stream_rows(load, False, (2, 4)):
                if i % 2 == 0:
                    held = y
                    continue
                at, b = 8 * (i - 1), i // 16
                y = jnp.concatenate([held, y], axis=0)
                for block in (0, 4) if b == 0 else (b,):
                    r = at + 128 * (block - b)
                    rows = slice(r, r + 16)
                    inner = slice(at % 128, at % 128 + 16)
                    x = x_scr[base + block, h, inner, 128 * (4 - block) : 128 * (5 - block)].astype(f32)
                    part = y
                    if block == 0:
                        part = jnp.where(iotas(16, 128)[0] + at > iotas(16, 128)[1], y, end)
                    T = s_scr[rows, cols] + bias_scr[t, rows, :] + part + x
                    t_scr[rows, cols] = T
                    most = jnp.maximum(T[:8], T[8:])
                    top = most if top is None else jnp.maximum(top, most)
            m_scr[:, cols] = top

    def soft(n, t_scr, m_scr):
        n = jnp.clip(n, 0, items - 1)
        m = jnp.max(m_scr[...], axis=0, keepdims=True)
        total = None
        for i in range(40):
            e = jnp.exp2((t_scr[16 * i : 16 * i + 16, :] - m) * (SC * LOG2E))
            part = e[:8] + e[8:]
            total = part if total is None else total + part
            p_ref[n // nblk, n % nblk, 16 * i : 16 * i + 16, :] = e.astype(bf)
        inv_ref[n // nblk, n % nblk] = jnp.broadcast_to(1.0 / jnp.sum(total, axis=0, keepdims=True), (8, 256))

    def context(n):
        n = jnp.clip(n, 0, items - 1)
        p, t = n // nblk, n % nblk
        ctxT = own_heads(dot(vT_ref[p, :, window(t)], p_ref[p, t]) * inv_ref[p, t, 0:1, :])
        ctx_ref[p, tile(t), :] = ctxT.astype(bf).T

    half = nblk // 2
    per = keys // half

    def body(m, slot):
        context(2 * m - 2)
        soft(2 * m - 1, t1, m1)
        scores(2 * m, s0, z0, t0, m0)
        context(2 * m - 1)
        soft(2 * m, t0, m0)
        scores(2 * m + 1, s1, z1, t1, m1)
        p, first = jnp.minimum(m // half + 1, PAIRS - 1), per * (m % half)
        for i in range(per):
            keyside(p, first + i, slot + i)
        return jnp.where(slot + per == 2 * keys, 0, slot + per)

    lax.fori_loop(0, items // 2 + 1, body, jnp.int32(keys))


def unreversed(values, JR):
    high = values.astype(bf)
    low = (values - high.astype(f32)).astype(bf)
    both = dot(JR, jnp.concatenate([high, low], axis=1))
    return both[:, :128] + both[:, 128:]


def att_bwd_body(nblk, q_ref, kT_ref, kTr_ref, v_ref, krtT_ref, qrt_ref, qend_ref, dctxT_ref, p_ref, inv_ref, dq_ref, dkc_ref, dkp_ref, dv_ref, dkr_ref, dqr_ref,
                 gt_scr, dp_scr, gm_scr, gb0, gb1, gu0, gu1):
    row, lane = iotas(128, 128)
    row16, lane16 = iotas(16, 256)
    JR = (row + lane == 127).astype(bf)
    zero = jnp.zeros((128, 128), bf)
    items, keys, half = PAIRS * nblk, nblk + 4, nblk // 2
    per = keys // half
    gt_scr[...] = jnp.zeros(gt_scr.shape, bf)
    gb1[...] = jnp.zeros(gb1.shape, bf)
    gu1[...] = jnp.zeros(gu1.shape, bf)
    for ref in (dkc_ref, dv_ref, dkr_ref, dqr_ref):
        ref[...] = jnp.zeros(ref.shape, f32)

    def kblocks(p, first, base):
        turned = [[], []]
        for i in range(per):
            for h in range(2):
                GT = gt_scr[base + first + i, h]
                Gm = jnp.concatenate([jnp.where(lane > row, GT[:, :128], GT[:, 512:]), GT[:, 128:512]], axis=1)
                turned[h].append(turn_lanes(dot(JR, Gm), 385).astype(bf))
        stacked = [jnp.concatenate(part, axis=0) for part in turned]
        dk = dot(jnp.concatenate(stacked, axis=1), qrt_ref[p])
        for i in range(per):
            dkp_ref[p, tile(first + i), :] = unreversed(dk[128 * i : 128 * i + 128], JR)
        span = pl.ds(pl.multiple_of(first * 128, 128), 128 * per)
        for h in range(2):
            heads = slice(64 * h, 64 * h + 64)
            dqr_ref[p, heads, 0:512] += dot(kTr_ref[p, heads, span], stacked[h])

    def upstream(n, slot, gb, gu):
        p, t = n // nblk, n % nblk
        D2 = wide_diagonal(dctxT_ref[p, :, tile(t)])
        inv = inv_ref[p, t, 0:1, :]
        dp_scr[...] = dot(v_ref[p, window(t), :], D2)
        total = None
        for i in range(40):
            rows = slice(16 * i, 16 * i + 16)
            w = p_ref[p, t, rows, :].astype(f32) * dp_scr[rows, :]
            part = w[:8] + w[8:]
            total = part if total is None else total + part
        less = jnp.sum(total, axis=0, keepdims=True) * inv * inv

        def grad(i):
            rows = slice(16 * i, 16 * i + 16)
            G = p_ref[p, t, rows, :].astype(f32) * (dp_scr[rows, :] * inv - less)
            Gb = G.astype(bf)
            gb[rows, :] = Gb
            b = i // 8
            for h in range(2):
                gt_scr[slot + b, h, 16 * (i % 8) : 16 * (i % 8) + 16, 128 * (4 - b) : 128 * (5 - b)] = Gb[:, 128 * h : 128 * h + 128]
            return G

        ends = None
        final = None
        for i in range(32):
            G = grad(i)
            if i < 8:
                at = row16 + 16 * i - lane16 % 128
                part = jnp.where(at == 0, G, 0.0)
                part = part[:8] + part[8:]
                ends = part if ends is None else ends + part
                other = grad(32 + i)
                part = jnp.where(at == 0, other, 0.0)
                part = part[:8] + part[8:]
                final = part if final is None else final + part
                G = jnp.where(at > 0, G, other)
            gm_scr[16 * i : 16 * i + 16, :] = G
        ends = jnp.sum(ends, axis=0, keepdims=True)
        final = jnp.sum(final, axis=0, keepdims=True)
        final = jnp.concatenate([jnp.broadcast_to(final[:, :128], (64, 128)), jnp.broadcast_to(final[:, 128:], (64, 128))], axis=0)
        dqr_ref[p, :, 512:640] += kT_ref[p, :, tile(t + 4)].astype(f32) * final
        dkc_ref[p, tile(t + 4), :] += (qend_ref[p].astype(f32) * final).T
        dv_ref[p, window(t), :] += dot(p_ref[p, t], (D2.astype(f32) * inv).astype(bf).T)
        for h in range(2):
            cols = slice(128 * h, 128 * h + 128)
            held = None
            for i, y in stream_rows(lambda i: gm_scr[8 * i : 8 * i + 8, cols], True, (1, 2, 4)):
                if i == 0:
                    y = y + jnp.where(row[:8] == 1, ends[:, cols], 0.0)
                if i % 2 == 1:
                    held = y
                else:
                    gu[8 * i : 8 * i + 16, cols] = jnp.concatenate([y, held], axis=0).astype(bf)

    def downstream(n, gb, gu):
        n = jnp.maximum(n, 0)
        p, t = n // nblk, n % nblk
        dqT = own_heads(dot(kT_ref[p, :, window(t)], gb[...]) + dot(krtT_ref[p], gu[...]))
        dq_ref[p, tile(t), :] = (SC * dqT).astype(bf).T
        Qm = tall_diagonal(q_ref[p, tile(t), :])
        dkc_ref[p, window(t), :] += dot(gb[...], Qm)
        dkr_ref[p] += dot(gu[...], Qm)

    def body(m, slot, late):
        p = m // half
        if late:
            kblocks(p - 1, per * (m % half), (1 - p % 2) * keys)
        downstream(2 * m - 1, gb1, gu1)
        upstream(2 * m, slot, gb0, gu0)
        downstream(2 * m, gb0, gu0)
        upstream(2 * m + 1, slot + 1, gb1, gu1)
        following = slot + 2
        following = jnp.where(following == nblk, keys, following)
        return jnp.where(following == keys + nblk, 0, following)

    slot = lax.fori_loop(0, half, lambda m, slot: body(m, slot, False), jnp.int32(0))
    lax.fori_loop(half, items // 2, lambda m, slot: body(m, slot, True), slot)
    downstream(items - 1, gb1, gu1)

    def last(i, carry):
        kblocks(PAIRS - 1, per * i, ((PAIRS - 1) % 2) * keys)
        return carry

    lax.fori_loop(0, half, last, 0)


def vector(vec_ref, name):
    at, wide = vector_rows()[0][name]
    return jnp.concatenate([vec_ref[at + i : at + i + 1, :] for i in range(wide)], axis=1)


def put_vector(vec_ref, name, value):
    at, wide = vector_rows()[0][name]
    for i in range(wide):
        vec_ref[at + i : at + i + 1, :] = value[:, 128 * i : 128 * i + 128]


def add_vector(vec_ref, name, value):
    at, wide = vector_rows()[0][name]
    for i in range(wide):
        vec_ref[at + i : at + i + 1, :] += value[:, 128 * i : 128 * i + 128]


def normalized(values):
    centered = values - jnp.mean(values, axis=1, keepdims=True)
    inverse = lax.rsqrt(jnp.mean(centered * centered, axis=1, keepdims=True) + EPSILON)
    return centered * inverse, inverse


def norm_back(upstream, gain, unit, inverse):
    scaled = upstream * gain
    mean = jnp.mean(scaled, axis=1, keepdims=True)
    along = jnp.mean(scaled * unit, axis=1, keepdims=True)
    return inverse * (scaled - mean - unit * along)


def column_sum(values):
    return jnp.sum(values, axis=0, keepdims=True)


def reversal():
    row = lax.broadcasted_iota(jnp.int32, (128, 128), 0)
    lane = lax.broadcasted_iota(jnp.int32, (128, 128), 1)
    return (row + lane == 127).astype(bf)


def reversed_rows(values, JR):
    blocks = values.shape[0] // 128
    return jnp.concatenate([dot(JR, values[128 * b : 128 * b + 128]).astype(bf) for b in reversed(range(blocks))], axis=0)


def project_body(x_ref, query_w, key_w, value_w, table_ref, vec_ref, q_ref, qT_ref, k_ref, kT_ref, kTr_ref, v_ref, vT_ref, krt_ref, krtT_ref, qrt_ref, qrtT_ref, pos_ref):
    tokens = q_ref.shape[1]
    JR = reversal()
    lane = iotas(512, 128)[1]
    unit, _ = normalized(table_ref[...].astype(f32))
    pos = (unit * vector(vec_ref, "rel_gain") + vector(vec_ref, "rel_shift")).astype(bf)
    pos = pltpu.roll(reversed_rows(pos, JR).astype(f32), 1, 0).astype(bf)
    pos_ref[...] = pos
    keys = dot(pos, key_w[...]) + vector(vec_ref, "key_b")
    moved = pltpu.roll(keys, 1, 0).astype(bf)
    keys = keys.astype(bf)
    queries = (dot(pos, query_w[...]) + vector(vec_ref, "query_b")).astype(bf)
    for p in range(PAIRS):
        cols = slice(128 * p, 128 * p + 128)
        krt_ref[p] = keys[:, cols]
        krt_ref[PAIRS + p] = moved[:, cols]
        krtT_ref[p] = keys[:, cols].T
        qrtT_ref[p, :, 0:512] = queries[:, cols].T
        qrtT_ref[p, :, 512:640] = jnp.broadcast_to(queries[1:2, cols], (128, 128)).T
        zero = jnp.zeros((512, 128), bf)
        qrt_ref[p, 0:512, :] = jnp.where(lane < 64, queries[:, cols], zero)
        qrt_ref[p, 512:1024, :] = jnp.where(lane < 64, zero, queries[:, cols])
    bias = {name: vector(vec_ref, name) for name in ("query_b", "key_b", "value_b")}

    def chunk(i, carry):
        rows = pl.ds(pl.multiple_of(i * 256, 256), 256)
        x = x_ref[rows, :]
        y = (dot(x, key_w[...]) + bias["key_b"]).astype(bf)
        w = (dot(x, value_w[...]) + bias["value_b"]).astype(bf)
        for p in range(PAIRS):
            cols = slice(128 * p, 128 * p + 128)
            k_ref[p, rows, :] = y[:, cols]
            turned = y[:, cols].T
            kT_ref[p, :, rows] = turned
            kTr_ref[p, :, rows] = jnp.concatenate([dot(turned[:, :128], JR), dot(turned[:, 128:], JR)], axis=1).astype(bf)
            v_ref[p, rows, :] = w[:, cols]
            vT_ref[p, :, rows] = w[:, cols].T
        return carry

    lax.fori_loop(0, x_ref.shape[0] // 256, chunk, 0)

    def own(i, carry):
        rows = pl.ds(pl.multiple_of(i * 256, 256), 256)
        x = x_ref[pl.ds(pl.multiple_of(i * 256 + SPAN, 256), 256), :]
        y = (dot(x, query_w[...]) + bias["query_b"]).astype(bf)
        for p in range(PAIRS):
            q_ref[p, rows, :] = y[:, 128 * p : 128 * p + 128]
            qT_ref[p, :, rows] = y[:, 128 * p : 128 * p + 128].T
        return carry

    lax.fori_loop(0, tokens // 256, own, 0)


SQRT_HALF = 0.7071067811865476
PHI_SCALE = 0.3989422804014327


def gelu_and_slope(u):
    cdf = 0.5 + 0.5 * lax.erf(u * SQRT_HALF)
    return u * cdf, cdf + u * (PHI_SCALE * jnp.exp(-0.5 * u * u))


def feed_body(x_ref, ctx_ref, og_ref, output_w, up_w, down_w, vec_ref, out_ref, dz1_ref, dctx_ref, wide, dvec_ref,
              ml_scr, dup_scr, act_scr, ddown_scr, dattn_scr, slope_scr):
    tokens = out_ref.shape[0]
    dvec_ref[...] = jnp.zeros(dvec_ref.shape, f32)
    vecs = {name: vector(vec_ref, name) for name in ("output_b", "attn_gain", "attn_shift", "up_bias", "down_bias", "ffn_gain", "ffn_shift")}
    C = 256

    def chunk(i, carry):
        rows = pl.ds(pl.multiple_of(i * C, C), C)
        h = x_ref[pl.ds(pl.multiple_of(i * C + SPAN, C), C), :].astype(f32)
        z1 = h + dot(jnp.concatenate([ctx_ref[p, rows, :] for p in range(PAIRS)], axis=1), output_w[...]) + vecs["output_b"]
        unit1, inv1 = normalized(z1)
        mid = unit1 * vecs["attn_gain"] + vecs["attn_shift"]
        ml = mid.astype(bf)
        ml_scr[rows, :] = ml
        z2 = mid + vecs["down_bias"]
        for f in range(FF // 256):
            cols = slice(256 * f, 256 * f + 256)
            up = dot(ml, up_w[:, cols]) + vecs["up_bias"][:, cols]
            act, slope = gelu_and_slope(up)
            act_scr[rows, cols] = act.astype(bf)
            slope_scr[:, cols] = slope
        z2 = z2 + dot(act_scr[rows, :], down_w[...])
        unit2, inv2 = normalized(z2)
        out_ref[rows, :] = (unit2 * vecs["ffn_gain"] + vecs["ffn_shift"]).astype(bf)
        dh = og_ref[rows, :].astype(f32)
        add_vector(dvec_ref, "ffn_gain", column_sum(dh * unit2))
        add_vector(dvec_ref, "ffn_shift", column_sum(dh))
        dz2 = norm_back(dh, vecs["ffn_gain"], unit2, inv2)
        ddown = dz2.astype(bf)
        ddown_scr[rows, :] = ddown
        add_vector(dvec_ref, "down_bias", column_sum(ddown.astype(f32)))
        for f in range(FF // 256):
            cols = slice(256 * f, 256 * f + 256)
            dup = (dot(ddown, down_w[cols, :], NT) * slope_scr[:, cols]).astype(bf)
            dup_scr[rows, cols] = dup
        add_vector(dvec_ref, "up_bias", column_sum(dup_scr[rows, :].astype(f32)))
        dmid = dz2 + dot(dup_scr[rows, :], up_w[...], NT)
        add_vector(dvec_ref, "attn_gain", column_sum(dmid * unit1))
        add_vector(dvec_ref, "attn_shift", column_sum(dmid))
        dz1 = norm_back(dmid, vecs["attn_gain"], unit1, inv1)
        dz1_ref[rows, :] = dz1
        dattn = dz1.astype(bf)
        dattn_scr[rows, :] = dattn
        add_vector(dvec_ref, "output_b", column_sum(dattn.astype(f32)))
        dctx = dot(dattn, output_w[...], NT).astype(bf)
        for p in range(PAIRS):
            dctx_ref[p, :, rows] = dctx[:, 128 * p : 128 * p + 128].T
        return carry

    lax.fori_loop(0, tokens // C, chunk, 0)
    place = matrix_rows()

    def put(name, first, rows, value):
        base, _, pieces = place[name]
        for c in range(value.shape[1] // 128):
            wide[pl.ds(base - FEED_FIRST + pieces * first[0] + first[1] + c, rows, stride=pieces), :] = value[:, 128 * c : 128 * c + 128]

    ctx = jnp.concatenate([ctx_ref[p] for p in range(PAIRS)], axis=1)
    put("output_w", (0, 0), D, dot(ctx, dattn_scr[...], TN))
    for f in range(FF // 256):
        cols = slice(256 * f, 256 * f + 256)
        put("up_w", (0, 2 * f), D, dot(ml_scr[...], dup_scr[:, cols], TN))
        put("down_w", (256 * f, 0), 256, dot(act_scr[:, cols], ddown_scr[...], TN))


def split(values):
    high = values.astype(bf)
    return high, (values - high.astype(f32)).astype(bf)


def dot2(left, right, dims=NN):
    if left.dtype == f32:
        return sum(dot(part, right, dims) for part in split(left))
    return sum(dot(left, part, dims) for part in split(right))


def tail_local(dq_ref, x_ref, dz1_ref, query_w, dx_ref, dwq_ref, dvec_ref):
    tokens = dx_ref.shape[0]
    dq = jnp.concatenate([dq_ref[p] for p in range(PAIRS)], axis=1)
    dx_ref[...] = dz1_ref[...] + dot(dq, query_w[...], NT)
    dwq_ref[...] = dot(x_ref[SPAN : SPAN + tokens, :], dq, TN)
    put_vector(dvec_ref, "query_b", column_sum(dq.astype(f32)))


def tail_table(dkr_ref, dqr_ref, pos_ref, table_ref, vec_ref, query_w, key_w, dwq_ref, dwk_ref, dtable_ref, dvec_ref):
    JR = reversal()
    second = iotas(512, 128)[0] == 1
    tabs = {"key_b": jnp.concatenate([SC * dkr_ref[p] for p in range(PAIRS)], axis=1)}
    parts = []
    for p in range(PAIRS):
        part = dqr_ref[p].T
        parts.append(SC * (part[:512] + jnp.where(second, column_sum(part[512:]), 0.0)))
    tabs["query_b"] = jnp.concatenate(parts, axis=1)
    dpos = None
    for w, dw, name in ((key_w, dwk_ref, "key_b"), (query_w, dwq_ref, "query_b")):
        tab = tabs[name]
        if name == "key_b":
            dw[...] = dot2(pos_ref[...], tab, TN)
            put_vector(dvec_ref, name, column_sum(tab))
        else:
            dw[...] += dot2(pos_ref[...], tab, TN)
            add_vector(dvec_ref, name, column_sum(tab))
        part = dot2(tab, w[...], NT)
        dpos = part if dpos is None else dpos + part
    table = jnp.concatenate([dot(JR, table_ref[128 * b : 128 * b + 128, :]) for b in reversed(range(4))], axis=0)
    unit, inverse = normalized(pltpu.roll(table, 1, 0))
    put_vector(dvec_ref, "rel_gain", column_sum(dpos * unit))
    put_vector(dvec_ref, "rel_shift", column_sum(dpos))
    dpos = pltpu.roll(norm_back(dpos, vector(vec_ref, "rel_gain"), unit, inverse), 511, 0).astype(bf)
    for b in range(4):
        dtable_ref[128 * b : 128 * b + 128, :] = dot(JR, dpos[128 * (3 - b) : 128 * (4 - b)])


def tail_keys(dkc_ref, dkp_ref, dv_ref, halo_ref, x_ref, key_w, value_w, dx_ref, dwk_ref, dwv_ref, dvec_ref):
    tokens = dx_ref.shape[0]
    x = x_ref[SPAN : SPAN + tokens, :]
    for which, (ref, w, dw, name) in enumerate(((None, key_w, dwk_ref, "key_b"), (dv_ref, value_w, dwv_ref, "value_b"))):
        pieces = []
        for p in range(PAIRS):
            middle = slice(SPAN, SPAN + tokens)
            own = SC * (dkc_ref[p, middle, :] + dkp_ref[p, middle, :]) if ref is None else ref[p, middle, :]
            edge = [halo_ref[side, which, p].astype(f32) for side in (0, 1)]
            pieces.append(jnp.concatenate([own[:SPAN] + edge[0], own[SPAN : tokens - SPAN], own[tokens - SPAN :] + edge[1]], axis=0).astype(bf))
        d = jnp.concatenate(pieces, axis=1)
        dx_ref[...] += dot(d, w[...], NT)
        if name == "key_b":
            dw[...] += dot(x, d, TN)
            add_vector(dvec_ref, name, column_sum(d.astype(f32)))
        else:
            dw[...] = dot(x, d, TN)
            put_vector(dvec_ref, name, column_sum(d.astype(f32)))


def beside(grid, step):
    return {"seq": lax.axis_index("seq") + step, "row": lax.axis_index("row")}


def seq_edges(grid):
    s = lax.axis_index("seq")
    return s > 0, s < grid.seq - 1


def enter_all(grid, p):
    sem = pltpu.get_barrier_semaphore()
    total = jnp.int32(0)
    before, after = seq_edges(grid)
    targets = [(grid.device(q), cond) for _, q, cond in neighbours_of(grid, p)]
    targets += [(beside(grid, -1), before), (beside(grid, 1), after)]
    for device, cond in targets:
        guarded(cond, lambda device=device: pl.semaphore_signal(sem, inc=1, device_id=device, device_id_type=MESH))
        total = total + (1 if cond is None else cond.astype(jnp.int32))
    pl.semaphore_wait(sem, total)


def remote(source, target, send_sem, recv_sem, device):
    return pltpu.make_async_remote_copy(
        src_ref=source, dst_ref=target, send_sem=send_sem, recv_sem=recv_sem, device_id=device, device_id_type=MESH)


def assemble(grid, shard, slots, wide):
    for k in range(grid.count):
        low, high = shard * k // GROUP, -(-shard * (k + 1) // GROUP)
        shared = k + 1 < grid.count and shard * (k + 1) % GROUP != 0
        begin = low + (1 if k > 0 and shard * k % GROUP != 0 else 0)
        end = high - (1 if shared else 0)
        if end > begin:
            wide[16 * begin : 16 * end, :] = slots[k, 16 * (begin - low) : 16 * (end - low), :].astype(f32)
        if shared:
            wide[16 * end : 16 * high, :] = slots[k, 16 * (end - low) : 16 * (high - low), :].astype(f32) + slots[k + 1, 0:16, :].astype(f32)


def unpack(wide, outs, vec_ref):
    place = matrix_rows()
    for name, out in zip(MATRICES, outs):
        base, rows, pieces = place[name]
        for c in range(pieces):
            out[:, 128 * c : 128 * c + 128] = wide[pl.ds(base + c, rows, stride=pieces), :].astype(bf)
    vec_at, vec_total = vector_rows()
    vec_ref[...] = jnp.zeros((vec_total, 128), f32)
    for name in VECTORS:
        base, _, pieces = place[name]
        vec_ref[vec_at[name][0] : vec_at[name][0] + pieces, :] = wide[base : base + pieces, :]


def gather_kernel(grid, shard, slot_ref, x_ref, seg_ref, *refs):
    many = len(MATRICES)
    outs, (vec_ref, x_ext, seg_ext) = refs[:many], refs[many : many + 3]
    slots, wide, local_sem, send_sem, recv_sem, halo_send, halo_recv = refs[many + 3 :]
    p = grid.here()
    tokens = x_ref.shape[0]
    _, groups = shard_groups(shard, grid.count)
    before, after = seq_edges(grid)
    own = pltpu.make_async_copy(slot_ref, slots.at[grid.flat(p)], local_sem)
    own.start()
    enter_all(grid, p)
    own.wait()

    def halo_copies(side):
        step = -1 if side == 0 else 1
        take = pl.ds(0, SPAN) if side == 0 else pl.ds(tokens - SPAN, SPAN)
        land = pl.ds(tokens + SPAN, SPAN) if side == 0 else pl.ds(0, SPAN)
        return [
            remote(x_ref.at[take, :], x_ext.at[land, :], halo_send.at[side, 0], halo_recv.at[side, 0], beside(grid, step)),
            remote(seg_ref.at[:, take], seg_ext.at[:, land], halo_send.at[side, 1], halo_recv.at[side, 1], beside(grid, step)),
        ]

    def start(side):
        for copy in halo_copies(side):
            copy.start()

    pl.when(before)(lambda: start(0))
    pl.when(after)(lambda: start(1))

    def clear(rows):
        x_ext[rows, :] = jnp.zeros((SPAN, D), bf)
        seg_ext[:, rows] = jnp.zeros((8, SPAN), jnp.int32)

    pl.when(jnp.logical_not(before))(lambda: clear(pl.ds(0, SPAN)))
    pl.when(jnp.logical_not(after))(lambda: clear(pl.ds(tokens + SPAN, SPAN)))
    x_ext[SPAN : SPAN + tokens, :] = x_ref[...]
    seg_ext[:, SPAN : SPAN + tokens] = seg_ref[...]
    Gather(grid, p, slots, send_sem, recv_sem, groups).run()
    assemble(grid, shard, slots, wide)
    unpack(wide, outs, vec_ref)

    def end(side):
        for copy in halo_copies(side):
            copy.wait_send()

    def landed(side):
        for copy in halo_copies(side):
            copy.wait_recv()

    pl.when(before)(lambda: end(0))
    pl.when(after)(lambda: end(1))
    pl.when(after)(lambda: landed(0))
    pl.when(before)(lambda: landed(1))


VMEM = pl.BlockSpec(memory_space=pltpu.VMEM)


def matrix_shapes(dtype):
    return [jax.ShapeDtypeStruct((matrix_rows()[name][1], 128 * matrix_rows()[name][2]), dtype) for name in MATRICES]


def gather_params(grid, shard, slot, x, seg):
    _, groups = shard_groups(shard, grid.count)
    tokens = x.shape[0]
    total = flat_rows(shard, grid.count)
    return pl.pallas_call(
        functools.partial(gather_kernel, grid, shard),
        out_shape=matrix_shapes(bf)
        + [
            jax.ShapeDtypeStruct((vector_rows()[1], 128), f32),
            jax.ShapeDtypeStruct((tokens + 2 * SPAN, D), bf),
            jax.ShapeDtypeStruct((8, tokens + 2 * SPAN), jnp.int32),
        ],
        in_specs=[VMEM] * 3,
        out_specs=[VMEM] * (len(MATRICES) + 3),
        scratch_shapes=[
            pltpu.VMEM((grid.count, 16 * groups, 128), bf),
            pltpu.VMEM((total, 128), f32),
            pltpu.SemaphoreType.DMA,
            pltpu.SemaphoreType.DMA((count_sends(grid, groups),)),
            pltpu.SemaphoreType.DMA((len(orders_of(groups)), grid.count)),
            pltpu.SemaphoreType.DMA((2, 2)),
            pltpu.SemaphoreType.DMA((2, 2)),
        ],
        compiler_params=pltpu.CompilerParams(collective_id=0, has_side_effects=True, vmem_limit_bytes=48 << 20),
    )(slot, x, seg)


def projected(T):
    shape = jax.ShapeDtypeStruct
    E = T + 2 * SPAN
    natural = {"q": (T, 128), "qT": (128, T), "k": (E, 128), "kT": (128, E), "kTr": (128, E), "v": (E, 128), "vT": (128, E)}
    tables = {"krt": (512, 128), "krtT": (128, 512), "qrt": (1024, 128), "qrtT": (128, 640)}
    out = {name: shape((PAIRS,) + extent, bf) for name, extent in (natural | tables).items()}
    out["krt"] = shape((2 * PAIRS, 512, 128), bf)
    out["pos"] = shape((512, D), bf)
    out["ctx"] = shape((PAIRS, T, 128), bf)
    out["e"] = shape((PAIRS, T // 128, 640, 256), bf)
    out["inv"] = shape((PAIRS, T // 128, 8, 256), f32)
    return out


def forward_kernel(x_ref, seg_ref, query_w, key_w, value_w, table_ref, vec_ref, *refs):
    names = list(projected(128))
    outs = dict(zip(names, refs))
    project_body(x_ref, query_w, key_w, value_w, table_ref, vec_ref, *[outs[n] for n in names[:12]])
    att_fwd_body(outs["q"].shape[1] // 128, outs["qT"], outs["k"], outs["vT"], outs["krt"], outs["qrtT"], seg_ref, outs["ctx"], outs["e"], outs["inv"], *refs[len(names) :])


def forward(x_ext, seg_ext, query_w, key_w, value_w, table, vec):
    T = x_ext.shape[0] - 2 * SPAN
    blocks = T // 128
    outs = projected(T)
    results = pl.pallas_call(
        forward_kernel,
        out_shape=list(outs.values()),
        in_specs=[VMEM] * 7,
        out_specs=[VMEM] * len(outs),
        scratch_shapes=[pltpu.VMEM((2 * (blocks + 4), 2, 128, 640), bf), pltpu.VMEM((blocks, 640, 128), f32)]
        + [pltpu.VMEM((640, 256), f32)] * 2 + [pltpu.VMEM((512, 256), f32)] * 2 + [pltpu.VMEM((640, 256), f32)] * 2 + [pltpu.VMEM((8, 256), f32)] * 2,
        compiler_params=pltpu.CompilerParams(vmem_limit_bytes=60 << 20),
    )(x_ext, seg_ext, query_w, key_w, value_w, table, vec)
    return dict(zip(outs, results))


def backward(f, dctxT):
    T = dctxT.shape[2]
    E, blocks = T + 2 * SPAN, T // 128
    shape = jax.ShapeDtypeStruct
    accumulator = shape((PAIRS, E, 128), f32)
    return pl.pallas_call(
        functools.partial(att_bwd_body, blocks),
        out_shape=[shape((PAIRS, T, 128), bf), accumulator, accumulator, accumulator, shape((PAIRS, 512, 128), f32), shape((PAIRS, 128, 640), f32)],
        in_specs=[VMEM] * 10,
        out_specs=[VMEM] * 6,
        scratch_shapes=[pltpu.VMEM((2 * (blocks + 4), 2, 128, 640), bf), pltpu.VMEM((640, 256), f32), pltpu.VMEM((512, 256), f32)]
        + [pltpu.VMEM((640, 256), bf)] * 2 + [pltpu.VMEM((512, 256), bf)] * 2,
        compiler_params=pltpu.CompilerParams(vmem_limit_bytes=60 << 20),
    )(f["q"], f["kT"], f["kTr"], f["v"], f["krtT"], f["qrt"], f["qrtT"][:, :, 512:], dctxT, f["e"], f["inv"])


def feed_kernel(x_ref, ctx_ref, og_ref, output_w, up_w, down_w, vec_ref, out_ref, dz1_ref, dctx_ref, dflat_ref, dvec_ref, ml, dup, act, ddown, dattn, slope, wide):
    feed_body(x_ref, ctx_ref, og_ref, output_w, up_w, down_w, vec_ref, out_ref, dz1_ref, dctx_ref, wide, dvec_ref, ml, dup, act, ddown, dattn, slope)
    dflat_ref[...] = wide[...].astype(bf)


def feed(x_ext, ctx, out_grad, output_w, up_w, down_w, vec):
    T = out_grad.shape[0]
    shape = jax.ShapeDtypeStruct
    return pl.pallas_call(
        feed_kernel,
        out_shape=[shape((T, D), bf), shape((T, D), f32), shape((PAIRS, 128, T), bf), shape((FEED_ROWS, 128), bf), shape(vec.shape, f32)],
        in_specs=[VMEM] * 7,
        out_specs=[VMEM] * 5,
        scratch_shapes=[
            pltpu.VMEM((T, D), bf), pltpu.VMEM((T, FF), bf), pltpu.VMEM((T, FF), bf), pltpu.VMEM((T, D), bf), pltpu.VMEM((T, D), bf),
            pltpu.VMEM((256, FF), f32), pltpu.VMEM((FEED_ROWS, 128), f32),
        ],
        compiler_params=pltpu.CompilerParams(vmem_limit_bytes=56 << 20),
    )(x_ext, ctx, out_grad, output_w, up_w, down_w, vec)


def tail_kernel(grid, shard, dq_ref, dkc_ref, dkp_ref, dv_ref, dkr_ref, dqr_ref, dz1_ref, x_ref, pos_ref, table_ref, vec_ref, query_w, key_w, value_w, dflat_ref, dvec_in,
                dx_ref, sum_ref, dvec_ref, dwq, dwk, dwv, dtable, wide, flat, kids, outgoing, total, halo_out, halo_in, send_sem, recv_sem, halo_send, halo_recv):
    p = grid.here()
    tokens = dx_ref.shape[0]
    _, groups = shard_groups(shard, grid.count)
    before, after = seq_edges(grid)
    enter_all(grid, p)
    rims = (pl.ds(0, SPAN), pl.ds(tokens + SPAN, SPAN))
    for side in (0, 1):
        halo_out[side, 0] = (SC * (dkc_ref[:, rims[side], :] + dkp_ref[:, rims[side], :])).astype(bf)
        halo_out[side, 1] = dv_ref[:, rims[side], :].astype(bf)

    def halo_copy(side):
        return remote(halo_out.at[side], halo_in.at[1 - side], halo_send.at[side], halo_recv.at[1 - side], beside(grid, -1 if side == 0 else 1))

    pl.when(before)(lambda: halo_copy(0).start())
    pl.when(after)(lambda: halo_copy(1).start())

    def clear(side):
        halo_in[side] = jnp.zeros(halo_in.shape[1:], bf)

    pl.when(jnp.logical_not(before))(lambda: clear(0))
    pl.when(jnp.logical_not(after))(lambda: clear(1))
    dvec_ref[...] = dvec_in[...]
    tail_local(dq_ref, x_ref, dz1_ref, query_w, dx_ref, dwq, dvec_ref)
    tail_table(dkr_ref, dqr_ref, pos_ref, table_ref, vec_ref, query_w, key_w, dwq, dwk, dtable, dvec_ref)
    pl.when(before)(lambda: halo_copy(0).wait_send())
    pl.when(after)(lambda: halo_copy(1).wait_send())
    pl.when(before)(lambda: halo_copy(1).wait_recv())
    pl.when(after)(lambda: halo_copy(0).wait_recv())
    tail_keys(dkc_ref, dkp_ref, dv_ref, halo_in, x_ref, key_w, value_w, dx_ref, dwk, dwv, dvec_ref)
    place = matrix_rows()
    rest = flat.shape[0] - FEED_FIRST - FEED_ROWS
    wide[FEED_FIRST:, :] = jnp.zeros((rest, 128), f32)
    moved = lambda row: row if row < FEED_FIRST else row - FEED_ROWS
    for name, ref in (("query_w", dwq), ("key_w", dwk), ("value_w", dwv), ("rel_table", dtable)):
        base, rows, pieces = place[name]
        for c in range(pieces):
            wide[pl.ds(moved(base) + c, rows, stride=pieces), :] = ref[:, 128 * c : 128 * c + 128]
    vec_at, _ = vector_rows()
    for name in VECTORS:
        base, _, pieces = place[name]
        wide[moved(base) : moved(base) + pieces, :] = dvec_ref[vec_at[name][0] : vec_at[name][0] + pieces, :]
    flat[0:FEED_FIRST, :] = wide[0:FEED_FIRST, :].astype(bf)
    flat[FEED_FIRST : FEED_FIRST + FEED_ROWS, :] = dflat_ref[...]
    flat[FEED_FIRST + FEED_ROWS :, :] = wide[FEED_FIRST:, :].astype(bf)
    Scatter(grid, p, flat, lambda k: (k * shard // GROUP) * 16, kids, outgoing, total, send_sem, recv_sem, groups).run(sum_ref)


def tail(grid, shard, *args):
    _, groups = shard_groups(shard, grid.count)
    rows = flat_rows(shard, grid.count)
    tokens = args[6].shape[0]
    names, half = len(direction_names(grid)), grid.count // 2
    shape = jax.ShapeDtypeStruct
    dx, summed, _ = pl.pallas_call(
        functools.partial(tail_kernel, grid, shard),
        out_shape=[shape((tokens, D), f32), shape((16 * groups, 128), f32), shape((vector_rows()[1], 128), f32)],
        in_specs=[VMEM] * 16,
        out_specs=[VMEM] * 3,
        scratch_shapes=[
            pltpu.VMEM((D, D), f32), pltpu.VMEM((D, D), f32), pltpu.VMEM((D, D), f32), pltpu.VMEM((2 * SPAN, D), f32),
            pltpu.VMEM((rows - FEED_ROWS, 128), f32),
            pltpu.VMEM((rows, 128), bf),
            pltpu.VMEM((names, half, 16 * groups, 128), bf),
            pltpu.VMEM((half, 16 * groups, 128), bf),
            pltpu.VMEM((16 * groups, 128), f32),
            pltpu.VMEM((2, 2, PAIRS, SPAN, 128), bf),
            pltpu.VMEM((2, 2, PAIRS, SPAN, 128), bf),
            pltpu.SemaphoreType.DMA((scatter_sends(grid, groups),)),
            pltpu.SemaphoreType.DMA((len(orders_of(groups)), names, half)),
            pltpu.SemaphoreType.DMA((2,)),
            pltpu.SemaphoreType.DMA((2,)),
        ],
        compiler_params=pltpu.CompilerParams(collective_id=1, has_side_effects=True, vmem_limit_bytes=60 << 20),
    )(*args)
    return dx, summed


def on_device(layer_input, segment_ids, out_grad, weights, momentum, average):
    tokens_here = layer_input.shape[1]
    grid = Grid(lax.axis_size("seq"), lax.axis_size("row"))
    shard = weights.shape[0]
    _, groups = shard_groups(shard, grid.count)
    shift = (lax.axis_index("seq") * grid.row + lax.axis_index("row")) * shard % GROUP
    slot = lax.dynamic_update_slice(jnp.zeros((GROUP * groups,), bf), weights.astype(bf), (shift,)).reshape(16 * groups, 128)
    seg = jnp.broadcast_to(segment_ids + 1, (8, tokens_here))
    *matrices, vec, x_ext, seg_ext = gather_params(grid, shard, slot, layer_input[0], seg)
    query_w, key_w, value_w, output_w, up_w, down_w, table = matrices
    f = forward(x_ext, seg_ext, query_w, key_w, value_w, table, vec)
    block_output, dz1, dctxT, dflat, dvec = feed(x_ext, f["ctx"], out_grad[0], output_w, up_w, down_w, vec)
    summed_up = backward(f, dctxT)
    dx, summed = tail(grid, shard, *summed_up, dz1, x_ext, f["pos"], table, vec, query_w, key_w, value_w, dflat, dvec)
    weight_grad = lax.dynamic_slice(summed.reshape(-1), (shift,), (shard,))
    all_tokens = tokens_here * grid.seq * layer_input.shape[0] * grid.row
    rate = 0.1 / math.sqrt(all_tokens)
    new_momentum = 0.5 * momentum + weight_grad
    new_weights = weights - rate * (weight_grad + 0.5 * new_momentum)
    new_average = 0.5 * average + 0.5 * new_weights
    return (
        block_output[None],
        dx[None],
        weight_grad,
        new_momentum,
        new_average,
        new_weights,
        new_weights.astype(jnp.bfloat16),
    )


def solution(mesh):
    flat = P(("seq", "row"))
    tokens = P("row", "seq", None)
    return jax.shard_map(
        on_device,
        mesh=mesh,
        in_specs=(tokens, P("row", "seq"), tokens, flat, flat, flat),
        out_specs=(tokens, tokens, flat, flat, flat, flat, flat),
        check_vma=False,
    )
```

```python
import functools
import itertools
import math

import jax
import jax.numpy as jnp
from jax import lax
from jax.experimental import pallas as pl
from jax.experimental.pallas import tpu as pltpu
from jax.sharding import PartitionSpec as P

D = 384
HEADS = 6
HEAD_DIM = 64
FF = 1536
SPAN = 256
PAIRS = HEADS // 2
NB = 5
EPSILON = 1e-07
(N_ATTN_GAIN, N_ATTN_SHIFT, N_CTX, N_DCTX_TURNED, N_DFLAT, N_DOWN_BIAS, N_DOWN_W, N_DVEC, N_DZ1, N_E, N_FFN_GAIN, N_FFN_SHIFT, N_INV, N_K, N_K_TURNED, N_K_TURNED_BACK, N_KEY_B, N_KEY_W, N_KRT, N_KRT_TURNED, N_OUT, N_OUTPUT_B, N_OUTPUT_W, N_POS, N_Q, N_Q_TURNED, N_QRT, N_QRT_TURNED, N_QUERY_B, N_QUERY_W, N_REL_GAIN, N_REL_SHIFT, N_REL_TABLE, N_SEG_EXT, N_UP_BIAS, N_UP_W, N_V, N_V_TURNED, N_VALUE_B, N_VALUE_W, N_VEC, N_X_EXT) = range(42)
bf = jnp.bfloat16
f32 = jnp.float32


MESH = pl.DeviceIdType.MESH
GROUP = 2048


class Grid:
    def __init__(self, seq, row):
        half = seq // 2
        wide = 1
        while wide * wide * 4 <= half:
            wide *= 2
        self.size = {"z": half // wide, "y": wide, "x": row}
        self.seq, self.row, self.count = seq, row, seq * row
        self.split = self.count <= 64

    def here(self):
        s, x = lax.axis_index("seq"), lax.axis_index("row")
        y_size = self.size["y"]
        return {"z": s // (2 * y_size), "y": (s // 2) % y_size, "c": s % 2, "x": x}

    def seq_of(self, p):
        return (p["z"] * self.size["y"] + p["y"]) * 2 + p["c"]

    def flat(self, p):
        return self.seq_of(p) * self.row + p["x"]

    def device(self, p):
        return {"seq": self.seq_of(p), "row": p["x"]}

    def plane(self, p):
        return (p["z"] * self.size["y"] + p["y"]) * self.row + p["x"]

    def offsets(self, order):
        choices = []
        for axis in order:
            n = self.size[axis]
            if n == 2:
                choices.append([0, "f"])
            else:
                choices.append([0] + [sign * d for d in range(1, n) for sign in (-1, 1)])
        hops = lambda off: sum(1 if o == "f" else abs(o) for o in off)
        return sorted(itertools.product(*choices), key=hops)


def both(conds):
    out = None
    for cond in conds:
        if cond is not None:
            out = cond if out is None else jnp.logical_and(out, cond)
    return out


def guarded(cond, fn):
    if cond is None:
        fn()
    else:
        pl.when(cond)(fn)


def source_of(grid, p, order, off):
    o, conds = dict(p), []
    for axis, d in zip(order, off):
        if d == "f":
            o[axis] = 1 - p[axis]
        elif d != 0:
            o[axis] = p[axis] + d
            conds.append(p[axis] + d >= 0 if d < 0 else p[axis] + d < grid.size[axis])
    return o, both(conds)


def parent_of(grid, p, order, off):
    last = max((i for i, d in enumerate(off) if d != 0), default=None)
    if last is None:
        return None, None
    q, axis, d = dict(p), order[last], off[last]
    if d == "f":
        q[axis] = 1 - p[axis]
        return q, axis + "0"
    q[axis] = p[axis] + (1 if d > 0 else -1)
    return q, axis + ("+" if d > 0 else "-")


def children_of(grid, p, order, off):
    last = max((i for i, d in enumerate(off) if d != 0), default=None)
    found = []
    if last is not None and off[last] != "f":
        axis, away = order[last], (-1 if off[last] > 0 else 1)
        q = dict(p)
        q[axis] = p[axis] + away
        found.append((axis + ("+" if away > 0 else "-"), q, p[axis] > 0 if away < 0 else p[axis] < grid.size[axis] - 1))
    for axis in order[0 if last is None else last + 1 :]:
        if grid.size[axis] == 2:
            q = dict(p)
            q[axis] = 1 - p[axis]
            found.append((axis + "0", q, None))
        elif grid.size[axis] > 2:
            for sign in (1, -1):
                q = dict(p)
                q[axis] = p[axis] + sign
                found.append((axis + ("+" if sign > 0 else "-"), q, p[axis] > 0 if sign < 0 else p[axis] < grid.size[axis] - 1))
    return found


def neighbours_of(grid, p):
    found = []
    for axis in ("z", "y", "x"):
        found += children_of(grid, p, (axis,), (0,))
    sibling = dict(p)
    sibling["c"] = 1 - p["c"]
    found.append(("c0", sibling, None))
    return found


def enter(grid, p, extra=()):
    sem = pltpu.get_barrier_semaphore()
    total = jnp.int32(0)
    for name, q, cond in neighbours_of(grid, p) + list(extra):
        guarded(cond, lambda q=q: pl.semaphore_signal(sem, inc=1, device_id=grid.device(q), device_id_type=MESH))
        total = total + (1 if cond is None else cond.astype(jnp.int32))
    pl.semaphore_wait(sem, total)


def orders_of(groups):
    return (("z", "y", "x"), ("x", "z", "y")) if groups >= 8 else (("z", "y", "x"),)


def spans(groups):
    if groups < 8:
        return ((0, 16 * groups),)
    first = (groups * 20 + 16) // 32
    return ((0, 16 * first), (16 * first, 16 * (groups - first)))


class Gather:
    def __init__(self, grid, p, slots, send_sem, recv_sem, groups):
        self.grid, self.p, self.slots = grid, p, slots
        self.send_sem, self.recv_sem, self.groups = send_sem, recv_sem, groups
        self.sends, self.used = [], 0

    def copy(self, part, k, q, index):
        start, rows = spans(self.groups)[part]
        block = self.slots.at[k, pl.ds(start, rows), :]
        return pltpu.make_async_remote_copy(
            src_ref=block, dst_ref=block, send_sem=self.send_sem.at[index], recv_sem=self.recv_sem.at[part, k],
            device_id=self.grid.device(q), device_id_type=MESH)

    def arrived(self, part, k):
        start, rows = spans(self.groups)[part]
        block = self.slots.at[k, pl.ds(start, rows), :]
        pltpu.make_async_remote_copy(
            src_ref=block, dst_ref=block, send_sem=self.send_sem.at[0], recv_sem=self.recv_sem.at[part, k],
            device_id=self.grid.device(self.p), device_id_type=MESH).wait_recv()

    def plan(self, chosen):
        grid, p = self.grid, self.p
        sibling = dict(p)
        sibling["c"] = 1 - p["c"]
        levels, ends, partners, used = {}, [], [], 0
        for part, order in enumerate(orders_of(self.groups)):
            for off in grid.offsets(order):
                hops = sum(1 if o == "f" else abs(o) for o in off)
                o, cond = source_of(grid, p, order, off)
                k = grid.flat(o)
                targets = children_of(grid, p, order, off) + [("c0", sibling, None)]
                indices = [used + i for i in range(len(targets))]
                used += len(targets)
                cond = both([cond, chosen(k)])

                def step(part=part, k=k, targets=targets, indices=indices, own=hops == 0):
                    if not own:
                        self.arrived(part, k)
                    for (name, q, when), index in zip(targets, indices):
                        guarded(when, lambda q=q, index=index: self.copy(part, k, q, index).start())

                def end(part=part, k=k, targets=targets, indices=indices):
                    for (name, q, when), index in zip(targets, indices):
                        guarded(when, lambda q=q, index=index: self.copy(part, k, q, index).wait_send())

                levels.setdefault(hops, []).append((cond, step))
                ends.append((cond, end))
                o, cond = source_of(grid, sibling, order, off)
                k = grid.flat(o)
                partners.append((both([cond, chosen(k)]), lambda part=part, k=k: self.arrived(part, k)))
        return [levels[h] for h in sorted(levels)], partners, ends


def perform(steps):
    for cond, step in steps:
        guarded(cond, step)


def count_sends(grid, groups):
    fake = {"z": jnp.int32(0), "y": jnp.int32(0), "x": jnp.int32(0), "c": jnp.int32(0)}
    return sum(len(children_of(grid, fake, order, off)) + 1 for order in orders_of(groups) for off in grid.offsets(order))


OPPOSITE = {"+": "-", "-": "+", "0": "0"}


def direction_names(grid):
    names = ["c0"]
    for axis in ("z", "y", "x"):
        if grid.size[axis] == 2:
            names.append(axis + "0")
        elif grid.size[axis] > 2:
            names += [axis + "+", axis + "-"]
    return names


class Scatter:
    def __init__(self, grid, p, flat, first_row, kids, total, send_sem, recv_sem, groups):
        self.grid, self.p, self.flat, self.first_row = grid, p, flat, first_row
        self.kids, self.total = kids, total
        self.send_sem, self.recv_sem, self.groups = send_sem, recv_sem, groups
        self.names = direction_names(grid)

    def incoming(self, part, name, place):
        start, rows = spans(self.groups)[part]
        return self.kids.at[self.names.index(name), place, pl.ds(start, rows), :]

    def transfer(self, source, part, name, place, q, send):
        return pltpu.make_async_remote_copy(
            src_ref=source, dst_ref=self.incoming(part, name, place), send_sem=self.send_sem.at[send],
            recv_sem=self.recv_sem.at[part, self.names.index(name), place], device_id=self.grid.device(q), device_id_type=MESH)

    def arrived(self, part, name, place):
        block = self.incoming(part, name, place)
        pltpu.make_async_remote_copy(
            src_ref=block, dst_ref=block, send_sem=self.send_sem.at[0],
            recv_sem=self.recv_sem.at[part, self.names.index(name), place],
            device_id=self.grid.device(self.p), device_id_type=MESH).wait_recv()

    def plan(self, result, chosen):
        grid, p = self.grid, self.p
        sibling = dict(p)
        sibling["c"] = 1 - p["c"]
        gifts, levels, ends, used = [], {}, [], 0
        for part, order in enumerate(orders_of(self.groups)):
            for off in sorted(grid.offsets(order), key=lambda off: -sum(1 if o == "f" else abs(o) for o in off)):
                hops = sum(1 if o == "f" else abs(o) for o in off)
                start, rows = spans(self.groups)[part]
                o, cond = source_of(grid, sibling, order, off)
                cond = both([cond, chosen(grid.flat(o))])

                def give(part=part, o=o, index=used, start=start, rows=rows):
                    block = self.flat.at[pl.ds(pl.multiple_of(self.first_row(grid.flat(o)) + start, 16), rows), :]
                    return self.transfer(block, part, "c0", grid.plane(o), sibling, index)

                gifts.append((cond, lambda give=give: give().start()))
                ends.append((cond, lambda give=give: give().wait_send()))
                used += 1
                o, cond = source_of(grid, p, order, off)
                place, k = grid.plane(o), grid.flat(o)
                cond = both([cond, chosen(k)])
                kids = children_of(grid, p, order, off)
                parent, side = parent_of(grid, p, order, off)

                def push(part=part, place=place, parent=parent, side=side, index=used, start=start, rows=rows):
                    return self.transfer(self.incoming(part, "c0", place), part, side[0] + OPPOSITE[side[1]], place, parent, index)

                def step(part=part, place=place, k=k, kids=kids, parent=parent, start=start, rows=rows, push=push):
                    self.arrived(part, "c0", place)
                    mine = self.flat[pl.ds(pl.multiple_of(self.first_row(k) + start, 16), rows), :].astype(f32)
                    self.total[0:rows, :] = mine + self.incoming(part, "c0", place)[...].astype(f32)
                    for name, q, when in kids:

                        def add(name=name):
                            self.arrived(part, name, place)
                            self.total[0:rows, :] += self.incoming(part, name, place)[...].astype(f32)

                        guarded(when, add)
                    if parent is None:
                        result[pl.ds(start, rows), :] = self.total[0:rows, :]
                    else:
                        self.kids[0, place, pl.ds(start, rows), :] = self.total[0:rows, :].astype(bf)
                        push().start()

                levels.setdefault(-hops, []).append((cond, step))
                if parent is not None:
                    ends.append((cond, lambda push=push: push().wait_send()))
                    used += 1
        return gifts, [levels[h] for h in sorted(levels)], ends


def scatter_sends(grid, groups):
    return 2 * sum(len(grid.offsets(order)) for order in orders_of(groups))


def shard_groups(shard, count):
    first = [shard * k // GROUP for k in range(count)]
    groups = max(-(-shard * (k + 1) // GROUP) - first[k] for k in range(count))
    return first, max(groups, 2)


def flat_rows(shard, count):
    first, groups = shard_groups(shard, count)
    return 16 * (first[-1] + groups)


def layer_pieces():
    square, vector_of = (D, D), (D,)
    return (
        (N_QUERY_W, square), (N_KEY_W, square), (N_VALUE_W, square), (N_OUTPUT_W, square), (N_UP_W, (D, FF)), (N_DOWN_W, (FF, D)),
        (N_QUERY_B, vector_of), (N_KEY_B, vector_of), (N_VALUE_B, vector_of), (N_OUTPUT_B, vector_of), (N_ATTN_GAIN, vector_of),
        (N_ATTN_SHIFT, vector_of), (N_UP_BIAS, (FF,)), (N_DOWN_BIAS, vector_of), (N_FFN_GAIN, vector_of), (N_FFN_SHIFT, vector_of),
        (N_REL_TABLE, (2 * SPAN, D)), (N_REL_GAIN, vector_of), (N_REL_SHIFT, vector_of),
    )


def matrix_rows():
    place, at = {}, 0
    for name, extent in layer_pieces():
        if len(extent) == 2:
            place[name] = (at // 128, extent[0], extent[1] // 128)
        else:
            place[name] = (at // 128, 1, extent[0] // 128)
        at += math.prod(extent)
    return place


MATRICES = (N_QUERY_W, N_KEY_W, N_VALUE_W, N_OUTPUT_W, N_UP_W, N_DOWN_W, N_REL_TABLE)
VECTORS = tuple(name for name, extent in layer_pieces() if len(extent) == 1)
FEED_FIRST = matrix_rows()[N_OUTPUT_W][0]
FEED_ROWS = matrix_rows()[N_QUERY_B][0] - FEED_FIRST
USED_ROWS = sum(rows * pieces for _, rows, pieces in matrix_rows().values())


def vector_rows():
    place, at = {}, 0
    for name in VECTORS:
        wide = matrix_rows()[name][2]
        place[name] = (at, wide)
        at += wide
    return place, -(-at // 8) * 8


SC = 1.0 / math.sqrt(3.0 * HEAD_DIM)
LOG2E = 1.4426950408889634
NT = (((1,), (1,)), ((), ()))
NN = (((1,), (0,)), ((), ()))
TN = (((0,), (0,)), ((), ()))


def dot(a, b, dims=NN):
    return lax.dot_general(a, b, dims, preferred_element_type=f32)


def iotas(rows, lanes):
    return lax.broadcasted_iota(jnp.int32, (rows, lanes), 0), lax.broadcasted_iota(jnp.int32, (rows, lanes), 1)


def tile(i):
    return pl.ds(pl.multiple_of(i * 128, 128), 128)


def window(i):
    return pl.ds(pl.multiple_of(i * 128, 128), NB * 128)


def wide_diagonal(columns):
    zero = jnp.zeros((64, 128), columns.dtype)
    return jnp.concatenate([jnp.concatenate([columns[:64], zero], axis=1), jnp.concatenate([zero, columns[64:]], axis=1)], axis=0)


def tall_diagonal(rows):
    lane = iotas(128, 128)[1]
    zero = jnp.zeros_like(rows)
    return jnp.concatenate([jnp.where(lane < 64, rows, zero), jnp.where(lane >= 64, rows, zero)], axis=0)


def own_heads(wide):
    return jnp.concatenate([wide[:64, :128], wide[64:, 128:]], axis=0)


def turn_rows(values, back):
    size = values.shape[0]
    lane = iotas(*values.shape)[1]
    for step in (64, 32, 16, 8, 4, 2, 1):
        moved = pltpu.roll(values, size - step if back else step, 0)
        values = jnp.where(lane & step != 0, moved, values)
    return values


def turn_lanes(values, first):
    return jnp.concatenate([pltpu.roll(values[8 * g : 8 * g + 8, :512], first + 8 * g, 1, stride=1, stride_axis=0) for g in range(16)], axis=0)


def stream_rows(load, up, fine):
    row, lane = iotas(8, 128)
    inner = [(step, lane & step != 0, row < step if not up else row >= 8 - step) for step in fine]
    masks = [lane & step != 0 for step in (8, 16, 32, 64)]
    turned = [None for _ in inner]
    past = [[] for _ in masks]
    extra = 15 + len(inner)
    order = list(range(64 - extra, 64)) + list(range(64)) if not up else list(reversed(list(range(64)) + list(range(extra))))
    for n, i in enumerate(order):
        value = load(i)
        for level, (step, mask, edge) in enumerate(inner):
            now = pltpu.roll(value, step if not up else 8 - step, 0)
            if turned[level] is not None:
                value = jnp.where(mask, jnp.where(edge, turned[level], now), value)
            turned[level] = now
        for level, mask in enumerate(masks):
            past[level].append(value)
            if len(past[level]) > 1 << level:
                value = jnp.where(mask, past[level].pop(0), value)
        if n >= extra:
            yield i, value


def att_fwd_body(nblk, qT_ref, k_ref, vT_ref, krt_ref, qrtT_ref, seg_ref, ctx_ref, p_ref, inv_ref, x_scr, bias_scr, s0, s1, z0, z1, t0, t1, m0, m1, hook=None):
    row, lane = iotas(128, 128)
    lane2 = iotas(128, 256)[1]
    lane512 = iotas(512, 256)[1]
    items, keys = PAIRS * nblk, nblk + 4

    def mk_bias(t, carry):
        sq = seg_ref[0:1, tile(t + 2)].astype(f32)
        for b in range(NB):
            sk = jnp.broadcast_to(seg_ref[0:1, tile(t + b)], (128, 128)).astype(f32).T
            ok = sk == sq
            if b == 0:
                ok = ok & (row >= lane)
            if b == NB - 1:
                ok = ok & (row <= lane)
            bias_scr[t, 128 * b : 128 * b + 128, :] = jnp.where(ok, 0.0, -1e30).astype(f32)
        return carry

    lax.fori_loop(0, nblk, mk_bias, 0)

    def keyside(p, J, slot):
        C = dot(tall_diagonal(k_ref[p, tile(J), :]), qrtT_ref[p])
        for h in range(2):
            Ch = C[128 * h : 128 * h + 128]
            R = turn_lanes(Ch, 0)
            x_scr[slot, h, :, 0:128] = jnp.where(lane > row, R[:, :128], Ch[:, 512:]).astype(bf)
            x_scr[slot, h, :, 128:512] = R[:, 128:].astype(bf)
            x_scr[slot, h, :, 512:640] = R[:, :128].astype(bf)

    def start(J, carry):
        keyside(0, J, J)
        return carry

    lax.fori_loop(0, keys, start, 0)

    def scores(n, s_scr, z_scr, t_scr, m_scr):
        n = jnp.minimum(n, items - 1)
        p, t = n // nblk, n % nblk
        base = (p % 2) * keys + t
        Q2 = wide_diagonal(qT_ref[p, :, tile(t)])
        odd = lane2 % 2 == 1
        zero = jnp.zeros_like(Q2)
        table = krt_ref[p]
        moved = krt_ref[PAIRS + p]
        Z = dot(jnp.concatenate([table, moved], axis=1), jnp.concatenate([jnp.where(odd, zero, Q2), jnp.where(odd, Q2, zero)], axis=0))
        ends = jnp.where(odd[:1], Z[2:3], Z[1:2])
        z_scr[...] = Z
        s_scr[...] = dot(k_ref[p, window(t), :], Q2)
        for h in range(2):
            cols = slice(128 * h, 128 * h + 128)

            def load(i):
                return z_scr[8 * i : 8 * i + 8, cols]

            end = ends[:, cols]
            top = None
            held = None
            for i, y in stream_rows(load, False, (2, 4)):
                if i % 2 == 0:
                    held = y
                    continue
                at, b = 8 * (i - 1), i // 16
                y = jnp.concatenate([held, y], axis=0)
                for block in (0, 4) if b == 0 else (b,):
                    r = at + 128 * (block - b)
                    rows = slice(r, r + 16)
                    inner = slice(at % 128, at % 128 + 16)
                    x = x_scr[base + block, h, inner, 128 * (4 - block) : 128 * (5 - block)].astype(f32)
                    part = y
                    if block == 0:
                        part = jnp.where(iotas(16, 128)[0] + at > iotas(16, 128)[1], y, end)
                    T = s_scr[rows, cols] + bias_scr[t, rows, :] + part + x
                    t_scr[rows, cols] = T
                    most = jnp.maximum(T[:8], T[8:])
                    top = most if top is None else jnp.maximum(top, most)
            m_scr[:, cols] = top

    def soft(n, t_scr, m_scr):
        n = jnp.clip(n, 0, items - 1)
        m = jnp.max(m_scr[...], axis=0, keepdims=True)
        total = None
        for i in range(40):
            e = jnp.exp2((t_scr[16 * i : 16 * i + 16, :] - m) * (SC * LOG2E))
            part = e[:8] + e[8:]
            total = part if total is None else total + part
            p_ref[n // nblk, n % nblk, 16 * i : 16 * i + 16, :] = e.astype(bf)
        inv_ref[n // nblk, n % nblk] = jnp.broadcast_to(1.0 / jnp.sum(total, axis=0, keepdims=True), (8, 256))

    def context(n):
        n = jnp.clip(n, 0, items - 1)
        p, t = n // nblk, n % nblk
        ctxT = own_heads(dot(vT_ref[p, :, window(t)], p_ref[p, t]) * inv_ref[p, t, 0:1, :])
        ctx_ref[p, tile(t), :] = ctxT.astype(bf).T

    half = nblk // 2
    per = keys // half

    def body(m, slot):
        context(2 * m - 2)
        soft(2 * m - 1, t1, m1)
        scores(2 * m, s0, z0, t0, m0)
        context(2 * m - 1)
        soft(2 * m, t0, m0)
        scores(2 * m + 1, s1, z1, t1, m1)
        p, first = jnp.minimum(m // half + 1, PAIRS - 1), per * (m % half)
        for i in range(per):
            keyside(p, first + i, slot + i)
        if hook is not None:
            hook(m)
        return jnp.where(slot + per == 2 * keys, 0, slot + per)

    lax.fori_loop(0, items // 2 + 1, body, jnp.int32(keys))


def unreversed(values, JR):
    high = values.astype(bf)
    low = (values - high.astype(f32)).astype(bf)
    both = dot(JR, jnp.concatenate([high, low], axis=1))
    return both[:, :128] + both[:, 128:]


def att_bwd_body(nblk, q_ref, kT_ref, kTr_ref, v_ref, krtT_ref, qrt_ref, qrtT_ref, dctxT_ref, e_ref, inv_ref, dq_ref, dkc_ref, dkp_ref, dv_ref, dkr_ref, dqr_ref,
                 gt_scr, dp_scr, gm_scr, gb0, gb1, gu0, gu1, e_scr, e_sem, hook):
    row, lane = iotas(128, 128)
    row16, lane16 = iotas(16, 256)
    JR = (row + lane == 127).astype(bf)
    zero = jnp.zeros((128, 128), bf)
    items, keys, half = PAIRS * nblk, nblk + 4, nblk // 2
    per = keys // half
    gt_scr[...] = jnp.zeros(gt_scr.shape, bf)
    gb1[...] = jnp.zeros(gb1.shape, bf)
    gu1[...] = jnp.zeros(gu1.shape, bf)
    for ref in (dkc_ref, dv_ref, dkr_ref, dqr_ref):
        ref[...] = jnp.zeros(ref.shape, f32)

    def kblocks(p, first, base):
        turned = [[], []]
        for i in range(per):
            for h in range(2):
                GT = gt_scr[base + first + i, h]
                Gm = jnp.concatenate([jnp.where(lane > row, GT[:, :128], GT[:, 512:]), GT[:, 128:512]], axis=1)
                turned[h].append(turn_lanes(dot(JR, Gm), 385).astype(bf))
        stacked = [jnp.concatenate(part, axis=0) for part in turned]
        dk = dot(jnp.concatenate(stacked, axis=1), qrt_ref[p])
        for i in range(per):
            dkp_ref[p, tile(first + i), :] = unreversed(dk[128 * i : 128 * i + 128], JR)
        span = pl.ds(pl.multiple_of(first * 128, 128), 128 * per)
        for h in range(2):
            heads = slice(64 * h, 64 * h + 64)
            dqr_ref[p, heads, 0:512] += dot(kTr_ref[p, heads, span], stacked[h])

    def upstream(n, slot, gb, gu, held):
        p, t = n // nblk, n % nblk
        D2 = wide_diagonal(dctxT_ref[p, :, tile(t)])
        inv = inv_ref[p, t, 0:1, :]
        dp_scr[...] = dot(v_ref[p, window(t), :], D2)
        total = None
        for i in range(40):
            rows = slice(16 * i, 16 * i + 16)
            w = e_scr[held, rows, :].astype(f32) * dp_scr[rows, :]
            part = w[:8] + w[8:]
            total = part if total is None else total + part
        less = jnp.sum(total, axis=0, keepdims=True) * inv * inv

        def grad(i):
            rows = slice(16 * i, 16 * i + 16)
            G = e_scr[held, rows, :].astype(f32) * (dp_scr[rows, :] * inv - less)
            Gb = G.astype(bf)
            gb[rows, :] = Gb
            b = i // 8
            for h in range(2):
                gt_scr[slot + b, h, 16 * (i % 8) : 16 * (i % 8) + 16, 128 * (4 - b) : 128 * (5 - b)] = Gb[:, 128 * h : 128 * h + 128]
            return G

        ends = None
        final = None
        for i in range(32):
            G = grad(i)
            if i < 8:
                at = row16 + 16 * i - lane16 % 128
                part = jnp.where(at == 0, G, 0.0)
                part = part[:8] + part[8:]
                ends = part if ends is None else ends + part
                other = grad(32 + i)
                part = jnp.where(at == 0, other, 0.0)
                part = part[:8] + part[8:]
                final = part if final is None else final + part
                G = jnp.where(at > 0, G, other)
            gm_scr[16 * i : 16 * i + 16, :] = G
        ends = jnp.sum(ends, axis=0, keepdims=True)
        final = jnp.sum(final, axis=0, keepdims=True)
        final = jnp.concatenate([jnp.broadcast_to(final[:, :128], (64, 128)), jnp.broadcast_to(final[:, 128:], (64, 128))], axis=0)
        dqr_ref[p, :, 512:640] += kT_ref[p, :, tile(t + 4)].astype(f32) * final
        dkc_ref[p, tile(t + 4), :] += (qrtT_ref[p, :, 512:640].astype(f32) * final).T
        dv_ref[p, window(t), :] += dot(e_scr[held], (D2.astype(f32) * inv).astype(bf).T)
        for h in range(2):
            cols = slice(128 * h, 128 * h + 128)
            held = None
            for i, y in stream_rows(lambda i: gm_scr[8 * i : 8 * i + 8, cols], True, (1, 2, 4)):
                if i == 0:
                    y = y + jnp.where(row[:8] == 1, ends[:, cols], 0.0)
                if i % 2 == 1:
                    held = y
                else:
                    gu[8 * i : 8 * i + 16, cols] = jnp.concatenate([y, held], axis=0).astype(bf)

    def downstream(n, gb, gu):
        n = jnp.maximum(n, 0)
        p, t = n // nblk, n % nblk
        dqT = own_heads(dot(kT_ref[p, :, window(t)], gb[...]) + dot(krtT_ref[p], gu[...]))
        dq_ref[p, tile(t), :] = (SC * dqT).astype(bf).T
        Qm = tall_diagonal(q_ref[p, tile(t), :])
        dkc_ref[p, window(t), :] += dot(gb[...], Qm)
        dkr_ref[p] += dot(gu[...], Qm)

    def fetch(m):
        source = e_ref.at[m // half, pl.ds(2 * (m % half), 2)]
        return pltpu.make_async_copy(source, e_scr.at[pl.ds(2 * (m % 2), 2)], e_sem.at[m % 2])

    def body(m, slot, late):
        p = m // half
        fetch(m).wait()
        pl.when(m + 1 < items // 2)(lambda: fetch(m + 1).start())
        if late:
            kblocks(p - 1, per * (m % half), (1 - p % 2) * keys)
        downstream(2 * m - 1, gb1, gu1)
        upstream(2 * m, slot, gb0, gu0, 2 * (m % 2))
        downstream(2 * m, gb0, gu0)
        upstream(2 * m + 1, slot + 1, gb1, gu1, 2 * (m % 2) + 1)
        hook(m)
        following = slot + 2
        following = jnp.where(following == nblk, keys, following)
        return jnp.where(following == keys + nblk, 0, following)

    fetch(jnp.int32(0)).start()
    slot = lax.fori_loop(0, half, lambda m, slot: body(m, slot, False), jnp.int32(0))
    lax.fori_loop(half, items // 2, lambda m, slot: body(m, slot, True), slot)
    downstream(items - 1, gb1, gu1)

    def last(i, carry):
        kblocks(PAIRS - 1, per * i, ((PAIRS - 1) % 2) * keys)
        return carry

    lax.fori_loop(0, half, last, 0)


def vector(vec_ref, name):
    at, wide = vector_rows()[0][name]
    return jnp.concatenate([vec_ref[at + i : at + i + 1, :] for i in range(wide)], axis=1)


def put_vector(vec_ref, name, value):
    at, wide = vector_rows()[0][name]
    for i in range(wide):
        vec_ref[at + i : at + i + 1, :] = value[:, 128 * i : 128 * i + 128]


def add_vector(vec_ref, name, value):
    at, wide = vector_rows()[0][name]
    for i in range(wide):
        vec_ref[at + i : at + i + 1, :] += value[:, 128 * i : 128 * i + 128]


def normalized(values):
    centered = values - jnp.mean(values, axis=1, keepdims=True)
    inverse = lax.rsqrt(jnp.mean(centered * centered, axis=1, keepdims=True) + EPSILON)
    return centered * inverse, inverse


def norm_back(upstream, gain, unit, inverse):
    scaled = upstream * gain
    mean = jnp.mean(scaled, axis=1, keepdims=True)
    along = jnp.mean(scaled * unit, axis=1, keepdims=True)
    return inverse * (scaled - mean - unit * along)


def column_sum(values):
    return jnp.sum(values, axis=0, keepdims=True)


def reversal():
    row = lax.broadcasted_iota(jnp.int32, (128, 128), 0)
    lane = lax.broadcasted_iota(jnp.int32, (128, 128), 1)
    return (row + lane == 127).astype(bf)


def reversed_rows(values, JR):
    blocks = values.shape[0] // 128
    return jnp.concatenate([dot(JR, values[128 * b : 128 * b + 128]).astype(bf) for b in reversed(range(blocks))], axis=0)


def project_body(x_ref, query_w, key_w, value_w, table_ref, vec_ref, q_ref, qT_ref, k_ref, kT_ref, kTr_ref, v_ref, vT_ref, krt_ref, krtT_ref, qrt_ref, qrtT_ref, pos_ref):
    tokens = q_ref.shape[1]
    JR = reversal()
    lane = iotas(512, 128)[1]
    unit, _ = normalized(table_ref[...].astype(f32))
    pos = (unit * vector(vec_ref, N_REL_GAIN) + vector(vec_ref, N_REL_SHIFT)).astype(bf)
    pos = pltpu.roll(reversed_rows(pos, JR).astype(f32), 1, 0).astype(bf)
    pos_ref[...] = pos
    keys = dot(pos, key_w[...]) + vector(vec_ref, N_KEY_B)
    moved = pltpu.roll(keys, 1, 0).astype(bf)
    keys = keys.astype(bf)
    queries = (dot(pos, query_w[...]) + vector(vec_ref, N_QUERY_B)).astype(bf)
    for p in range(PAIRS):
        cols = slice(128 * p, 128 * p + 128)
        krt_ref[p] = keys[:, cols]
        krt_ref[PAIRS + p] = moved[:, cols]
        krtT_ref[p] = keys[:, cols].T
        qrtT_ref[p, :, 0:512] = queries[:, cols].T
        qrtT_ref[p, :, 512:640] = jnp.broadcast_to(queries[1:2, cols], (128, 128)).T
        zero = jnp.zeros((512, 128), bf)
        qrt_ref[p, 0:512, :] = jnp.where(lane < 64, queries[:, cols], zero)
        qrt_ref[p, 512:1024, :] = jnp.where(lane < 64, zero, queries[:, cols])
    bias = {name: vector(vec_ref, name) for name in (N_QUERY_B, N_KEY_B, N_VALUE_B)}

    def chunk(i, carry):
        rows = pl.ds(pl.multiple_of(i * 256, 256), 256)
        x = x_ref[rows, :]
        y = (dot(x, key_w[...]) + bias[N_KEY_B]).astype(bf)
        w = (dot(x, value_w[...]) + bias[N_VALUE_B]).astype(bf)
        for p in range(PAIRS):
            cols = slice(128 * p, 128 * p + 128)
            k_ref[p, rows, :] = y[:, cols]
            turned = y[:, cols].T
            kT_ref[p, :, rows] = turned
            kTr_ref[p, :, rows] = jnp.concatenate([dot(turned[:, :128], JR), dot(turned[:, 128:], JR)], axis=1).astype(bf)
            v_ref[p, rows, :] = w[:, cols]
            vT_ref[p, :, rows] = w[:, cols].T
        return carry

    lax.fori_loop(0, x_ref.shape[0] // 256, chunk, 0)

    def own(i, carry):
        rows = pl.ds(pl.multiple_of(i * 256, 256), 256)
        x = x_ref[pl.ds(pl.multiple_of(i * 256 + SPAN, 256), 256), :]
        y = (dot(x, query_w[...]) + bias[N_QUERY_B]).astype(bf)
        for p in range(PAIRS):
            q_ref[p, rows, :] = y[:, 128 * p : 128 * p + 128]
            qT_ref[p, :, rows] = y[:, 128 * p : 128 * p + 128].T
        return carry

    lax.fori_loop(0, tokens // 256, own, 0)


SQRT_HALF = 0.7071067811865476
PHI_SCALE = 0.3989422804014327


def gelu_and_slope(u):
    cdf = 0.5 + 0.5 * lax.erf(u * SQRT_HALF)
    return u * cdf, cdf + u * (PHI_SCALE * jnp.exp(-0.5 * u * u))


def feed_body(x_ref, ctx_ref, og_ref, output_w, up_w, down_w, vec_ref, out_ref, dz1_ref, dctx_ref, wide, dvec_ref,
              ml_scr, dup_scr, act_scr, ddown_scr, dattn_scr, slope_scr):
    tokens = out_ref.shape[0]
    dvec_ref[...] = jnp.zeros(dvec_ref.shape, f32)
    vecs = {name: vector(vec_ref, name) for name in (N_OUTPUT_B, N_ATTN_GAIN, N_ATTN_SHIFT, N_UP_BIAS, N_DOWN_BIAS, N_FFN_GAIN, N_FFN_SHIFT)}
    C = 256

    def chunk(i, carry):
        rows = pl.ds(pl.multiple_of(i * C, C), C)
        h = x_ref[pl.ds(pl.multiple_of(i * C + SPAN, C), C), :].astype(f32)
        z1 = h + dot(jnp.concatenate([ctx_ref[p, rows, :] for p in range(PAIRS)], axis=1), output_w[...]) + vecs[N_OUTPUT_B]
        unit1, inv1 = normalized(z1)
        mid = unit1 * vecs[N_ATTN_GAIN] + vecs[N_ATTN_SHIFT]
        ml = mid.astype(bf)
        ml_scr[rows, :] = ml
        z2 = mid + vecs[N_DOWN_BIAS]
        for f in range(FF // 256):
            cols = slice(256 * f, 256 * f + 256)
            up = dot(ml, up_w[:, cols]) + vecs[N_UP_BIAS][:, cols]
            act, slope = gelu_and_slope(up)
            act_scr[rows, cols] = act.astype(bf)
            slope_scr[:, cols] = slope
        z2 = z2 + dot(act_scr[rows, :], down_w[...])
        unit2, inv2 = normalized(z2)
        out_ref[rows, :] = (unit2 * vecs[N_FFN_GAIN] + vecs[N_FFN_SHIFT]).astype(bf)
        dh = og_ref[rows, :].astype(f32)
        add_vector(dvec_ref, N_FFN_GAIN, column_sum(dh * unit2))
        add_vector(dvec_ref, N_FFN_SHIFT, column_sum(dh))
        dz2 = norm_back(dh, vecs[N_FFN_GAIN], unit2, inv2)
        ddown = dz2.astype(bf)
        ddown_scr[rows, :] = ddown
        add_vector(dvec_ref, N_DOWN_BIAS, column_sum(ddown.astype(f32)))
        for f in range(FF // 256):
            cols = slice(256 * f, 256 * f + 256)
            dup = (dot(ddown, down_w[cols, :], NT) * slope_scr[:, cols]).astype(bf)
            dup_scr[rows, cols] = dup
        add_vector(dvec_ref, N_UP_BIAS, column_sum(dup_scr[rows, :].astype(f32)))
        dmid = dz2 + dot(dup_scr[rows, :], up_w[...], NT)
        add_vector(dvec_ref, N_ATTN_GAIN, column_sum(dmid * unit1))
        add_vector(dvec_ref, N_ATTN_SHIFT, column_sum(dmid))
        dz1 = norm_back(dmid, vecs[N_ATTN_GAIN], unit1, inv1)
        dz1_ref[rows, :] = dz1
        dattn = dz1.astype(bf)
        dattn_scr[rows, :] = dattn
        add_vector(dvec_ref, N_OUTPUT_B, column_sum(dattn.astype(f32)))
        dctx = dot(dattn, output_w[...], NT).astype(bf)
        for p in range(PAIRS):
            dctx_ref[p, :, rows] = dctx[:, 128 * p : 128 * p + 128].T
        return carry

    lax.fori_loop(0, tokens // C, chunk, 0)
    place = matrix_rows()

    def put(name, first, rows, value):
        base, _, pieces = place[name]
        for c in range(value.shape[1] // 128):
            wide[pl.ds(base - FEED_FIRST + pieces * first[0] + first[1] + c, rows, stride=pieces), :] = value[:, 128 * c : 128 * c + 128]

    ctx = jnp.concatenate([ctx_ref[p] for p in range(PAIRS)], axis=1)
    put(N_OUTPUT_W, (0, 0), D, dot(ctx, dattn_scr[...], TN))
    for f in range(FF // 256):
        cols = slice(256 * f, 256 * f + 256)
        put(N_UP_W, (0, 2 * f), D, dot(ml_scr[...], dup_scr[:, cols], TN))
        put(N_DOWN_W, (256 * f, 0), 256, dot(act_scr[:, cols], ddown_scr[...], TN))


def split(values):
    high = values.astype(bf)
    return high, (values - high.astype(f32)).astype(bf)


def dot2(left, right, dims=NN):
    if left.dtype == f32:
        return sum(dot(part, right, dims) for part in split(left))
    return sum(dot(left, part, dims) for part in split(right))


def tail_local(dq_ref, x_ref, query_w, dx_ref, dwq_ref, dvec_ref):
    tokens = dx_ref.shape[0]
    dq = jnp.concatenate([dq_ref[p] for p in range(PAIRS)], axis=1)
    dx_ref[...] += dot(dq, query_w[...], NT)
    dwq_ref[...] = dot(x_ref[...], dq, TN)
    put_vector(dvec_ref, N_QUERY_B, column_sum(dq.astype(f32)))


def tail_table(dkr_ref, dqr_ref, pos_ref, table_ref, vec_ref, query_w, key_w, dwq_ref, dwk_ref, dtable_ref, dvec_ref):
    JR = reversal()
    second = iotas(512, 128)[0] == 1
    tabs = {N_KEY_B: jnp.concatenate([SC * dkr_ref[p] for p in range(PAIRS)], axis=1)}
    parts = []
    for p in range(PAIRS):
        part = dqr_ref[p].T
        parts.append(SC * (part[:512] + jnp.where(second, column_sum(part[512:]), 0.0)))
    tabs[N_QUERY_B] = jnp.concatenate(parts, axis=1)
    dpos = None
    for w, dw, name in ((key_w, dwk_ref, N_KEY_B), (query_w, dwq_ref, N_QUERY_B)):
        tab = tabs[name]
        if name == N_KEY_B:
            dw[...] = dot2(pos_ref[...], tab, TN)
            put_vector(dvec_ref, name, column_sum(tab))
        else:
            dw[...] += dot2(pos_ref[...], tab, TN)
            add_vector(dvec_ref, name, column_sum(tab))
        part = dot2(tab, w[...], NT)
        dpos = part if dpos is None else dpos + part
    table = jnp.concatenate([dot(JR, table_ref[128 * b : 128 * b + 128, :]) for b in reversed(range(4))], axis=0)
    unit, inverse = normalized(pltpu.roll(table, 1, 0))
    put_vector(dvec_ref, N_REL_GAIN, column_sum(dpos * unit))
    put_vector(dvec_ref, N_REL_SHIFT, column_sum(dpos))
    dpos = pltpu.roll(norm_back(dpos, vector(vec_ref, N_REL_GAIN), unit, inverse), 511, 0).astype(bf)
    for b in range(4):
        dtable_ref[128 * b : 128 * b + 128, :] = dot(JR, dpos[128 * (3 - b) : 128 * (4 - b)])


def tail_keys(dkc_ref, dkp_ref, dv_ref, halo_ref, x_ref, key_w, value_w, dx_ref, dwk_ref, dwv_ref, dvec_ref):
    tokens = dx_ref.shape[0]
    x = x_ref[...]
    for which, (ref, w, dw, name) in enumerate(((None, key_w, dwk_ref, N_KEY_B), (dv_ref, value_w, dwv_ref, N_VALUE_B))):
        pieces = []
        for p in range(PAIRS):
            middle = slice(SPAN, SPAN + tokens)
            own = SC * (dkc_ref[p, middle, :] + dkp_ref[p, middle, :]) if ref is None else ref[p, middle, :]
            edge = [halo_ref[side, which, p].astype(f32) for side in (0, 1)]
            pieces.append(jnp.concatenate([own[:SPAN] + edge[0], own[SPAN : tokens - SPAN], own[tokens - SPAN :] + edge[1]], axis=0).astype(bf))
        d = jnp.concatenate(pieces, axis=1)
        dx_ref[...] += dot(d, w[...], NT)
        if name == N_KEY_B:
            dw[...] += dot(x, d, TN)
            add_vector(dvec_ref, name, column_sum(d.astype(f32)))
        else:
            dw[...] = dot(x, d, TN)
            put_vector(dvec_ref, name, column_sum(d.astype(f32)))


def beside(grid, step):
    return {"seq": lax.axis_index("seq") + step, "row": lax.axis_index("row")}


def seq_edges(grid):
    s = lax.axis_index("seq")
    return s > 0, s < grid.seq - 1


def enter_all(grid, p):
    sem = pltpu.get_barrier_semaphore()
    total = jnp.int32(0)
    before, after = seq_edges(grid)
    targets = [(grid.device(q), cond) for _, q, cond in neighbours_of(grid, p)]
    targets += [(beside(grid, -1), before), (beside(grid, 1), after)]
    for device, cond in targets:
        guarded(cond, lambda device=device: pl.semaphore_signal(sem, inc=1, device_id=device, device_id_type=MESH))
        total = total + (1 if cond is None else cond.astype(jnp.int32))
    pl.semaphore_wait(sem, total)


def remote(source, target, send_sem, recv_sem, device):
    return pltpu.make_async_remote_copy(
        src_ref=source, dst_ref=target, send_sem=send_sem, recv_sem=recv_sem, device_id=device, device_id_type=MESH)


def assemble(grid, shard, slots, wide, first, final):
    for k in range(grid.count):
        low, high = shard * k // GROUP, -(-shard * (k + 1) // GROUP)
        shared = k + 1 < grid.count and shard * (k + 1) % GROUP != 0
        begin = max(first, low + (1 if k > 0 and shard * k % GROUP != 0 else 0))
        end = min(final, high - (1 if shared else 0))
        if end > begin:
            wide[16 * (begin - first) : 16 * (end - first), :] = slots[k, 16 * (begin - low) : 16 * (end - low), :].astype(f32)
        if shared and first <= high - 1 < final:
            at = high - 1
            wide[16 * (at - first) : 16 * (at - first) + 16, :] = slots[k, 16 * (at - low) : 16 * (at - low) + 16, :].astype(f32) + slots[k + 1, 0:16, :].astype(f32)


def unpack(wide, first, outs):
    place = matrix_rows()
    for name, out in outs.items():
        base, rows, pieces = place[name]
        for c in range(pieces):
            out[:, 128 * c : 128 * c + 128] = wide[pl.ds(base - 16 * first + c, rows, stride=pieces), :].astype(bf)


VMEM = pl.BlockSpec(memory_space=pltpu.VMEM)
ANY = pl.BlockSpec(memory_space=pl.ANY)
FEED_FROM, FEED_TO = FEED_FIRST * 128, (FEED_FIRST + FEED_ROWS) * 128
LATE = (N_OUTPUT_W, N_UP_W, N_DOWN_W)


def projected(T):
    shape = jax.ShapeDtypeStruct
    E = T + 2 * SPAN
    natural = {N_Q: (T, 128), N_Q_TURNED: (128, T), N_K: (E, 128), N_K_TURNED: (128, E), N_K_TURNED_BACK: (128, E), N_V: (E, 128), N_V_TURNED: (128, E)}
    tables = {N_KRT: (512, 128), N_KRT_TURNED: (128, 512), N_QRT: (1024, 128), N_QRT_TURNED: (128, 640)}
    out = {name: shape((PAIRS,) + extent, bf) for name, extent in (natural | tables).items()}
    out[N_KRT] = shape((2 * PAIRS, 512, 128), bf)
    out[N_POS] = shape((512, D), bf)
    out[N_CTX] = shape((PAIRS, T, 128), bf)
    out[N_E] = shape((PAIRS, T // 128, 640, 256), bf)
    out[N_INV] = shape((PAIRS, T // 128, 8, 256), f32)
    return out


def front_outputs(T):
    shape = jax.ShapeDtypeStruct
    proj = projected(T)
    place = matrix_rows()
    out = {name: proj[name] for name in (N_Q, N_K_TURNED, N_K_TURNED_BACK, N_V, N_KRT_TURNED, N_QRT, N_QRT_TURNED, N_POS, N_E, N_INV)}
    for name in (N_QUERY_W, N_KEY_W, N_VALUE_W, N_REL_TABLE):
        out[name] = shape((place[name][1], 128 * place[name][2]), bf)
    out[N_VEC] = shape((vector_rows()[1], 128), f32)
    out[N_OUT] = shape((T, D), bf)
    out[N_DZ1] = shape((T, D), f32)
    out[N_DCTX_TURNED] = shape((PAIRS, 128, T), bf)
    out[N_DFLAT] = shape((FEED_ROWS, 128), bf)
    out[N_DVEC] = shape((vector_rows()[1], 128), f32)
    return out


def front_held(T):
    shape = jax.ShapeDtypeStruct
    proj = projected(T)
    place = matrix_rows()
    held = {name: proj[name] for name in (N_Q_TURNED, N_K, N_V_TURNED, N_KRT, N_CTX)}
    for name in LATE:
        held[name] = shape((place[name][1], 128 * place[name][2]), bf)
    held[N_X_EXT] = shape((T + 2 * SPAN, D), bf)
    held[N_SEG_EXT] = shape((8, T + 2 * SPAN), jnp.int32)
    return held


def front_kernel(grid, shard, slot_ref, x_ref, seg_ref, og_ref, *refs):
    tokens = x_ref.shape[0]
    blocks = tokens // 128
    outs, held = front_outputs(tokens), front_held(tokens)
    target = dict(zip(outs, refs))
    names = list(outs) + list(held)
    here = dict(zip(names, refs[len(outs) :]))
    slots, local_sem, out_sem, send_sem, recv_sem, halo_send, halo_recv = refs[len(outs) + len(names) :]
    p = grid.here()
    _, groups = shard_groups(shard, grid.count)
    before, after = seq_edges(grid)
    early = lambda k: jnp.logical_or(k * shard < FEED_FROM, (k + 1) * shard > FEED_TO)
    late = lambda k: jnp.logical_not(early(k))
    own = pltpu.make_async_copy(slot_ref, slots.at[grid.flat(p)] if grid.split else slots, local_sem)
    own.start()
    enter_all(grid, p)
    own.wait()
    x_ext, seg_ext = here[N_X_EXT], here[N_SEG_EXT]

    def halo_copies(side):
        step = -1 if side == 0 else 1
        take = pl.ds(0, SPAN) if side == 0 else pl.ds(tokens - SPAN, SPAN)
        land = pl.ds(tokens + SPAN, SPAN) if side == 0 else pl.ds(0, SPAN)
        return [
            remote(x_ref.at[take, :], x_ext.at[land, :], halo_send.at[side, 0], halo_recv.at[side, 0], beside(grid, step)),
            remote(seg_ref.at[:, take], seg_ext.at[:, land], halo_send.at[side, 1], halo_recv.at[side, 1], beside(grid, step)),
        ]

    def start(side):
        for copy in halo_copies(side):
            copy.start()

    def sent(side):
        for copy in halo_copies(side):
            copy.wait_send()

    def landed(side):
        for copy in halo_copies(side):
            copy.wait_recv()

    first_levels, first_partners, first_ends, levels, partners, ends = ([[]], [], [], [[]], [], [])
    if grid.split:
        gather = Gather(grid, p, slots, send_sem, recv_sem, groups)
        first_levels, first_partners, first_ends = gather.plan(early)
        levels, partners, ends = gather.plan(late)
    perform(first_levels[0])
    pl.when(before)(lambda: start(0))
    pl.when(after)(lambda: start(1))

    def clear(rows):
        x_ext[rows, :] = jnp.zeros((SPAN, D), bf)
        seg_ext[:, rows] = jnp.zeros((8, SPAN), jnp.int32)

    pl.when(jnp.logical_not(before))(lambda: clear(pl.ds(0, SPAN)))
    pl.when(jnp.logical_not(after))(lambda: clear(pl.ds(tokens + SPAN, SPAN)))
    x_ext[SPAN : SPAN + tokens, :] = x_ref[...]
    seg_ext[:, SPAN : SPAN + tokens] = seg_ref[...]
    for level in first_levels[1:]:
        perform(level)
    perform(first_partners)
    perform(first_ends)
    place = matrix_rows()
    feed_group, end_group = FEED_FIRST // 16, (FEED_FIRST + FEED_ROWS) // 16
    all_groups = flat_rows(shard, grid.count) // 16

    def first_part(wide):
        assemble(grid, shard, slots, wide, 0, feed_group)
        unpack(wide, 0, {name: here[name] for name in (N_QUERY_W, N_KEY_W, N_VALUE_W)})
        assemble(grid, shard, slots, wide, end_group, all_groups)
        unpack(wide, end_group, {N_REL_TABLE: here[N_REL_TABLE]})
        vec_at, vec_total = vector_rows()
        here[N_VEC][...] = jnp.zeros((vec_total, 128), f32)
        for name in VECTORS:
            base, _, pieces = place[name]
            at = base - 16 * end_group
            here[N_VEC][vec_at[name][0] : vec_at[name][0] + pieces, :] = wide[at : at + pieces, :]

    pl.run_scoped(first_part, pltpu.VMEM((16 * max(feed_group, all_groups - end_group), 128), f32))
    pl.when(before)(lambda: sent(0))
    pl.when(after)(lambda: sent(1))
    pl.when(after)(lambda: landed(0))
    pl.when(before)(lambda: landed(1))
    perform(levels[0])
    project_body(x_ext, *[here[n] for n in (N_QUERY_W, N_KEY_W, N_VALUE_W, N_REL_TABLE, N_VEC, N_Q, N_Q_TURNED, N_K, N_K_TURNED, N_K_TURNED_BACK, N_V, N_V_TURNED, N_KRT, N_KRT_TURNED, N_QRT, N_QRT_TURNED, N_POS)])

    def hook(m):
        for i, level in enumerate(levels[1:]):
            pl.when(m == 2 * i)(lambda level=level: perform(level))

    def attend(*scratch):
        att_fwd_body(blocks, *[here[n] for n in (N_Q_TURNED, N_K, N_V_TURNED, N_KRT, N_QRT_TURNED, N_SEG_EXT, N_CTX, N_E, N_INV)], *scratch, hook)

    pl.run_scoped(attend, pltpu.VMEM((2 * (blocks + 4), 2, 128, 640), bf), pltpu.VMEM((blocks, 640, 128), f32), *FORWARD_SCRATCH)
    leaving = {name: pltpu.make_async_copy(here[name], target[name], out_sem.at[i]) for i, name in enumerate(outs)}
    finished = (N_OUT, N_DZ1, N_DCTX_TURNED, N_DFLAT, N_DVEC)
    for name in outs:
        if name not in finished:
            leaving[name].start()
    perform(partners)
    perform(ends)

    def second_part(wide):
        assemble(grid, shard, slots, wide, feed_group, end_group)
        unpack(wide, feed_group, {name: here[name] for name in LATE})

    pl.run_scoped(second_part, pltpu.VMEM((FEED_ROWS, 128), f32))

    def feed_part(wide, *scratch):
        feed_body(*[x_ext, here[N_CTX], og_ref] + [here[n] for n in LATE + (N_VEC, N_OUT, N_DZ1, N_DCTX_TURNED)], wide, here[N_DVEC], *scratch)
        here[N_DFLAT][...] = wide[...].astype(bf)

    pl.run_scoped(
        feed_part, pltpu.VMEM((FEED_ROWS, 128), f32), pltpu.VMEM((tokens, D), bf), pltpu.VMEM((tokens, FF), bf), pltpu.VMEM((tokens, FF), bf),
        pltpu.VMEM((tokens, D), bf), pltpu.VMEM((tokens, D), bf), pltpu.VMEM((256, FF), f32))
    for name in finished:
        leaving[name].start()
    for name in outs:
        leaving[name].wait()


FORWARD_SCRATCH = (
    [pltpu.VMEM((640, 256), f32)] * 2 + [pltpu.VMEM((512, 256), f32)] * 2 + [pltpu.VMEM((640, 256), f32)] * 2 + [pltpu.VMEM((8, 256), f32)] * 2
)


def front(grid, shard, slot, x, seg, out_grad):
    tokens = x.shape[0]
    _, groups = shard_groups(shard, grid.count)
    outs, held = front_outputs(tokens), front_held(tokens)
    if not grid.split:
        slot = lax.all_gather(slot, ("seq", "row"))
    results = pl.pallas_call(
        functools.partial(front_kernel, grid, shard),
        out_shape=list(outs.values()),
        in_specs=[VMEM] * 4,
        out_specs=[ANY] * len(outs),
        scratch_shapes=[pltpu.VMEM(a.shape, a.dtype) for a in list(outs.values()) + list(held.values())]
        + [
            pltpu.VMEM((grid.count, 16 * groups, 128), bf),
            pltpu.SemaphoreType.DMA,
            pltpu.SemaphoreType.DMA((len(outs),)),
            pltpu.SemaphoreType.DMA((count_sends(grid, groups) if grid.split else 1,)),
            pltpu.SemaphoreType.DMA((len(orders_of(groups)), grid.count)),
            pltpu.SemaphoreType.DMA((2, 2)),
            pltpu.SemaphoreType.DMA((2, 2)),
        ],
        compiler_params=pltpu.CompilerParams(collective_id=0, has_side_effects=True, vmem_limit_bytes=62 << 20),
    )(slot, x, seg, out_grad)
    return dict(zip(outs, results))


def back_scratch(grid, shard, tokens):
    _, groups = shard_groups(shard, grid.count)
    rows = flat_rows(shard, grid.count)
    names, half, blocks = len(direction_names(grid)), (grid.count // 2 if grid.split else 1), tokens // 128
    square = pltpu.VMEM((D, D), bf)
    accumulator = pltpu.VMEM((PAIRS, tokens + 2 * SPAN, 128), f32)
    rim = pltpu.VMEM((2, 2, PAIRS, SPAN, 128), bf)
    return (
        [square, square, square, pltpu.VMEM((2 * SPAN, D), bf), pltpu.VMEM((512, D), bf), pltpu.VMEM((tokens, D), bf), pltpu.VMEM((tokens, D), f32)]
        + [pltpu.VMEM((PAIRS, tokens, 128), bf), accumulator, accumulator, accumulator, pltpu.VMEM((PAIRS, 512, 128), f32), pltpu.VMEM((PAIRS, 128, 640), f32)]
        + [pltpu.VMEM((2 * (blocks + 4), 2, 128, 640), bf), pltpu.VMEM((640, 256), f32), pltpu.VMEM((512, 256), f32)]
        + [pltpu.VMEM((640, 256), bf)] * 2 + [pltpu.VMEM((512, 256), bf)] * 2 + [pltpu.VMEM((4, 640, 256), bf), pltpu.SemaphoreType.DMA((2,))]
        + [pltpu.VMEM((D, D), f32)] * 3 + [pltpu.VMEM((2 * SPAN, D), f32), pltpu.VMEM((vector_rows()[1], 128), f32)]
        + [pltpu.VMEM((max(3 * D, rows - FEED_FIRST - FEED_ROWS), 128), f32), pltpu.VMEM((rows, 128), bf)]
        + [pltpu.VMEM((names, half, 16 * groups, 128), bf), pltpu.VMEM((16 * groups, 128), f32)]
        + [rim, rim, pltpu.SemaphoreType.DMA((8,)), pltpu.SemaphoreType.DMA((scatter_sends(grid, groups) if grid.split else 1,))]
        + [pltpu.SemaphoreType.DMA((len(orders_of(groups)), names, half)), pltpu.SemaphoreType.DMA((2,)), pltpu.SemaphoreType.DMA((2,))]
    )


def back_kernel(grid, shard, q_ref, kT_ref, kTr_ref, v_ref, krtT_ref, qrt_ref, qrtT_ref, dctxT_ref, e_ref, inv_ref, vec_ref, dvec_in, *refs):
    sources, (dx_out, sum_ref) = refs[:8], refs[8:10]
    query_w, key_w, value_w, table_ref, pos_ref, x_ref, dx_ref = refs[10:17]
    dq, dkc, dkp, dv, dkr, dqr = refs[17:23]
    work = refs[23:32]
    dwq, dwk, dwv, dtable, dvec_ref, wide, flat, kids, total, halo_out, halo_in, load_sem, send_sem, recv_sem, halo_send, halo_recv = refs[32:]
    p = grid.here()
    tokens = dx_ref.shape[0]
    blocks = tokens // 128
    _, groups = shard_groups(shard, grid.count)
    before, after = seq_edges(grid)
    feed = pl.ds(FEED_FIRST, FEED_ROWS)
    targets = (flat.at[feed, :], query_w, key_w, value_w, table_ref, pos_ref, x_ref, dx_ref)
    loads = [pltpu.make_async_copy(source, target, load_sem.at[i]) for i, (source, target) in enumerate(zip(sources, targets))]
    for load in loads:
        load.start()
    enter_all(grid, p)
    first_row = lambda k: (k * shard // GROUP) * 16
    early = lambda k: jnp.logical_and(first_row(k) >= FEED_FIRST, first_row(k) + 16 * groups <= FEED_FIRST + FEED_ROWS)
    gifts, levels, ends, last_gifts, last_levels, last_ends = ([], [], [], [], [], [])
    if grid.split:
        scatter = Scatter(grid, p, flat, first_row, kids, total, send_sem, recv_sem, groups)
        gifts, levels, ends = scatter.plan(sum_ref, early)
        last_gifts, last_levels, last_ends = scatter.plan(sum_ref, lambda k: jnp.logical_not(early(k)))
    loads[0].wait()
    perform(gifts)

    def hook(m):
        for i, level in enumerate(levels):
            pl.when(m == min(2 * i + 1, PAIRS * blocks // 2 - 1))(lambda level=level: perform(level))

    att_bwd_body(blocks, q_ref, kT_ref, kTr_ref, v_ref, krtT_ref, qrt_ref, qrtT_ref, dctxT_ref, e_ref, inv_ref, dq, dkc, dkp, dv, dkr, dqr, *work, hook)
    rims = (pl.ds(0, SPAN), pl.ds(tokens + SPAN, SPAN))
    for side in (0, 1):
        halo_out[side, 0] = (SC * (dkc[:, rims[side], :] + dkp[:, rims[side], :])).astype(bf)
        halo_out[side, 1] = dv[:, rims[side], :].astype(bf)

    def halo_copy(side):
        return remote(halo_out.at[side], halo_in.at[1 - side], halo_send.at[side], halo_recv.at[1 - side], beside(grid, -1 if side == 0 else 1))

    pl.when(before)(lambda: halo_copy(0).start())
    pl.when(after)(lambda: halo_copy(1).start())

    def clear(side):
        halo_in[side] = jnp.zeros(halo_in.shape[1:], bf)

    pl.when(jnp.logical_not(before))(lambda: clear(0))
    pl.when(jnp.logical_not(after))(lambda: clear(1))
    for load in loads[1:]:
        load.wait()
    dvec_ref[...] = dvec_in[...]
    tail_local(dq, x_ref, query_w, dx_ref, dwq, dvec_ref)
    tail_table(dkr, dqr, pos_ref, table_ref, vec_ref, query_w, key_w, dwq, dwk, dtable, dvec_ref)
    pl.when(before)(lambda: halo_copy(0).wait_send())
    pl.when(after)(lambda: halo_copy(1).wait_send())
    pl.when(before)(lambda: halo_copy(1).wait_recv())
    pl.when(after)(lambda: halo_copy(0).wait_recv())
    tail_keys(dkc, dkp, dv, halo_in, x_ref, key_w, value_w, dx_ref, dwk, dwv, dvec_ref)
    leave = pltpu.make_async_copy(dx_ref, dx_out, load_sem.at[0])
    leave.start()
    place = matrix_rows()
    vec_at, _ = vector_rows()
    final = FEED_FIRST + FEED_ROWS
    for name, ref in ((N_QUERY_W, dwq), (N_KEY_W, dwk), (N_VALUE_W, dwv)):
        base, rows, pieces = place[name]
        for c in range(pieces):
            wide[pl.ds(c, rows, stride=pieces), :] = ref[:, 128 * c : 128 * c + 128]
        flat[base : base + rows * pieces, :] = wide[0 : rows * pieces, :].astype(bf)
    rest = flat.shape[0] - final
    wide[0:rest, :] = jnp.zeros((rest, 128), f32)
    base, rows, pieces = place[N_REL_TABLE]
    for c in range(pieces):
        wide[pl.ds(base - final + c, rows, stride=pieces), :] = dtable[:, 128 * c : 128 * c + 128]
    for name in VECTORS:
        base, _, pieces = place[name]
        wide[base - final : base - final + pieces, :] = dvec_ref[vec_at[name][0] : vec_at[name][0] + pieces, :]
    flat[final:, :] = wide[0:rest, :].astype(bf)
    if not grid.split:
        sum_ref[...] = flat[...]
    perform(last_gifts)
    for level in last_levels:
        perform(level)
    perform(ends)
    perform(last_ends)
    leave.wait()


def back(grid, shard, f, x):
    _, groups = shard_groups(shard, grid.count)
    tokens = x.shape[0]
    shape = jax.ShapeDtypeStruct
    leaving = shape((16 * groups, 128), f32) if grid.split else shape((flat_rows(shard, grid.count), 128), bf)
    dx, summed = pl.pallas_call(
        functools.partial(back_kernel, grid, shard),
        out_shape=[shape((tokens, D), f32), leaving],
        in_specs=[VMEM] * 8 + [ANY] + [VMEM] * 3 + [ANY] * 8,
        out_specs=[ANY, VMEM],
        scratch_shapes=back_scratch(grid, shard, tokens),
        compiler_params=pltpu.CompilerParams(collective_id=1, has_side_effects=True, vmem_limit_bytes=62 << 20),
    )(
        *[f[n] for n in (N_Q, N_K_TURNED, N_K_TURNED_BACK, N_V, N_KRT_TURNED, N_QRT, N_QRT_TURNED, N_DCTX_TURNED, N_E, N_INV, N_VEC, N_DVEC)],
        *[f[n] for n in (N_DFLAT, N_QUERY_W, N_KEY_W, N_VALUE_W, N_REL_TABLE, N_POS)], x, f[N_DZ1])
    if not grid.split:
        first, _ = shard_groups(shard, grid.count)
        pieces = jnp.concatenate([summed[16 * at : 16 * (at + groups)] for at in first], axis=0)
        summed = lax.psum_scatter(pieces.astype(f32), ("seq", "row"), scatter_dimension=0, tiled=True)
    return dx, summed


def on_device(layer_input, segment_ids, out_grad, weights, momentum, average):
    tokens_here = layer_input.shape[1]
    grid = Grid(lax.axis_size("seq"), lax.axis_size("row"))
    shard = weights.shape[0]
    _, groups = shard_groups(shard, grid.count)
    shift = (lax.axis_index("seq") * grid.row + lax.axis_index("row")) * shard % GROUP
    slot = lax.dynamic_update_slice(jnp.zeros((GROUP * groups,), bf), weights.astype(bf), (shift,)).reshape(16 * groups, 128)
    seg = jnp.broadcast_to(segment_ids + 1, (8, tokens_here))
    f = front(grid, shard, slot, layer_input[0], seg, out_grad[0])
    block_output = f[N_OUT]
    dx, summed = back(grid, shard, f, layer_input[0])
    weight_grad = lax.dynamic_slice(summed.reshape(-1), (shift,), (shard,))
    all_tokens = tokens_here * grid.seq * layer_input.shape[0] * grid.row
    rate = 0.1 / math.sqrt(all_tokens)
    new_momentum = 0.5 * momentum + weight_grad
    new_weights = weights - rate * (weight_grad + 0.5 * new_momentum)
    new_average = 0.5 * average + 0.5 * new_weights
    return (
        block_output[None],
        dx[None],
        weight_grad,
        new_momentum,
        new_average,
        new_weights,
        new_weights.astype(jnp.bfloat16),
    )


def solution(mesh):
    flat = P(("seq", "row"))
    tokens = P("row", "seq", None)
    return jax.shard_map(
        on_device,
        mesh=mesh,
        in_specs=(tokens, P("row", "seq"), tokens, flat, flat, flat),
        out_specs=(tokens, tokens, flat, flat, flat, flat, flat),
        check_vma=False,
    )
```

```python
import functools
import itertools
import math

import jax
import jax.numpy as jnp
from jax import lax
from jax.experimental import pallas as pl
from jax.experimental.pallas import tpu as pltpu
from jax.sharding import PartitionSpec as P

D = 384
HEADS = 6
HEAD_DIM = 64
FF = 1536
SPAN = 256
PAIRS = HEADS // 2
NB = 5
EPSILON = 1e-07
(N_ATTN_GAIN, N_ATTN_SHIFT, N_CTX, N_DCTX_TURNED, N_DFLAT, N_DOWN_BIAS, N_DOWN_W, N_DVEC, N_DZ1, N_E, N_FFN_GAIN, N_FFN_SHIFT, N_INV, N_K, N_K_TURNED, N_K_TURNED_BACK, N_KEY_B, N_KEY_W, N_KRT, N_KRT_TURNED, N_OUT, N_OUTPUT_B, N_OUTPUT_W, N_POS, N_Q, N_Q_TURNED, N_QRT, N_QRT_TURNED, N_QUERY_B, N_QUERY_W, N_REL_GAIN, N_REL_SHIFT, N_REL_TABLE, N_SEG_EXT, N_UP_BIAS, N_UP_W, N_V, N_V_TURNED, N_VALUE_B, N_VALUE_W, N_VEC, N_X_EXT) = range(42)
bf = jnp.bfloat16
f32 = jnp.float32


MESH = pl.DeviceIdType.MESH
GROUP = 2048


class Grid:
    def __init__(self, seq, row):
        half = seq // 2
        wide = 1
        while wide * wide * 4 <= half:
            wide *= 2
        self.size = {"z": half // wide, "y": wide, "x": row}
        self.seq, self.row, self.count = seq, row, seq * row
        self.split = self.size["y"] == 2 and row == 2 and half > 4

    def here(self):
        s, x = lax.axis_index("seq"), lax.axis_index("row")
        y_size = self.size["y"]
        return {"z": s // (2 * y_size), "y": (s // 2) % y_size, "c": s % 2, "x": x}

    def seq_of(self, p):
        return (p["z"] * self.size["y"] + p["y"]) * 2 + p["c"]

    def flat(self, p):
        return self.seq_of(p) * self.row + p["x"]

    def device(self, p):
        return {"seq": self.seq_of(p), "row": p["x"]}

    def place(self, k):
        s, x = divmod(k, self.row)
        line, c = divmod(s, 2)
        z, y = divmod(line, self.size["y"])
        return z, y, c, x

    def plane(self, p):
        return (p["z"] * self.size["y"] + p["y"]) * self.row + p["x"]

    def offsets(self, order):
        choices = []
        for axis in order:
            n = self.size[axis]
            if n == 2:
                choices.append([0, "f"])
            else:
                choices.append([0] + [sign * d for d in range(1, n) for sign in (-1, 1)])
        hops = lambda off: sum(1 if o == "f" else abs(o) for o in off)
        return sorted(itertools.product(*choices), key=hops)


def both(conds):
    out = None
    for cond in conds:
        if cond is not None:
            out = cond if out is None else jnp.logical_and(out, cond)
    return out


def guarded(cond, fn):
    if cond is None:
        fn()
    else:
        pl.when(cond)(fn)


def source_of(grid, p, order, off):
    o, conds = dict(p), []
    for axis, d in zip(order, off):
        if d == "f":
            o[axis] = 1 - p[axis]
        elif d != 0:
            o[axis] = p[axis] + d
            conds.append(p[axis] + d >= 0 if d < 0 else p[axis] + d < grid.size[axis])
    return o, both(conds)


def parent_of(grid, p, order, off):
    last = max((i for i, d in enumerate(off) if d != 0), default=None)
    if last is None:
        return None, None
    q, axis, d = dict(p), order[last], off[last]
    if d == "f":
        q[axis] = 1 - p[axis]
        return q, axis + "0"
    q[axis] = p[axis] + (1 if d > 0 else -1)
    return q, axis + ("+" if d > 0 else "-")


def children_of(grid, p, order, off):
    last = max((i for i, d in enumerate(off) if d != 0), default=None)
    found = []
    if last is not None and off[last] != "f":
        axis, away = order[last], (-1 if off[last] > 0 else 1)
        q = dict(p)
        q[axis] = p[axis] + away
        found.append((axis + ("+" if away > 0 else "-"), q, p[axis] > 0 if away < 0 else p[axis] < grid.size[axis] - 1))
    for axis in order[0 if last is None else last + 1 :]:
        if grid.size[axis] == 2:
            q = dict(p)
            q[axis] = 1 - p[axis]
            found.append((axis + "0", q, None))
        elif grid.size[axis] > 2:
            for sign in (1, -1):
                q = dict(p)
                q[axis] = p[axis] + sign
                found.append((axis + ("+" if sign > 0 else "-"), q, p[axis] > 0 if sign < 0 else p[axis] < grid.size[axis] - 1))
    return found


def neighbours_of(grid, p):
    found = []
    for axis in ("z", "y", "x"):
        found += children_of(grid, p, (axis,), (0,))
    sibling = dict(p)
    sibling["c"] = 1 - p["c"]
    found.append(("c0", sibling, None))
    return found


def enter(grid, p, extra=()):
    sem = pltpu.get_barrier_semaphore()
    total = jnp.int32(0)
    for name, q, cond in neighbours_of(grid, p) + list(extra):
        guarded(cond, lambda q=q: pl.semaphore_signal(sem, inc=1, device_id=grid.device(q), device_id_type=MESH))
        total = total + (1 if cond is None else cond.astype(jnp.int32))
    pl.semaphore_wait(sem, total)


def parts_of(groups, whole):
    if whole:
        return ((("z", "y", "x"), 0, 16 * groups),)
    first = 16 * (groups // 2)
    return ((("z", "y", "x"), 0, first), (("x", "z", "y"), first, 16 * groups - first))


class Gather:
    def __init__(self, grid, p, slots, send_sem, recv_sem, groups):
        self.grid, self.p, self.slots = grid, p, slots
        self.send_sem, self.recv_sem, self.groups = send_sem, recv_sem, groups
        self.sends, self.used = [], 0

    def block(self, o, start, rows):
        return self.slots.at[o["z"], o["y"], o["c"], o["x"], pl.ds(start, rows), :]

    def copy(self, part, start, rows, o, q, index):
        block, k = self.block(o, start, rows), self.grid.flat(o)
        return pltpu.make_async_remote_copy(
            src_ref=block, dst_ref=block, send_sem=self.send_sem.at[index], recv_sem=self.recv_sem.at[part, k],
            device_id=self.grid.device(q), device_id_type=MESH)

    def arrived(self, part, start, rows, o):
        block, k = self.block(o, start, rows), self.grid.flat(o)
        pltpu.make_async_remote_copy(
            src_ref=block, dst_ref=block, send_sem=self.send_sem.at[0], recv_sem=self.recv_sem.at[part, k],
            device_id=self.grid.device(self.p), device_id_type=MESH).wait_recv()

    def plan(self, chosen, whole, used):
        grid, p = self.grid, self.p
        sibling = dict(p)
        sibling["c"] = 1 - p["c"]
        levels, ends, partners = {}, [], []
        for part, (order, start, rows) in enumerate(parts_of(self.groups, whole)):
            for off in grid.offsets(order):
                hops = sum(1 if o == "f" else abs(o) for o in off)
                o, cond = source_of(grid, p, order, off)
                k = grid.flat(o)
                targets = children_of(grid, p, order, off) + [("c0", sibling, None)]
                indices = [used + i for i in range(len(targets))]
                used += len(targets)
                cond = both([cond, chosen(o)])

                def step(what=(part, start, rows, o), targets=targets, indices=indices, own=hops == 0):
                    if not own:
                        self.arrived(*what)
                    for (name, q, when), index in zip(targets, indices):
                        guarded(when, lambda q=q, index=index: self.copy(*what, q, index).start())

                def end(what=(part, start, rows, o), targets=targets, indices=indices):
                    for (name, q, when), index in zip(targets, indices):
                        guarded(when, lambda q=q, index=index: self.copy(*what, q, index).wait_send())

                levels.setdefault(hops, []).append((cond, step))
                ends.append((cond, end))
                o, cond = source_of(grid, sibling, order, off)
                k = grid.flat(o)
                partners.append((both([cond, chosen(o)]), lambda what=(part, start, rows, o): self.arrived(*what)))
        return [levels[h] for h in sorted(levels)], partners, ends


def perform(steps):
    for cond, step in steps:
        guarded(cond, step)


def count_sends(grid, groups, whole):
    fake = {"z": jnp.int32(0), "y": jnp.int32(0), "x": jnp.int32(0), "c": jnp.int32(0)}
    return sum(len(children_of(grid, fake, order, off)) + 1 for order, _, _ in parts_of(groups, whole) for off in grid.offsets(order))


OPPOSITE = {"+": "-", "-": "+", "0": "0"}


def direction_names(grid):
    names = ["c0"]
    for axis in ("z", "y", "x"):
        if grid.size[axis] == 2:
            names.append(axis + "0")
        elif grid.size[axis] > 2:
            names += [axis + "+", axis + "-"]
    return names


class Scatter:
    def __init__(self, grid, p, flat, first_row, kids, total, send_sem, recv_sem, groups):
        self.grid, self.p, self.flat, self.first_row = grid, p, flat, first_row
        self.kids, self.total = kids, total
        self.send_sem, self.recv_sem, self.groups = send_sem, recv_sem, groups
        self.names = direction_names(grid)

    def incoming(self, part, name, place):
        start, rows = self.spans[part]
        return self.kids.at[self.names.index(name), place, pl.ds(start, rows), :]

    def transfer(self, source, part, name, place, q, send):
        return pltpu.make_async_remote_copy(
            src_ref=source, dst_ref=self.incoming(part, name, place), send_sem=self.send_sem.at[send],
            recv_sem=self.recv_sem.at[part, self.names.index(name), place], device_id=self.grid.device(q), device_id_type=MESH)

    def arrived(self, part, name, place):
        block = self.incoming(part, name, place)
        pltpu.make_async_remote_copy(
            src_ref=block, dst_ref=block, send_sem=self.send_sem.at[0],
            recv_sem=self.recv_sem.at[part, self.names.index(name), place],
            device_id=self.grid.device(self.p), device_id_type=MESH).wait_recv()

    def plan(self, result, chosen, whole, used):
        grid, p = self.grid, self.p
        sibling = dict(p)
        sibling["c"] = 1 - p["c"]
        gifts, levels, ends = [], {}, []
        self.spans = [part[1:] for part in parts_of(self.groups, whole)]
        for part, (order, start, rows) in enumerate(parts_of(self.groups, whole)):
            for off in sorted(grid.offsets(order), key=lambda off: -sum(1 if o == "f" else abs(o) for o in off)):
                hops = sum(1 if o == "f" else abs(o) for o in off)
                o, cond = source_of(grid, sibling, order, off)
                cond = both([cond, chosen(grid.flat(o))])

                def give(part=part, o=o, index=used, start=start, rows=rows):
                    block = self.flat.at[pl.ds(pl.multiple_of(self.first_row(grid.flat(o)) + start, 16), rows), :]
                    return self.transfer(block, part, "c0", grid.plane(o), sibling, index)

                gifts.append((cond, lambda give=give: give().start()))
                ends.append((cond, lambda give=give: give().wait_send()))
                used += 1
                o, cond = source_of(grid, p, order, off)
                place, k = grid.plane(o), grid.flat(o)
                cond = both([cond, chosen(k)])
                kids = children_of(grid, p, order, off)
                parent, side = parent_of(grid, p, order, off)

                def push(part=part, place=place, parent=parent, side=side, index=used, start=start, rows=rows):
                    return self.transfer(self.incoming(part, "c0", place), part, side[0] + OPPOSITE[side[1]], place, parent, index)

                def step(part=part, place=place, k=k, kids=kids, parent=parent, start=start, rows=rows, push=push):
                    self.arrived(part, "c0", place)
                    mine = self.flat[pl.ds(pl.multiple_of(self.first_row(k) + start, 16), rows), :].astype(f32)
                    self.total[0:rows, :] = mine + self.incoming(part, "c0", place)[...].astype(f32)
                    for name, q, when in kids:

                        def add(name=name):
                            self.arrived(part, name, place)
                            self.total[0:rows, :] += self.incoming(part, name, place)[...].astype(f32)

                        guarded(when, add)
                    if parent is None:
                        result[pl.ds(start, rows), :] = self.total[0:rows, :]
                    else:
                        self.kids[0, place, pl.ds(start, rows), :] = self.total[0:rows, :].astype(bf)
                        push().start()

                levels.setdefault(-hops, []).append((cond, step))
                if parent is not None:
                    ends.append((cond, lambda push=push: push().wait_send()))
                    used += 1
        return gifts, [levels[h] for h in sorted(levels)], ends


def scatter_sends(grid, groups, whole):
    return 2 * sum(len(grid.offsets(order)) for order, _, _ in parts_of(groups, whole))


def shard_groups(shard, count):
    first = [shard * k // GROUP for k in range(count)]
    groups = max(-(-shard * (k + 1) // GROUP) - first[k] for k in range(count))
    return first, max(groups, 2)


def flat_rows(shard, count):
    first, groups = shard_groups(shard, count)
    return 16 * (first[-1] + groups)


def layer_pieces():
    square, vector_of = (D, D), (D,)
    return (
        (N_QUERY_W, square), (N_KEY_W, square), (N_VALUE_W, square), (N_OUTPUT_W, square), (N_UP_W, (D, FF)), (N_DOWN_W, (FF, D)),
        (N_QUERY_B, vector_of), (N_KEY_B, vector_of), (N_VALUE_B, vector_of), (N_OUTPUT_B, vector_of), (N_ATTN_GAIN, vector_of),
        (N_ATTN_SHIFT, vector_of), (N_UP_BIAS, (FF,)), (N_DOWN_BIAS, vector_of), (N_FFN_GAIN, vector_of), (N_FFN_SHIFT, vector_of),
        (N_REL_TABLE, (2 * SPAN, D)), (N_REL_GAIN, vector_of), (N_REL_SHIFT, vector_of),
    )


def matrix_rows():
    place, at = {}, 0
    for name, extent in layer_pieces():
        if len(extent) == 2:
            place[name] = (at // 128, extent[0], extent[1] // 128)
        else:
            place[name] = (at // 128, 1, extent[0] // 128)
        at += math.prod(extent)
    return place


MATRICES = (N_QUERY_W, N_KEY_W, N_VALUE_W, N_OUTPUT_W, N_UP_W, N_DOWN_W, N_REL_TABLE)
VECTORS = tuple(name for name, extent in layer_pieces() if len(extent) == 1)
FEED_FIRST = matrix_rows()[N_OUTPUT_W][0]
FEED_ROWS = matrix_rows()[N_QUERY_B][0] - FEED_FIRST
USED_ROWS = sum(rows * pieces for _, rows, pieces in matrix_rows().values())


def vector_rows():
    place, at = {}, 0
    for name in VECTORS:
        wide = matrix_rows()[name][2]
        place[name] = (at, wide)
        at += wide
    return place, -(-at // 8) * 8


SC = 1.0 / math.sqrt(3.0 * HEAD_DIM)
LOG2E = 1.4426950408889634
NT = (((1,), (1,)), ((), ()))
NN = (((1,), (0,)), ((), ()))
TN = (((0,), (0,)), ((), ()))


def dot(a, b, dims=NN):
    return lax.dot_general(a, b, dims, preferred_element_type=f32)


def iotas(rows, lanes):
    return lax.broadcasted_iota(jnp.int32, (rows, lanes), 0), lax.broadcasted_iota(jnp.int32, (rows, lanes), 1)


def tile(i):
    return pl.ds(pl.multiple_of(i * 128, 128), 128)


def window(i):
    return pl.ds(pl.multiple_of(i * 128, 128), NB * 128)


def wide_diagonal(columns):
    zero = jnp.zeros((64, 128), columns.dtype)
    return jnp.concatenate([jnp.concatenate([columns[:64], zero], axis=1), jnp.concatenate([zero, columns[64:]], axis=1)], axis=0)


def tall_diagonal(rows):
    lane = iotas(128, 128)[1]
    zero = jnp.zeros_like(rows)
    return jnp.concatenate([jnp.where(lane < 64, rows, zero), jnp.where(lane >= 64, rows, zero)], axis=0)


def own_heads(wide):
    return jnp.concatenate([wide[:64, :128], wide[64:, 128:]], axis=0)


def turn_rows(values, back):
    size = values.shape[0]
    lane = iotas(*values.shape)[1]
    for step in (64, 32, 16, 8, 4, 2, 1):
        moved = pltpu.roll(values, size - step if back else step, 0)
        values = jnp.where(lane & step != 0, moved, values)
    return values


def turn_lanes(values, first):
    return jnp.concatenate([pltpu.roll(values[8 * g : 8 * g + 8, :512], first + 8 * g, 1, stride=1, stride_axis=0) for g in range(16)], axis=0)


def stream_rows(load, up, fine):
    row, lane = iotas(8, 128)
    inner = [(step, lane & step != 0, row < step if not up else row >= 8 - step) for step in fine]
    masks = [lane & step != 0 for step in (8, 16, 32, 64)]
    turned = [None for _ in inner]
    past = [[] for _ in masks]
    extra = 15 + len(inner)
    order = list(range(64 - extra, 64)) + list(range(64)) if not up else list(reversed(list(range(64)) + list(range(extra))))
    for n, i in enumerate(order):
        value = load(i)
        for level, (step, mask, edge) in enumerate(inner):
            now = pltpu.roll(value, step if not up else 8 - step, 0)
            if turned[level] is not None:
                value = jnp.where(mask, jnp.where(edge, turned[level], now), value)
            turned[level] = now
        for level, mask in enumerate(masks):
            past[level].append(value)
            if len(past[level]) > 1 << level:
                value = jnp.where(mask, past[level].pop(0), value)
        if n >= extra:
            yield i, value


def att_fwd_body(nblk, qT_ref, k_ref, vT_ref, krt_ref, qrtT_ref, seg_ref, ctx_ref, p_ref, inv_ref, x_scr, bias_scr, s0, s1, z0, z1, t0, t1, m0, m1, hook=None):
    row, lane = iotas(128, 128)
    lane2 = iotas(128, 256)[1]
    lane512 = iotas(512, 256)[1]
    items, keys = PAIRS * nblk, nblk + 4

    def mk_bias(t, carry):
        sq = seg_ref[0:1, tile(t + 2)].astype(f32)
        for b in range(NB):
            sk = jnp.broadcast_to(seg_ref[0:1, tile(t + b)], (128, 128)).astype(f32).T
            ok = sk == sq
            if b == 0:
                ok = ok & (row >= lane)
            if b == NB - 1:
                ok = ok & (row <= lane)
            bias_scr[t, 128 * b : 128 * b + 128, :] = jnp.where(ok, 0.0, -1e30).astype(f32)
        return carry

    lax.fori_loop(0, nblk, mk_bias, 0)

    def keyside(p, J, slot):
        C = dot(tall_diagonal(k_ref[p, tile(J), :]), qrtT_ref[p])
        for h in range(2):
            Ch = C[128 * h : 128 * h + 128]
            R = turn_lanes(Ch, 0)
            x_scr[slot, h, :, 0:128] = jnp.where(lane > row, R[:, :128], Ch[:, 512:]).astype(bf)
            x_scr[slot, h, :, 128:512] = R[:, 128:].astype(bf)
            x_scr[slot, h, :, 512:640] = R[:, :128].astype(bf)

    def start(J, carry):
        keyside(0, J, J)
        return carry

    lax.fori_loop(0, keys, start, 0)

    def scores(n, s_scr, z_scr, t_scr, m_scr):
        n = jnp.minimum(n, items - 1)
        p, t = n // nblk, n % nblk
        base = (p % 2) * keys + t
        Q2 = wide_diagonal(qT_ref[p, :, tile(t)])
        odd = lane2 % 2 == 1
        zero = jnp.zeros_like(Q2)
        table = krt_ref[p]
        moved = krt_ref[PAIRS + p]
        Z = dot(jnp.concatenate([table, moved], axis=1), jnp.concatenate([jnp.where(odd, zero, Q2), jnp.where(odd, Q2, zero)], axis=0))
        ends = jnp.where(odd[:1], Z[2:3], Z[1:2])
        z_scr[...] = Z
        s_scr[...] = dot(k_ref[p, window(t), :], Q2)
        for h in range(2):
            cols = slice(128 * h, 128 * h + 128)

            def load(i):
                return z_scr[8 * i : 8 * i + 8, cols]

            end = ends[:, cols]
            top = None
            held = None
            for i, y in stream_rows(load, False, (2, 4)):
                if i % 2 == 0:
                    held = y
                    continue
                at, b = 8 * (i - 1), i // 16
                y = jnp.concatenate([held, y], axis=0)
                for block in (0, 4) if b == 0 else (b,):
                    r = at + 128 * (block - b)
                    rows = slice(r, r + 16)
                    inner = slice(at % 128, at % 128 + 16)
                    x = x_scr[base + block, h, inner, 128 * (4 - block) : 128 * (5 - block)].astype(f32)
                    part = y
                    if block == 0:
                        part = jnp.where(iotas(16, 128)[0] + at > iotas(16, 128)[1], y, end)
                    T = s_scr[rows, cols] + bias_scr[t, rows, :] + part + x
                    t_scr[rows, cols] = T
                    most = jnp.maximum(T[:8], T[8:])
                    top = most if top is None else jnp.maximum(top, most)
            m_scr[:, cols] = top

    def soft(n, t_scr, m_scr):
        n = jnp.clip(n, 0, items - 1)
        m = jnp.max(m_scr[...], axis=0, keepdims=True)
        total = None
        for i in range(40):
            e = jnp.exp2((t_scr[16 * i : 16 * i + 16, :] - m) * (SC * LOG2E))
            part = e[:8] + e[8:]
            total = part if total is None else total + part
            p_ref[n // nblk, n % nblk, 16 * i : 16 * i + 16, :] = e.astype(bf)
        inv_ref[n // nblk, n % nblk] = jnp.broadcast_to(1.0 / jnp.sum(total, axis=0, keepdims=True), (8, 256))

    def context(n):
        n = jnp.clip(n, 0, items - 1)
        p, t = n // nblk, n % nblk
        ctxT = own_heads(dot(vT_ref[p, :, window(t)], p_ref[p, t]) * inv_ref[p, t, 0:1, :])
        ctx_ref[p, tile(t), :] = ctxT.astype(bf).T

    half = nblk // 2
    per = keys // half

    def body(m, slot):
        context(2 * m - 2)
        soft(2 * m - 1, t1, m1)
        scores(2 * m, s0, z0, t0, m0)
        context(2 * m - 1)
        soft(2 * m, t0, m0)
        scores(2 * m + 1, s1, z1, t1, m1)
        p, first = jnp.minimum(m // half + 1, PAIRS - 1), per * (m % half)
        for i in range(per):
            keyside(p, first + i, slot + i)
        if hook is not None:
            hook(m)
        return jnp.where(slot + per == 2 * keys, 0, slot + per)

    lax.fori_loop(0, items // 2 + 1, body, jnp.int32(keys))


def unreversed(values, JR):
    high = values.astype(bf)
    low = (values - high.astype(f32)).astype(bf)
    both = dot(JR, jnp.concatenate([high, low], axis=1))
    return both[:, :128] + both[:, 128:]


def att_bwd_body(nblk, q_ref, kT_ref, kTr_ref, v_ref, krtT_ref, qrt_ref, qrtT_ref, dctxT_ref, e_ref, inv_ref, dq_ref, dkc_ref, dkp_ref, dv_ref, dkr_ref, dqr_ref,
                 gt_scr, dp_scr, gm_scr, gb0, gb1, gu0, gu1, e_scr, e_sem, hook):
    row, lane = iotas(128, 128)
    row16, lane16 = iotas(16, 256)
    JR = (row + lane == 127).astype(bf)
    zero = jnp.zeros((128, 128), bf)
    items, keys, half = PAIRS * nblk, nblk + 4, nblk // 2
    per = keys // half
    gt_scr[...] = jnp.zeros(gt_scr.shape, bf)
    gb1[...] = jnp.zeros(gb1.shape, bf)
    gu1[...] = jnp.zeros(gu1.shape, bf)
    for ref in (dkc_ref, dv_ref, dkr_ref, dqr_ref):
        ref[...] = jnp.zeros(ref.shape, f32)

    def kblocks(p, first, base):
        turned = [[], []]
        for i in range(per):
            for h in range(2):
                GT = gt_scr[base + first + i, h]
                Gm = jnp.concatenate([jnp.where(lane > row, GT[:, :128], GT[:, 512:]), GT[:, 128:512]], axis=1)
                turned[h].append(turn_lanes(dot(JR, Gm), 385).astype(bf))
        stacked = [jnp.concatenate(part, axis=0) for part in turned]
        dk = dot(jnp.concatenate(stacked, axis=1), qrt_ref[p])
        for i in range(per):
            dkp_ref[p, tile(first + i), :] = unreversed(dk[128 * i : 128 * i + 128], JR)
        span = pl.ds(pl.multiple_of(first * 128, 128), 128 * per)
        for h in range(2):
            heads = slice(64 * h, 64 * h + 64)
            dqr_ref[p, heads, 0:512] += dot(kTr_ref[p, heads, span], stacked[h])

    def upstream(n, slot, gb, gu, held):
        p, t = n // nblk, n % nblk
        D2 = wide_diagonal(dctxT_ref[p, :, tile(t)])
        inv = inv_ref[p, t, 0:1, :]
        dp_scr[...] = dot(v_ref[p, window(t), :], D2)
        total = None
        for i in range(40):
            rows = slice(16 * i, 16 * i + 16)
            w = e_scr[held, rows, :].astype(f32) * dp_scr[rows, :]
            part = w[:8] + w[8:]
            total = part if total is None else total + part
        less = jnp.sum(total, axis=0, keepdims=True) * inv * inv

        def grad(i):
            rows = slice(16 * i, 16 * i + 16)
            G = e_scr[held, rows, :].astype(f32) * (dp_scr[rows, :] * inv - less)
            Gb = G.astype(bf)
            gb[rows, :] = Gb
            b = i // 8
            for h in range(2):
                gt_scr[slot + b, h, 16 * (i % 8) : 16 * (i % 8) + 16, 128 * (4 - b) : 128 * (5 - b)] = Gb[:, 128 * h : 128 * h + 128]
            return G

        ends = None
        final = None
        for i in range(32):
            G = grad(i)
            if i < 8:
                at = row16 + 16 * i - lane16 % 128
                part = jnp.where(at == 0, G, 0.0)
                part = part[:8] + part[8:]
                ends = part if ends is None else ends + part
                other = grad(32 + i)
                part = jnp.where(at == 0, other, 0.0)
                part = part[:8] + part[8:]
                final = part if final is None else final + part
                G = jnp.where(at > 0, G, other)
            gm_scr[16 * i : 16 * i + 16, :] = G
        ends = jnp.sum(ends, axis=0, keepdims=True)
        final = jnp.sum(final, axis=0, keepdims=True)
        final = jnp.concatenate([jnp.broadcast_to(final[:, :128], (64, 128)), jnp.broadcast_to(final[:, 128:], (64, 128))], axis=0)
        dqr_ref[p, :, 512:640] += kT_ref[p, :, tile(t + 4)].astype(f32) * final
        dkc_ref[p, tile(t + 4), :] += (qrtT_ref[p, :, 512:640].astype(f32) * final).T
        dv_ref[p, window(t), :] += dot(e_scr[held], (D2.astype(f32) * inv).astype(bf).T)
        for h in range(2):
            cols = slice(128 * h, 128 * h + 128)
            held = None
            for i, y in stream_rows(lambda i: gm_scr[8 * i : 8 * i + 8, cols], True, (1, 2, 4)):
                if i == 0:
                    y = y + jnp.where(row[:8] == 1, ends[:, cols], 0.0)
                if i % 2 == 1:
                    held = y
                else:
                    gu[8 * i : 8 * i + 16, cols] = jnp.concatenate([y, held], axis=0).astype(bf)

    def downstream(n, gb, gu):
        n = jnp.maximum(n, 0)
        p, t = n // nblk, n % nblk
        dqT = own_heads(dot(kT_ref[p, :, window(t)], gb[...]) + dot(krtT_ref[p], gu[...]))
        dq_ref[p, tile(t), :] = (SC * dqT).astype(bf).T
        Qm = tall_diagonal(q_ref[p, tile(t), :])
        dkc_ref[p, window(t), :] += dot(gb[...], Qm)
        dkr_ref[p] += dot(gu[...], Qm)

    def fetch(m):
        source = e_ref.at[m // half, pl.ds(2 * (m % half), 2)]
        return pltpu.make_async_copy(source, e_scr.at[pl.ds(2 * (m % 2), 2)], e_sem.at[m % 2])

    def body(m, slot, late):
        p = m // half
        fetch(m).wait()
        pl.when(m + 1 < items // 2)(lambda: fetch(m + 1).start())
        if late:
            kblocks(p - 1, per * (m % half), (1 - p % 2) * keys)
        downstream(2 * m - 1, gb1, gu1)
        upstream(2 * m, slot, gb0, gu0, 2 * (m % 2))
        downstream(2 * m, gb0, gu0)
        upstream(2 * m + 1, slot + 1, gb1, gu1, 2 * (m % 2) + 1)
        hook(m)
        following = slot + 2
        following = jnp.where(following == nblk, keys, following)
        return jnp.where(following == keys + nblk, 0, following)

    fetch(jnp.int32(0)).start()
    slot = lax.fori_loop(0, half, lambda m, slot: body(m, slot, False), jnp.int32(0))
    lax.fori_loop(half, items // 2, lambda m, slot: body(m, slot, True), slot)
    downstream(items - 1, gb1, gu1)

    def last(i, carry):
        kblocks(PAIRS - 1, per * i, ((PAIRS - 1) % 2) * keys)
        return carry

    lax.fori_loop(0, half, last, 0)


def vector(vec_ref, name):
    at, wide = vector_rows()[0][name]
    return jnp.concatenate([vec_ref[at + i : at + i + 1, :] for i in range(wide)], axis=1)


def put_vector(vec_ref, name, value):
    at, wide = vector_rows()[0][name]
    for i in range(wide):
        vec_ref[at + i : at + i + 1, :] = value[:, 128 * i : 128 * i + 128]


def add_vector(vec_ref, name, value):
    at, wide = vector_rows()[0][name]
    for i in range(wide):
        vec_ref[at + i : at + i + 1, :] += value[:, 128 * i : 128 * i + 128]


def normalized(values):
    centered = values - jnp.mean(values, axis=1, keepdims=True)
    inverse = lax.rsqrt(jnp.mean(centered * centered, axis=1, keepdims=True) + EPSILON)
    return centered * inverse, inverse


def norm_back(upstream, gain, unit, inverse):
    scaled = upstream * gain
    mean = jnp.mean(scaled, axis=1, keepdims=True)
    along = jnp.mean(scaled * unit, axis=1, keepdims=True)
    return inverse * (scaled - mean - unit * along)


def column_sum(values):
    return jnp.sum(values, axis=0, keepdims=True)


def reversal():
    row = lax.broadcasted_iota(jnp.int32, (128, 128), 0)
    lane = lax.broadcasted_iota(jnp.int32, (128, 128), 1)
    return (row + lane == 127).astype(bf)


def reversed_rows(values, JR):
    blocks = values.shape[0] // 128
    return jnp.concatenate([dot(JR, values[128 * b : 128 * b + 128]).astype(bf) for b in reversed(range(blocks))], axis=0)


def project_body(x_ref, query_w, key_w, value_w, table_ref, vec_ref, q_ref, qT_ref, k_ref, kT_ref, kTr_ref, v_ref, vT_ref, krt_ref, krtT_ref, qrt_ref, qrtT_ref, pos_ref):
    tokens = q_ref.shape[1]
    JR = reversal()
    lane = iotas(512, 128)[1]
    unit, _ = normalized(table_ref[...].astype(f32))
    pos = (unit * vector(vec_ref, N_REL_GAIN) + vector(vec_ref, N_REL_SHIFT)).astype(bf)
    pos = pltpu.roll(reversed_rows(pos, JR).astype(f32), 1, 0).astype(bf)
    pos_ref[...] = pos
    keys = dot(pos, key_w[...]) + vector(vec_ref, N_KEY_B)
    moved = pltpu.roll(keys, 1, 0).astype(bf)
    keys = keys.astype(bf)
    queries = (dot(pos, query_w[...]) + vector(vec_ref, N_QUERY_B)).astype(bf)
    for p in range(PAIRS):
        cols = slice(128 * p, 128 * p + 128)
        krt_ref[p] = keys[:, cols]
        krt_ref[PAIRS + p] = moved[:, cols]
        krtT_ref[p] = keys[:, cols].T
        qrtT_ref[p, :, 0:512] = queries[:, cols].T
        qrtT_ref[p, :, 512:640] = jnp.broadcast_to(queries[1:2, cols], (128, 128)).T
        zero = jnp.zeros((512, 128), bf)
        qrt_ref[p, 0:512, :] = jnp.where(lane < 64, queries[:, cols], zero)
        qrt_ref[p, 512:1024, :] = jnp.where(lane < 64, zero, queries[:, cols])
    bias = {name: vector(vec_ref, name) for name in (N_QUERY_B, N_KEY_B, N_VALUE_B)}

    def chunk(i, carry):
        rows = pl.ds(pl.multiple_of(i * 256, 256), 256)
        x = x_ref[rows, :]
        y = (dot(x, key_w[...]) + bias[N_KEY_B]).astype(bf)
        w = (dot(x, value_w[...]) + bias[N_VALUE_B]).astype(bf)
        for p in range(PAIRS):
            cols = slice(128 * p, 128 * p + 128)
            k_ref[p, rows, :] = y[:, cols]
            turned = y[:, cols].T
            kT_ref[p, :, rows] = turned
            kTr_ref[p, :, rows] = jnp.concatenate([dot(turned[:, :128], JR), dot(turned[:, 128:], JR)], axis=1).astype(bf)
            v_ref[p, rows, :] = w[:, cols]
            vT_ref[p, :, rows] = w[:, cols].T
        return carry

    lax.fori_loop(0, x_ref.shape[0] // 256, chunk, 0)

    def own(i, carry):
        rows = pl.ds(pl.multiple_of(i * 256, 256), 256)
        x = x_ref[pl.ds(pl.multiple_of(i * 256 + SPAN, 256), 256), :]
        y = (dot(x, query_w[...]) + bias[N_QUERY_B]).astype(bf)
        for p in range(PAIRS):
            q_ref[p, rows, :] = y[:, 128 * p : 128 * p + 128]
            qT_ref[p, :, rows] = y[:, 128 * p : 128 * p + 128].T
        return carry

    lax.fori_loop(0, tokens // 256, own, 0)


SQRT_HALF = 0.7071067811865476
PHI_SCALE = 0.3989422804014327


def gelu_and_slope(u):
    cdf = 0.5 + 0.5 * lax.erf(u * SQRT_HALF)
    return u * cdf, cdf + u * (PHI_SCALE * jnp.exp(-0.5 * u * u))


def feed_body(x_ref, ctx_ref, og_ref, output_w, up_w, down_w, vec_ref, out_ref, dz1_ref, dctx_ref, wide, dvec_ref,
              ml_scr, dup_scr, act_scr, ddown_scr, dattn_scr, slope_scr):
    tokens = out_ref.shape[0]
    dvec_ref[...] = jnp.zeros(dvec_ref.shape, f32)
    vecs = {name: vector(vec_ref, name) for name in (N_OUTPUT_B, N_ATTN_GAIN, N_ATTN_SHIFT, N_UP_BIAS, N_DOWN_BIAS, N_FFN_GAIN, N_FFN_SHIFT)}
    C = 256

    def chunk(i, carry):
        rows = pl.ds(pl.multiple_of(i * C, C), C)
        h = x_ref[pl.ds(pl.multiple_of(i * C + SPAN, C), C), :].astype(f32)
        z1 = h + dot(jnp.concatenate([ctx_ref[p, rows, :] for p in range(PAIRS)], axis=1), output_w[...]) + vecs[N_OUTPUT_B]
        unit1, inv1 = normalized(z1)
        mid = unit1 * vecs[N_ATTN_GAIN] + vecs[N_ATTN_SHIFT]
        ml = mid.astype(bf)
        ml_scr[rows, :] = ml
        z2 = mid + vecs[N_DOWN_BIAS]
        for f in range(FF // 256):
            cols = slice(256 * f, 256 * f + 256)
            up = dot(ml, up_w[:, cols]) + vecs[N_UP_BIAS][:, cols]
            act, slope = gelu_and_slope(up)
            act_scr[rows, cols] = act.astype(bf)
            slope_scr[:, cols] = slope
        z2 = z2 + dot(act_scr[rows, :], down_w[...])
        unit2, inv2 = normalized(z2)
        out_ref[rows, :] = (unit2 * vecs[N_FFN_GAIN] + vecs[N_FFN_SHIFT]).astype(bf)
        dh = og_ref[rows, :].astype(f32)
        add_vector(dvec_ref, N_FFN_GAIN, column_sum(dh * unit2))
        add_vector(dvec_ref, N_FFN_SHIFT, column_sum(dh))
        dz2 = norm_back(dh, vecs[N_FFN_GAIN], unit2, inv2)
        ddown = dz2.astype(bf)
        ddown_scr[rows, :] = ddown
        add_vector(dvec_ref, N_DOWN_BIAS, column_sum(ddown.astype(f32)))
        for f in range(FF // 256):
            cols = slice(256 * f, 256 * f + 256)
            dup = (dot(ddown, down_w[cols, :], NT) * slope_scr[:, cols]).astype(bf)
            dup_scr[rows, cols] = dup
        add_vector(dvec_ref, N_UP_BIAS, column_sum(dup_scr[rows, :].astype(f32)))
        dmid = dz2 + dot(dup_scr[rows, :], up_w[...], NT)
        add_vector(dvec_ref, N_ATTN_GAIN, column_sum(dmid * unit1))
        add_vector(dvec_ref, N_ATTN_SHIFT, column_sum(dmid))
        dz1 = norm_back(dmid, vecs[N_ATTN_GAIN], unit1, inv1)
        dz1_ref[rows, :] = dz1
        dattn = dz1.astype(bf)
        dattn_scr[rows, :] = dattn
        add_vector(dvec_ref, N_OUTPUT_B, column_sum(dattn.astype(f32)))
        dctx = dot(dattn, output_w[...], NT).astype(bf)
        for p in range(PAIRS):
            dctx_ref[p, :, rows] = dctx[:, 128 * p : 128 * p + 128].T
        return carry

    lax.fori_loop(0, tokens // C, chunk, 0)
    place = matrix_rows()

    def put(name, first, rows, value):
        base, _, pieces = place[name]
        for c in range(value.shape[1] // 128):
            wide[pl.ds(base - FEED_FIRST + pieces * first[0] + first[1] + c, rows, stride=pieces), :] = value[:, 128 * c : 128 * c + 128]

    ctx = jnp.concatenate([ctx_ref[p] for p in range(PAIRS)], axis=1)
    put(N_OUTPUT_W, (0, 0), D, dot(ctx, dattn_scr[...], TN))
    for f in range(FF // 256):
        cols = slice(256 * f, 256 * f + 256)
        put(N_UP_W, (0, 2 * f), D, dot(ml_scr[...], dup_scr[:, cols], TN))
        put(N_DOWN_W, (256 * f, 0), 256, dot(act_scr[:, cols], ddown_scr[...], TN))


def split(values):
    high = values.astype(bf)
    return high, (values - high.astype(f32)).astype(bf)


def dot2(left, right, dims=NN):
    if left.dtype == f32:
        return sum(dot(part, right, dims) for part in split(left))
    return sum(dot(left, part, dims) for part in split(right))


def tail_local(dq_ref, x_ref, query_w, dx_ref, dwq_ref, dvec_ref):
    tokens = dx_ref.shape[0]
    dq = jnp.concatenate([dq_ref[p] for p in range(PAIRS)], axis=1)
    dx_ref[...] += dot(dq, query_w[...], NT)
    dwq_ref[...] = dot(x_ref[...], dq, TN)
    put_vector(dvec_ref, N_QUERY_B, column_sum(dq.astype(f32)))


def tail_table(dkr_ref, dqr_ref, pos_ref, table_ref, vec_ref, query_w, key_w, dwq_ref, dwk_ref, dtable_ref, dvec_ref):
    JR = reversal()
    second = iotas(512, 128)[0] == 1
    tabs = {N_KEY_B: jnp.concatenate([SC * dkr_ref[p] for p in range(PAIRS)], axis=1)}
    parts = []
    for p in range(PAIRS):
        part = dqr_ref[p].T
        parts.append(SC * (part[:512] + jnp.where(second, column_sum(part[512:]), 0.0)))
    tabs[N_QUERY_B] = jnp.concatenate(parts, axis=1)
    dpos = None
    for w, dw, name in ((key_w, dwk_ref, N_KEY_B), (query_w, dwq_ref, N_QUERY_B)):
        tab = tabs[name]
        if name == N_KEY_B:
            dw[...] = dot2(pos_ref[...], tab, TN)
            put_vector(dvec_ref, name, column_sum(tab))
        else:
            dw[...] += dot2(pos_ref[...], tab, TN)
            add_vector(dvec_ref, name, column_sum(tab))
        part = dot2(tab, w[...], NT)
        dpos = part if dpos is None else dpos + part
    table = jnp.concatenate([dot(JR, table_ref[128 * b : 128 * b + 128, :]) for b in reversed(range(4))], axis=0)
    unit, inverse = normalized(pltpu.roll(table, 1, 0))
    put_vector(dvec_ref, N_REL_GAIN, column_sum(dpos * unit))
    put_vector(dvec_ref, N_REL_SHIFT, column_sum(dpos))
    dpos = pltpu.roll(norm_back(dpos, vector(vec_ref, N_REL_GAIN), unit, inverse), 511, 0).astype(bf)
    for b in range(4):
        dtable_ref[128 * b : 128 * b + 128, :] = dot(JR, dpos[128 * (3 - b) : 128 * (4 - b)])


def tail_keys(dkc_ref, dkp_ref, dv_ref, halo_ref, x_ref, key_w, value_w, dx_ref, dwk_ref, dwv_ref, dvec_ref):
    tokens = dx_ref.shape[0]
    x = x_ref[...]
    for which, (ref, w, dw, name) in enumerate(((None, key_w, dwk_ref, N_KEY_B), (dv_ref, value_w, dwv_ref, N_VALUE_B))):
        pieces = []
        for p in range(PAIRS):
            middle = slice(SPAN, SPAN + tokens)
            own = SC * (dkc_ref[p, middle, :] + dkp_ref[p, middle, :]) if ref is None else ref[p, middle, :]
            edge = [halo_ref[side, which, p].astype(f32) for side in (0, 1)]
            pieces.append(jnp.concatenate([own[:SPAN] + edge[0], own[SPAN : tokens - SPAN], own[tokens - SPAN :] + edge[1]], axis=0).astype(bf))
        d = jnp.concatenate(pieces, axis=1)
        dx_ref[...] += dot(d, w[...], NT)
        if name == N_KEY_B:
            dw[...] += dot(x, d, TN)
            add_vector(dvec_ref, name, column_sum(d.astype(f32)))
        else:
            dw[...] = dot(x, d, TN)
            put_vector(dvec_ref, name, column_sum(d.astype(f32)))


def beside(grid, step):
    return {"seq": lax.axis_index("seq") + step, "row": lax.axis_index("row")}


def seq_edges(grid):
    s = lax.axis_index("seq")
    return s > 0, s < grid.seq - 1


def enter_all(grid, p):
    sem = pltpu.get_barrier_semaphore()
    total = jnp.int32(0)
    before, after = seq_edges(grid)
    targets = [(grid.device(q), cond) for _, q, cond in neighbours_of(grid, p)]
    targets += [(beside(grid, -1), before), (beside(grid, 1), after)]
    for device, cond in targets:
        guarded(cond, lambda device=device: pl.semaphore_signal(sem, inc=1, device_id=device, device_id_type=MESH))
        total = total + (1 if cond is None else cond.astype(jnp.int32))
    pl.semaphore_wait(sem, total)


def remote(source, target, send_sem, recv_sem, device):
    return pltpu.make_async_remote_copy(
        src_ref=source, dst_ref=target, send_sem=send_sem, recv_sem=recv_sem, device_id=device, device_id_type=MESH)


def assemble(grid, shard, slots, wide, first, final):
    for k in range(grid.count):
        low, high = shard * k // GROUP, -(-shard * (k + 1) // GROUP)
        shared = k + 1 < grid.count and shard * (k + 1) % GROUP != 0
        begin = max(first, low + (1 if k > 0 and shard * k % GROUP != 0 else 0))
        end = min(final, high - (1 if shared else 0))
        block = slots.at[grid.place(k)]
        if end > begin:
            wide[16 * (begin - first) : 16 * (end - first), :] = block[16 * (begin - low) : 16 * (end - low), :].astype(f32)
        if shared and first <= high - 1 < final:
            at = high - 1
            both_parts = block[16 * (at - low) : 16 * (at - low) + 16, :].astype(f32) + slots.at[grid.place(k + 1)][0:16, :].astype(f32)
            wide[16 * (at - first) : 16 * (at - first) + 16, :] = both_parts


def unpack(wide, first, outs):
    place = matrix_rows()
    for name, out in outs.items():
        base, rows, pieces = place[name]
        for c in range(pieces):
            out[:, 128 * c : 128 * c + 128] = wide[pl.ds(base - 16 * first + c, rows, stride=pieces), :].astype(bf)


VMEM = pl.BlockSpec(memory_space=pltpu.VMEM)
ANY = pl.BlockSpec(memory_space=pl.ANY)
FEED_FROM, FEED_TO = FEED_FIRST * 128, (FEED_FIRST + FEED_ROWS) * 128
LATE = (N_OUTPUT_W, N_UP_W, N_DOWN_W)


def projected(T):
    shape = jax.ShapeDtypeStruct
    E = T + 2 * SPAN
    natural = {N_Q: (T, 128), N_Q_TURNED: (128, T), N_K: (E, 128), N_K_TURNED: (128, E), N_K_TURNED_BACK: (128, E), N_V: (E, 128), N_V_TURNED: (128, E)}
    tables = {N_KRT: (512, 128), N_KRT_TURNED: (128, 512), N_QRT: (1024, 128), N_QRT_TURNED: (128, 640)}
    out = {name: shape((PAIRS,) + extent, bf) for name, extent in (natural | tables).items()}
    out[N_KRT] = shape((2 * PAIRS, 512, 128), bf)
    out[N_POS] = shape((512, D), bf)
    out[N_CTX] = shape((PAIRS, T, 128), bf)
    out[N_E] = shape((PAIRS, T // 128, 640, 256), bf)
    out[N_INV] = shape((PAIRS, T // 128, 8, 256), f32)
    return out


def front_outputs(T):
    shape = jax.ShapeDtypeStruct
    proj = projected(T)
    place = matrix_rows()
    out = {name: proj[name] for name in (N_Q, N_K_TURNED, N_K_TURNED_BACK, N_V, N_KRT_TURNED, N_QRT, N_QRT_TURNED, N_POS, N_E, N_INV)}
    for name in (N_QUERY_W, N_KEY_W, N_VALUE_W, N_REL_TABLE):
        out[name] = shape((place[name][1], 128 * place[name][2]), bf)
    out[N_VEC] = shape((vector_rows()[1], 128), f32)
    out[N_OUT] = shape((T, D), bf)
    out[N_DZ1] = shape((T, D), f32)
    out[N_DCTX_TURNED] = shape((PAIRS, 128, T), bf)
    out[N_DFLAT] = shape((FEED_ROWS, 128), bf)
    out[N_DVEC] = shape((vector_rows()[1], 128), f32)
    return out


def front_held(T):
    shape = jax.ShapeDtypeStruct
    proj = projected(T)
    place = matrix_rows()
    held = {name: proj[name] for name in (N_Q_TURNED, N_K, N_V_TURNED, N_KRT, N_CTX)}
    for name in LATE:
        held[name] = shape((place[name][1], 128 * place[name][2]), bf)
    held[N_X_EXT] = shape((T + 2 * SPAN, D), bf)
    held[N_SEG_EXT] = shape((8, T + 2 * SPAN), jnp.int32)
    return held


def shifted_block(values, shift):
    lane = iotas(*values.shape)[1]
    moved = pltpu.roll(values, shift % 128, 1)
    moved = jnp.where(lane < shift % 128, pltpu.roll(moved, 1, 0), moved)
    return pltpu.roll(moved, shift // 128, 0)


def middle_stages(grid, p, slots, send_sem, recv_sem, groups):
    top = grid.size["z"] - 1
    z, y, c, x = p["z"], p["y"], p["c"], p["x"]
    inner = pl.ds(1, top - 1)
    half = 16 * (groups // 2)
    halves = (pl.ds(0, half), pl.ds(half, 16 * groups - half))
    middle = lambda at: jnp.logical_and(at > 0, at < top)
    flips = {axis: dict(p, **{axis: 1 - p[axis]}) for axis in ("y", "c", "x")}

    def line(at, up):
        block = slots.at[at, y, c, x]
        q = dict(p, z=z + (1 if up else -1))
        return remote(block, block, send_sem.at[1 if up else 0, at], recv_sem.at[at], grid.device(q))

    def sends(distance):
        found = [(both([middle(z - distance), z < top]), line(z - distance, True))]
        found.append((both([middle(z + distance), z > 0]), line(z + distance, False)))
        return found

    def take(distance):
        for at in (z - distance, z + distance):
            pl.when(middle(at))(lambda at=at: line(at, True).wait_recv())

    def pass_on(distance):
        for cond, copy in sends(distance):
            pl.when(cond)(copy.start)

    def across(i, first):
        axis = ("y", "x")[i] if first else ("x", "y")[i]
        part = (y, c, x) if first else ((y, c, slice(None)) if axis == "y" else (slice(None), c, x))
        block = slots.at[(inner,) + part + (halves[i], slice(None))]
        at = top + 1 + 2 * i + (0 if first else 1)
        return remote(block, block, send_sem.at[i, top + 1 + (0 if first else 1)], recv_sem.at[at], grid.device(flips[axis]))

    def hand_over():
        block = slots.at[inner, :, c]
        return remote(block, block, send_sem.at[0, top + 3], recv_sem.at[top + 5], grid.device(flips["c"]))

    def begin():
        pass_on(0)

    def second():
        take(1)
        pass_on(1)

    def third():
        for distance in range(2, top):
            take(distance)
            if distance < top - 1:
                pass_on(distance)
        for i in (0, 1):
            across(i, True).start()

    def fourth():
        for i in (0, 1):
            across(i, True).wait_recv()
        for i in (0, 1):
            across(i, False).start()

    def fifth():
        for i in (0, 1):
            across(i, False).wait_recv()
        hand_over().start()

    def finish():
        hand_over().wait_recv()
        hand_over().wait_send()
        for i in (0, 1):
            across(i, True).wait_send()
            across(i, False).wait_send()
        for distance in range(top - 1):
            for cond, copy in sends(distance):
                pl.when(cond)(copy.wait_send)

    return [begin, second, third, fourth, fifth, finish]


def front_kernel(grid, shard, slot_ref, seg_ref, x_any, og_any, *refs):
    tokens = x_any.shape[0]
    blocks = tokens // 128
    outs, held = front_outputs(tokens), front_held(tokens)
    target = dict(zip(outs, refs))
    names = list(outs) + list(held)
    here = dict(zip(names, refs[len(outs) :]))
    slots, og_ref, local_sem, out_sem, send_sem, recv_sem, late_send, late_recv, halo_send, halo_recv = refs[len(outs) + len(names) :]
    p = grid.here()
    _, groups = shard_groups(shard, grid.count)
    before, after = seq_edges(grid)
    early = lambda o: jnp.logical_or(o["z"] == 0, o["z"] == grid.size["z"] - 1)
    x_ext, seg_ext = here[N_X_EXT], here[N_SEG_EXT]
    own = pltpu.make_async_copy(x_any, x_ext.at[pl.ds(SPAN, tokens), :], local_sem.at[0])
    own.start()
    og_load = pltpu.make_async_copy(og_any, og_ref, local_sem.at[1])
    og_load.start()
    if grid.split:
        k = grid.flat(p)
        slots[p["z"], p["y"], p["c"], p["x"]] = shifted_block(slot_ref[...], k * shard % GROUP).astype(bf)
    else:
        for k in range(grid.count):
            slots[grid.place(k)] = slot_ref[k]
    seg_ext[:, SPAN : SPAN + tokens] = jnp.broadcast_to(seg_ref[...] + 1, (8, tokens))
    enter_all(grid, p)
    own.wait()

    def halo_copies(side):
        step = -1 if side == 0 else 1
        take = pl.ds(SPAN, SPAN) if side == 0 else pl.ds(tokens, SPAN)
        land = pl.ds(tokens + SPAN, SPAN) if side == 0 else pl.ds(0, SPAN)
        return [
            remote(x_ext.at[take, :], x_ext.at[land, :], halo_send.at[side, 0], halo_recv.at[side, 0], beside(grid, step)),
            remote(seg_ext.at[:, take], seg_ext.at[:, land], halo_send.at[side, 1], halo_recv.at[side, 1], beside(grid, step)),
        ]

    def start(side):
        for copy in halo_copies(side):
            copy.start()

    def sent(side):
        for copy in halo_copies(side):
            copy.wait_send()

    def landed(side):
        for copy in halo_copies(side):
            copy.wait_recv()

    first_levels, first_partners, first_ends = ([[]], [], [])
    stages = [lambda: None]
    if grid.split:
        gather = Gather(grid, p, slots, send_sem, recv_sem, groups)
        first_levels, first_partners, first_ends = gather.plan(early, False, 0)
        stages = middle_stages(grid, p, slots, late_send, late_recv, groups)
    perform(first_levels[0])
    pl.when(before)(lambda: start(0))
    pl.when(after)(lambda: start(1))

    def clear(rows):
        x_ext[rows, :] = jnp.zeros((SPAN, D), bf)
        seg_ext[:, rows] = jnp.zeros((8, SPAN), jnp.int32)

    pl.when(jnp.logical_not(before))(lambda: clear(pl.ds(0, SPAN)))
    pl.when(jnp.logical_not(after))(lambda: clear(pl.ds(tokens + SPAN, SPAN)))
    for level in first_levels[1:]:
        perform(level)
    perform(first_partners)
    perform(first_ends)
    place = matrix_rows()
    feed_group, end_group = FEED_FIRST // 16, (FEED_FIRST + FEED_ROWS) // 16
    all_groups = flat_rows(shard, grid.count) // 16

    def first_part(wide):
        assemble(grid, shard, slots, wide, 0, feed_group)
        unpack(wide, 0, {name: here[name] for name in (N_QUERY_W, N_KEY_W, N_VALUE_W)})
        assemble(grid, shard, slots, wide, end_group, all_groups)
        unpack(wide, end_group, {N_REL_TABLE: here[N_REL_TABLE]})
        vec_at, vec_total = vector_rows()
        here[N_VEC][...] = jnp.zeros((vec_total, 128), f32)
        for name in VECTORS:
            base, _, pieces = place[name]
            at = base - 16 * end_group
            here[N_VEC][vec_at[name][0] : vec_at[name][0] + pieces, :] = wide[at : at + pieces, :]

    pl.run_scoped(first_part, pltpu.VMEM((16 * max(feed_group, all_groups - end_group), 128), f32))
    pl.when(before)(lambda: sent(0))
    pl.when(after)(lambda: sent(1))
    pl.when(after)(lambda: landed(0))
    pl.when(before)(lambda: landed(1))
    stages[0]()
    project_body(x_ext, *[here[n] for n in (N_QUERY_W, N_KEY_W, N_VALUE_W, N_REL_TABLE, N_VEC, N_Q, N_Q_TURNED, N_K, N_K_TURNED, N_K_TURNED_BACK, N_V, N_V_TURNED, N_KRT, N_KRT_TURNED, N_QRT, N_QRT_TURNED, N_POS)])

    def hook(m):
        for at, stage in zip((0, 2, 4, 8), stages[1:-1]):
            pl.when(m == at)(stage)

    def attend(*scratch):
        att_fwd_body(blocks, *[here[n] for n in (N_Q_TURNED, N_K, N_V_TURNED, N_KRT, N_QRT_TURNED, N_SEG_EXT, N_CTX, N_E, N_INV)], *scratch, hook)

    pl.run_scoped(attend, pltpu.VMEM((2 * (blocks + 4), 2, 128, 640), bf), pltpu.VMEM((blocks, 640, 128), f32), *FORWARD_SCRATCH)
    leaving = {name: pltpu.make_async_copy(here[name], target[name], out_sem.at[i]) for i, name in enumerate(outs)}
    finished = (N_OUT, N_DZ1, N_DCTX_TURNED, N_DFLAT, N_DVEC)
    for name in outs:
        if name not in finished:
            leaving[name].start()
    stages[-1]()

    def second_part(wide):
        assemble(grid, shard, slots, wide, feed_group, end_group)
        unpack(wide, feed_group, {name: here[name] for name in LATE})

    pl.run_scoped(second_part, pltpu.VMEM((FEED_ROWS, 128), f32))

    og_load.wait()

    def feed_part(wide, *scratch):
        feed_body(*[x_ext, here[N_CTX], og_ref] + [here[n] for n in LATE + (N_VEC, N_OUT, N_DZ1, N_DCTX_TURNED)], wide, here[N_DVEC], *scratch)
        here[N_DFLAT][...] = wide[...].astype(bf)

    pl.run_scoped(
        feed_part, pltpu.VMEM((FEED_ROWS, 128), f32), pltpu.VMEM((tokens, D), bf), pltpu.VMEM((tokens, FF), bf), pltpu.VMEM((tokens, FF), bf),
        pltpu.VMEM((tokens, D), bf), pltpu.VMEM((tokens, D), bf), pltpu.VMEM((256, FF), f32))
    for name in finished:
        leaving[name].start()
    for name in outs:
        leaving[name].wait()


FORWARD_SCRATCH = (
    [pltpu.VMEM((640, 256), f32)] * 2 + [pltpu.VMEM((512, 256), f32)] * 2 + [pltpu.VMEM((640, 256), f32)] * 2 + [pltpu.VMEM((8, 256), f32)] * 2
)


def front(grid, shard, slot, x, seg, out_grad):
    tokens = x.shape[0]
    _, groups = shard_groups(shard, grid.count)
    outs, held = front_outputs(tokens), front_held(tokens)
    if not grid.split:
        slot = lax.all_gather(slot, ("seq", "row"))
    results = pl.pallas_call(
        functools.partial(front_kernel, grid, shard),
        out_shape=list(outs.values()),
        in_specs=[VMEM, VMEM, ANY, ANY],
        out_specs=[ANY] * len(outs),
        scratch_shapes=[pltpu.VMEM(a.shape, a.dtype) for a in list(outs.values()) + list(held.values())]
        + [
            pltpu.VMEM((grid.size["z"], grid.size["y"], 2, grid.size["x"], 16 * groups, 128), bf),
            pltpu.VMEM((tokens, D), bf),
            pltpu.SemaphoreType.DMA((2,)),
            pltpu.SemaphoreType.DMA((len(outs),)),
            pltpu.SemaphoreType.DMA((count_sends(grid, groups, False) if grid.split else 1,)),
            pltpu.SemaphoreType.DMA((2, grid.count)),
            pltpu.SemaphoreType.DMA((2, grid.size["z"] + 3)),
            pltpu.SemaphoreType.DMA((grid.size["z"] + 5,)),
            pltpu.SemaphoreType.DMA((2, 2)),
            pltpu.SemaphoreType.DMA((2, 2)),
        ],
        compiler_params=pltpu.CompilerParams(collective_id=0, has_side_effects=True, vmem_limit_bytes=62 << 20),
    )(slot, seg, x, out_grad)
    return dict(zip(outs, results))


def back_scratch(grid, shard, tokens):
    _, groups = shard_groups(shard, grid.count)
    rows = flat_rows(shard, grid.count)
    names, half, blocks = len(direction_names(grid)), (grid.count // 2 if grid.split else 1), tokens // 128
    square = pltpu.VMEM((D, D), bf)
    accumulator = pltpu.VMEM((PAIRS, tokens + 2 * SPAN, 128), f32)
    rim = pltpu.VMEM((2, 2, PAIRS, SPAN, 128), bf)
    return (
        [square, square, square, pltpu.VMEM((2 * SPAN, D), bf), pltpu.VMEM((512, D), bf), pltpu.VMEM((tokens, D), bf), pltpu.VMEM((tokens, D), f32)]
        + [pltpu.VMEM((PAIRS, tokens, 128), bf), accumulator, accumulator, accumulator, pltpu.VMEM((PAIRS, 512, 128), f32), pltpu.VMEM((PAIRS, 128, 640), f32)]
        + [pltpu.VMEM((2 * (blocks + 4), 2, 128, 640), bf), pltpu.VMEM((640, 256), f32), pltpu.VMEM((512, 256), f32)]
        + [pltpu.VMEM((640, 256), bf)] * 2 + [pltpu.VMEM((512, 256), bf)] * 2 + [pltpu.VMEM((4, 640, 256), bf), pltpu.SemaphoreType.DMA((2,))]
        + [pltpu.VMEM((D, D), f32)] * 3 + [pltpu.VMEM((2 * SPAN, D), f32), pltpu.VMEM((vector_rows()[1], 128), f32)]
        + [pltpu.VMEM((max(3 * D, rows - FEED_FIRST - FEED_ROWS), 128), f32), pltpu.VMEM((rows, 128), bf)]
        + [pltpu.VMEM((names, half, 16 * groups, 128), bf), pltpu.VMEM((16 * groups, 128), f32)]
        + [rim, rim, pltpu.SemaphoreType.DMA((8,)), pltpu.SemaphoreType.DMA((scatter_sends(grid, groups, False) + scatter_sends(grid, groups, True) if grid.split else 1,))]
        + [pltpu.SemaphoreType.DMA((2, names, half)), pltpu.SemaphoreType.DMA((2,)), pltpu.SemaphoreType.DMA((2,))]
    )


def back_kernel(grid, shard, q_ref, kT_ref, kTr_ref, v_ref, krtT_ref, qrt_ref, qrtT_ref, dctxT_ref, e_ref, inv_ref, vec_ref, dvec_in, *refs):
    sources, (dx_out, sum_ref) = refs[:8], refs[8:10]
    query_w, key_w, value_w, table_ref, pos_ref, x_ref, dx_ref = refs[10:17]
    dq, dkc, dkp, dv, dkr, dqr = refs[17:23]
    work = refs[23:32]
    dwq, dwk, dwv, dtable, dvec_ref, wide, flat, kids, total, halo_out, halo_in, load_sem, send_sem, recv_sem, halo_send, halo_recv = refs[32:]
    p = grid.here()
    tokens = dx_ref.shape[0]
    blocks = tokens // 128
    _, groups = shard_groups(shard, grid.count)
    before, after = seq_edges(grid)
    feed = pl.ds(FEED_FIRST, FEED_ROWS)
    targets = (flat.at[feed, :], query_w, key_w, value_w, table_ref, pos_ref, x_ref, dx_ref)
    loads = [pltpu.make_async_copy(source, target, load_sem.at[i]) for i, (source, target) in enumerate(zip(sources, targets))]
    for load in loads:
        load.start()
    enter_all(grid, p)
    first_row = lambda k: (k * shard // GROUP) * 16
    early = lambda k: jnp.logical_and(first_row(k) >= FEED_FIRST, first_row(k) + 16 * groups <= FEED_FIRST + FEED_ROWS)
    gifts, levels, ends, last_gifts, last_levels, last_ends = ([], [], [], [], [], [])
    if grid.split:
        scatter = lambda: Scatter(grid, p, flat, first_row, kids, total, send_sem, recv_sem, groups)
        gifts, levels, ends = scatter().plan(sum_ref, early, True, 0)
        last_gifts, last_levels, last_ends = scatter().plan(sum_ref, lambda k: jnp.logical_not(early(k)), False, scatter_sends(grid, groups, True))
    loads[0].wait()
    perform(gifts)

    def hook(m):
        for i, level in enumerate(levels):
            pl.when(m == min(2 * i + 1, PAIRS * blocks // 2 - 1))(lambda level=level: perform(level))

    att_bwd_body(blocks, q_ref, kT_ref, kTr_ref, v_ref, krtT_ref, qrt_ref, qrtT_ref, dctxT_ref, e_ref, inv_ref, dq, dkc, dkp, dv, dkr, dqr, *work, hook)
    rims = (pl.ds(0, SPAN), pl.ds(tokens + SPAN, SPAN))
    for side in (0, 1):
        halo_out[side, 0] = (SC * (dkc[:, rims[side], :] + dkp[:, rims[side], :])).astype(bf)
        halo_out[side, 1] = dv[:, rims[side], :].astype(bf)

    def halo_copy(side):
        return remote(halo_out.at[side], halo_in.at[1 - side], halo_send.at[side], halo_recv.at[1 - side], beside(grid, -1 if side == 0 else 1))

    pl.when(before)(lambda: halo_copy(0).start())
    pl.when(after)(lambda: halo_copy(1).start())

    def clear(side):
        halo_in[side] = jnp.zeros(halo_in.shape[1:], bf)

    pl.when(jnp.logical_not(before))(lambda: clear(0))
    pl.when(jnp.logical_not(after))(lambda: clear(1))
    for load in loads[1:]:
        load.wait()
    dvec_ref[...] = dvec_in[...]
    tail_local(dq, x_ref, query_w, dx_ref, dwq, dvec_ref)
    tail_table(dkr, dqr, pos_ref, table_ref, vec_ref, query_w, key_w, dwq, dwk, dtable, dvec_ref)
    pl.when(before)(lambda: halo_copy(0).wait_send())
    pl.when(after)(lambda: halo_copy(1).wait_send())
    pl.when(before)(lambda: halo_copy(1).wait_recv())
    pl.when(after)(lambda: halo_copy(0).wait_recv())
    tail_keys(dkc, dkp, dv, halo_in, x_ref, key_w, value_w, dx_ref, dwk, dwv, dvec_ref)
    leave = pltpu.make_async_copy(dx_ref, dx_out, load_sem.at[0])
    leave.start()
    place = matrix_rows()
    vec_at, _ = vector_rows()
    final = FEED_FIRST + FEED_ROWS
    for name, ref in ((N_QUERY_W, dwq), (N_KEY_W, dwk), (N_VALUE_W, dwv)):
        base, rows, pieces = place[name]
        for c in range(pieces):
            wide[pl.ds(c, rows, stride=pieces), :] = ref[:, 128 * c : 128 * c + 128]
        flat[base : base + rows * pieces, :] = wide[0 : rows * pieces, :].astype(bf)
    rest = flat.shape[0] - final
    wide[0:rest, :] = jnp.zeros((rest, 128), f32)
    base, rows, pieces = place[N_REL_TABLE]
    for c in range(pieces):
        wide[pl.ds(base - final + c, rows, stride=pieces), :] = dtable[:, 128 * c : 128 * c + 128]
    for name in VECTORS:
        base, _, pieces = place[name]
        wide[base - final : base - final + pieces, :] = dvec_ref[vec_at[name][0] : vec_at[name][0] + pieces, :]
    flat[final:, :] = wide[0:rest, :].astype(bf)
    if not grid.split:
        sum_ref[...] = flat[...]
    perform(last_gifts)
    for level in last_levels:
        perform(level)
    perform(ends)
    perform(last_ends)
    leave.wait()


def back(grid, shard, f, x):
    _, groups = shard_groups(shard, grid.count)
    tokens = x.shape[0]
    shape = jax.ShapeDtypeStruct
    leaving = shape((16 * groups, 128), f32) if grid.split else shape((flat_rows(shard, grid.count), 128), bf)
    dx, summed = pl.pallas_call(
        functools.partial(back_kernel, grid, shard),
        out_shape=[shape((tokens, D), f32), leaving],
        in_specs=[VMEM] * 8 + [ANY] + [VMEM] * 3 + [ANY] * 8,
        out_specs=[ANY, VMEM],
        scratch_shapes=back_scratch(grid, shard, tokens),
        compiler_params=pltpu.CompilerParams(collective_id=1, has_side_effects=True, vmem_limit_bytes=62 << 20),
    )(
        *[f[n] for n in (N_Q, N_K_TURNED, N_K_TURNED_BACK, N_V, N_KRT_TURNED, N_QRT, N_QRT_TURNED, N_DCTX_TURNED, N_E, N_INV, N_VEC, N_DVEC)],
        *[f[n] for n in (N_DFLAT, N_QUERY_W, N_KEY_W, N_VALUE_W, N_REL_TABLE, N_POS)], x, f[N_DZ1])
    if not grid.split:
        first, _ = shard_groups(shard, grid.count)
        pieces = jnp.concatenate([summed[16 * at : 16 * (at + groups)] for at in first], axis=0)
        summed = lax.psum_scatter(pieces.astype(f32), ("seq", "row"), scatter_dimension=0, tiled=True)
    return dx, summed


def on_device(layer_input, segment_ids, out_grad, weights, momentum, average):
    tokens_here = layer_input.shape[1]
    grid = Grid(lax.axis_size("seq"), lax.axis_size("row"))
    shard = weights.shape[0]
    _, groups = shard_groups(shard, grid.count)
    shift = (lax.axis_index("seq") * grid.row + lax.axis_index("row")) * shard % GROUP
    slot = jnp.pad(weights, (0, GROUP * groups - shard)).reshape(16 * groups, 128)
    if not grid.split:
        slot = lax.dynamic_update_slice(jnp.zeros((GROUP * groups,), bf), weights.astype(bf), (shift,)).reshape(16 * groups, 128)
    f = front(grid, shard, slot, layer_input[0], segment_ids, out_grad[0])
    block_output = f[N_OUT]
    dx, summed = back(grid, shard, f, layer_input[0])
    weight_grad = lax.dynamic_slice(summed.reshape(-1), (shift,), (shard,))
    all_tokens = tokens_here * grid.seq * layer_input.shape[0] * grid.row
    rate = 0.1 / math.sqrt(all_tokens)
    new_momentum = 0.5 * momentum + weight_grad
    new_weights = weights - rate * (weight_grad + 0.5 * new_momentum)
    new_average = 0.5 * average + 0.5 * new_weights
    return (
        block_output[None],
        dx[None],
        weight_grad,
        new_momentum,
        new_average,
        new_weights,
        new_weights.astype(jnp.bfloat16),
    )


def solution(mesh):
    flat = P(("seq", "row"))
    tokens = P("row", "seq", None)
    return jax.shard_map(
        on_device,
        mesh=mesh,
        in_specs=(tokens, P("row", "seq"), tokens, flat, flat, flat),
        out_specs=(tokens, tokens, flat, flat, flat, flat, flat),
        check_vma=False,
    )
```

```python
import functools
import itertools
import math

import jax
import jax.numpy as jnp
from jax import lax
from jax.experimental import pallas as pl
from jax.experimental.pallas import tpu as pltpu
from jax.sharding import PartitionSpec as P

D = 384
HEADS = 6
HEAD_DIM = 64
FF = 1536
SPAN = 256
PAIRS = HEADS // 2
NB = 5
EPSILON = 1e-07
(N_ATTN_GAIN, N_ATTN_SHIFT, N_CTX, N_DCTX_TURNED, N_DFLAT, N_DOWN_BIAS, N_DOWN_W, N_DVEC, N_DZ1, N_E, N_FFN_GAIN, N_FFN_SHIFT, N_INV, N_K, N_K_TURNED, N_K_TURNED_BACK, N_KEY_B, N_KEY_W, N_KRT, N_KRT_TURNED, N_OUT, N_OUTPUT_B, N_OUTPUT_W, N_POS, N_Q, N_Q_TURNED, N_QRT, N_QRT_TURNED, N_QUERY_B, N_QUERY_W, N_REL_GAIN, N_REL_SHIFT, N_REL_TABLE, N_SEG_EXT, N_UP_BIAS, N_UP_W, N_V, N_V_TURNED, N_VALUE_B, N_VALUE_W, N_VEC, N_X_EXT) = range(42)
bf = jnp.bfloat16
f32 = jnp.float32


MESH = pl.DeviceIdType.MESH
GROUP = 2048


class Grid:
    def __init__(self, seq, row):
        half = seq // 2
        wide = 1
        while wide * wide * 4 <= half:
            wide *= 2
        self.size = {"z": half // wide, "y": wide, "x": row}
        self.seq, self.row, self.count = seq, row, seq * row
        self.split = self.size["y"] == 2 and row == 2 and half > 4

    def here(self):
        s, x = lax.axis_index("seq"), lax.axis_index("row")
        y_size = self.size["y"]
        return {"z": s // (2 * y_size), "y": (s // 2) % y_size, "c": s % 2, "x": x}

    def seq_of(self, p):
        return (p["z"] * self.size["y"] + p["y"]) * 2 + p["c"]

    def flat(self, p):
        return self.seq_of(p) * self.row + p["x"]

    def device(self, p):
        return {"seq": self.seq_of(p), "row": p["x"]}

    def place(self, k):
        s, x = divmod(k, self.row)
        line, c = divmod(s, 2)
        z, y = divmod(line, self.size["y"])
        return z, y, c, x

    def plane(self, p):
        return (p["z"] * self.size["y"] + p["y"]) * self.row + p["x"]

    def offsets(self, order):
        choices = []
        for axis in order:
            n = self.size[axis]
            if n == 2:
                choices.append([0, "f"])
            else:
                choices.append([0] + [sign * d for d in range(1, n) for sign in (-1, 1)])
        hops = lambda off: sum(1 if o == "f" else abs(o) for o in off)
        return sorted(itertools.product(*choices), key=hops)


def both(conds):
    out = None
    for cond in conds:
        if cond is not None:
            out = cond if out is None else jnp.logical_and(out, cond)
    return out


def guarded(cond, fn):
    if cond is None:
        fn()
    else:
        pl.when(cond)(fn)


def source_of(grid, p, order, off):
    o, conds = dict(p), []
    for axis, d in zip(order, off):
        if d == "f":
            o[axis] = 1 - p[axis]
        elif d != 0:
            o[axis] = p[axis] + d
            conds.append(p[axis] + d >= 0 if d < 0 else p[axis] + d < grid.size[axis])
    return o, both(conds)


def children_of(grid, p, order, off):
    last = max((i for i, d in enumerate(off) if d != 0), default=None)
    found = []
    if last is not None and off[last] != "f":
        axis, away = order[last], (-1 if off[last] > 0 else 1)
        q = dict(p)
        q[axis] = p[axis] + away
        found.append((axis + ("+" if away > 0 else "-"), q, p[axis] > 0 if away < 0 else p[axis] < grid.size[axis] - 1))
    for axis in order[0 if last is None else last + 1 :]:
        if grid.size[axis] == 2:
            q = dict(p)
            q[axis] = 1 - p[axis]
            found.append((axis + "0", q, None))
        elif grid.size[axis] > 2:
            for sign in (1, -1):
                q = dict(p)
                q[axis] = p[axis] + sign
                found.append((axis + ("+" if sign > 0 else "-"), q, p[axis] > 0 if sign < 0 else p[axis] < grid.size[axis] - 1))
    return found


def neighbours_of(grid, p):
    found = []
    for axis in ("z", "y", "x"):
        found += children_of(grid, p, (axis,), (0,))
    sibling = dict(p)
    sibling["c"] = 1 - p["c"]
    found.append(("c0", sibling, None))
    return found


def enter(grid, p, extra=()):
    sem = pltpu.get_barrier_semaphore()
    total = jnp.int32(0)
    for name, q, cond in neighbours_of(grid, p) + list(extra):
        guarded(cond, lambda q=q: pl.semaphore_signal(sem, inc=1, device_id=grid.device(q), device_id_type=MESH))
        total = total + (1 if cond is None else cond.astype(jnp.int32))
    pl.semaphore_wait(sem, total)


def parts_of(groups, whole):
    if whole:
        return ((("z", "y", "x"), 0, 16 * groups),)
    first = 16 * (groups // 2)
    return ((("z", "y", "x"), 0, first), (("x", "z", "y"), first, 16 * groups - first))


class Gather:
    def __init__(self, grid, p, slots, send_sem, recv_sem, groups):
        self.grid, self.p, self.slots = grid, p, slots
        self.send_sem, self.recv_sem, self.groups = send_sem, recv_sem, groups
        self.sends, self.used = [], 0

    def block(self, o, start, rows):
        return self.slots.at[o["z"], o["y"], o["c"], o["x"], pl.ds(start, rows), :]

    def copy(self, part, start, rows, o, q, index):
        block, k = self.block(o, start, rows), self.grid.flat(o)
        return pltpu.make_async_remote_copy(
            src_ref=block, dst_ref=block, send_sem=self.send_sem.at[index], recv_sem=self.recv_sem.at[part, k],
            device_id=self.grid.device(q), device_id_type=MESH)

    def arrived(self, part, start, rows, o):
        block, k = self.block(o, start, rows), self.grid.flat(o)
        pltpu.make_async_remote_copy(
            src_ref=block, dst_ref=block, send_sem=self.send_sem.at[0], recv_sem=self.recv_sem.at[part, k],
            device_id=self.grid.device(self.p), device_id_type=MESH).wait_recv()

    def plan(self, chosen, whole, used):
        grid, p = self.grid, self.p
        sibling = dict(p)
        sibling["c"] = 1 - p["c"]
        levels, ends, partners = {}, [], []
        for part, (order, start, rows) in enumerate(parts_of(self.groups, whole)):
            for off in grid.offsets(order):
                hops = sum(1 if o == "f" else abs(o) for o in off)
                o, cond = source_of(grid, p, order, off)
                k = grid.flat(o)
                targets = children_of(grid, p, order, off) + [("c0", sibling, None)]
                indices = [used + i for i in range(len(targets))]
                used += len(targets)
                cond = both([cond, chosen(o)])

                def step(what=(part, start, rows, o), targets=targets, indices=indices, own=hops == 0):
                    if not own:
                        self.arrived(*what)
                    for (name, q, when), index in zip(targets, indices):
                        guarded(when, lambda q=q, index=index: self.copy(*what, q, index).start())

                def end(what=(part, start, rows, o), targets=targets, indices=indices):
                    for (name, q, when), index in zip(targets, indices):
                        guarded(when, lambda q=q, index=index: self.copy(*what, q, index).wait_send())

                levels.setdefault(hops, []).append((cond, step))
                ends.append((cond, end))
                o, cond = source_of(grid, sibling, order, off)
                k = grid.flat(o)
                partners.append((both([cond, chosen(o)]), lambda what=(part, start, rows, o): self.arrived(*what)))
        return [levels[h] for h in sorted(levels)], partners, ends


def perform(steps):
    for cond, step in steps:
        guarded(cond, step)


def count_sends(grid, groups, whole):
    fake = {"z": jnp.int32(0), "y": jnp.int32(0), "x": jnp.int32(0), "c": jnp.int32(0)}
    return sum(len(children_of(grid, fake, order, off)) + 1 for order, _, _ in parts_of(groups, whole) for off in grid.offsets(order))


class Scatter:
    def __init__(self, grid, p, flat, first_row, kids, total, send_sem, recv_sem, groups):
        self.grid, self.p, self.flat, self.first_row = grid, p, flat, first_row
        self.kids, self.total = kids, total
        self.send_sem, self.recv_sem, self.groups = send_sem, recv_sem, groups

    def incoming(self, part, kid, place):
        start, rows = self.spans[part]
        return self.kids.at[kid, place, pl.ds(start, rows), :]

    def transfer(self, source, part, kid, place, q, send):
        return pltpu.make_async_remote_copy(
            src_ref=source, dst_ref=self.incoming(part, kid, place), send_sem=self.send_sem.at[send],
            recv_sem=self.recv_sem.at[part, kid, place], device_id=self.grid.device(q), device_id_type=MESH)

    def arrived(self, part, kid, place):
        block = self.incoming(part, kid, place)
        pltpu.make_async_remote_copy(
            src_ref=block, dst_ref=block, send_sem=self.send_sem.at[0], recv_sem=self.recv_sem.at[part, kid, place],
            device_id=self.grid.device(self.p), device_id_type=MESH).wait_recv()

    def plan(self, result, chosen, whole, used):
        grid, p = self.grid, self.p
        sibling = dict(p)
        sibling["c"] = 1 - p["c"]
        along = {"y": 1, "x": 2}
        gifts, levels, ends = [], {}, []
        self.spans = [part[1:] for part in parts_of(self.groups, whole)]
        for part, (order, start, rows) in enumerate(parts_of(self.groups, whole)):
            for off in sorted(grid.offsets(order), key=lambda off: -sum(o != 0 for o in off)):
                hops = sum(o != 0 for o in off)
                o, cond = source_of(grid, sibling, order, off)
                cond = both([cond, chosen(grid.flat(o))])

                def give(part=part, o=o, index=used, start=start, rows=rows):
                    block = self.flat.at[pl.ds(pl.multiple_of(self.first_row(grid.flat(o)) + start, 16), rows), :]
                    return self.transfer(block, part, 0, grid.plane(o), sibling, index)

                gifts.append((cond, lambda give=give: give().start()))
                ends.append((cond, lambda give=give: give().wait_send()))
                used += 1
                o, cond = source_of(grid, p, order, off)
                place, k = grid.plane(o), grid.flat(o)
                cond = both([cond, chosen(k)])
                last = max((i for i, d in enumerate(off) if d != 0), default=None)
                kids = []
                for axis in order[0 if last is None else last + 1 :]:
                    if axis == "z":
                        kids += [(3 + s, p["z"] != s) for s in range(grid.size["z"])]
                    else:
                        kids.append((along[axis], None))
                parent, kid = None, None
                if last is not None:
                    parent = dict(p)
                    parent[order[last]] = o[order[last]]
                    kid = 3 + p["z"] if order[last] == "z" else along[order[last]]

                def push(part=part, place=place, parent=parent, kid=kid, index=used):
                    return self.transfer(self.incoming(part, 0, place), part, kid, place, parent, index)

                def step(part=part, place=place, k=k, kids=kids, parent=parent, start=start, rows=rows, push=push):
                    self.arrived(part, 0, place)
                    mine = self.flat[pl.ds(pl.multiple_of(self.first_row(k) + start, 16), rows), :].astype(f32)
                    self.total[0:rows, :] = mine + self.incoming(part, 0, place)[...].astype(f32)
                    for kid, when in kids:

                        def add(kid=kid):
                            self.arrived(part, kid, place)
                            self.total[0:rows, :] += self.incoming(part, kid, place)[...].astype(f32)

                        guarded(when, add)
                    if parent is None:
                        result[pl.ds(start, rows), :] = self.total[0:rows, :]
                    else:
                        self.kids[0, place, pl.ds(start, rows), :] = self.total[0:rows, :].astype(bf)
                        push().start()

                levels.setdefault(-hops, []).append((cond, step))
                if parent is not None:
                    ends.append((cond, lambda push=push: push().wait_send()))
                    used += 1
        return gifts, [levels[h] for h in sorted(levels)], ends


    def plan_outer(self, result, chosen, used):
        grid, p = self.grid, self.p
        sibling = dict(p, c=1 - p["c"])
        self.spans = [part[1:] for part in parts_of(self.groups, False)]
        gifts, steps, ends = [], [], []
        for distance in (2, 1, 0):
            for part, (start, rows) in enumerate(self.spans):
                for plane in (0, grid.size["z"] - 1):
                    for fy, fx in ((1, 1), (1, 0), (0, 1), (0, 0)):
                        if fy + fx != distance:
                            continue
                        o = dict(p, z=plane, y=1 - p["y"] if fy else p["y"], x=1 - p["x"] if fx else p["x"])
                        other = dict(o, c=sibling["c"])
                        here = p["z"] == plane

                        def give(part=part, o=other, index=used, start=start, rows=rows):
                            block = self.flat.at[pl.ds(pl.multiple_of(self.first_row(grid.flat(o)) + start, 16), rows), :]
                            return self.transfer(block, part, 0, grid.plane(o), sibling, index)

                        wanted = chosen(grid.flat(other)) if plane else None
                        first = (0 if fx else 1 + (not fy)) if part == 0 else 1 - fy
                        gifts.append((first, wanted, lambda give=give: give().start()))
                        ends.append((wanted, lambda give=give: give().wait_send()))
                        cond = chosen(grid.flat(o)) if plane else None
                        flip_x, flip_y, straight = (dict(p, x=1 - p["x"]), 2), (dict(p, y=1 - p["y"]), 1), (dict(p, z=plane), 3 + p["z"])
                        planes = [(3 + s, both([here, p["z"] != s])) for s in range(grid.size["z"])]
                        if part == 0:
                            kids = [] if fx else [(2, None)] if fy else [(2, None), (1, None)] + planes
                            routes = [(None, flip_x)] if fx else [(None, flip_y)] if fy else [(jnp.logical_not(here), straight)]
                        else:
                            kids = [] if fy else [(1, None)] + planes + ([] if fx else [(2, here)])
                            routes = [(None, flip_y)] if fy else [(jnp.logical_not(here), straight)] + ([(here, flip_x)] if fx else [])
                        place = grid.plane(o)
                        pushes = []
                        for n, (when, (q, kid)) in enumerate(routes):

                            def push(part=part, place=place, q=q, kid=kid, index=used + 1 + n):
                                return self.transfer(self.incoming(part, 0, place), part, kid, place, q, index)

                            pushes.append((when, push))
                            ends.append((both([cond, when]), lambda push=push: push().wait_send()))
                        used += 3

                        def step(part=part, place=place, o=o, kids=kids, pushes=pushes, start=start, rows=rows, owner=here if fy + fx == 0 else None):
                            self.arrived(part, 0, place)
                            mine = self.flat[pl.ds(pl.multiple_of(self.first_row(grid.flat(o)) + start, 16), rows), :].astype(f32)
                            self.total[0:rows, :] = mine + self.incoming(part, 0, place)[...].astype(f32)
                            for kid, when in kids:

                                def add(kid=kid):
                                    self.arrived(part, kid, place)
                                    self.total[0:rows, :] += self.incoming(part, kid, place)[...].astype(f32)

                                guarded(when, add)
                            self.kids[0, place, pl.ds(start, rows), :] = self.total[0:rows, :].astype(bf)
                            for when, push in pushes:
                                guarded(when, lambda push=push: push().start())
                            if owner is not None:

                                def finish():
                                    result[pl.ds(start, rows), :] = self.total[0:rows, :]

                                pl.when(owner)(finish)

                        away = jnp.logical_not(here)
                        if part == 0:
                            found = [(0, None)] if fx else [(1, None)] if fy else [(2, away), (3, here)]
                        else:
                            found = [(0, None)] if fy else [(1, away), (2, here)] if fx else [(1, away), (3, here)]
                        for ready, when in found:
                            steps.append((ready, both([cond, when]), step))
        steps.sort(key=lambda item: item[0])
        gifts.sort(key=lambda item: item[0])
        return [item[1:] for item in gifts], [item[1:] for item in steps], ends


def scatter_sends(grid, groups, whole):
    return 2 * sum(len(grid.offsets(order)) for order, _, _ in parts_of(groups, whole))


def shard_groups(shard, count):
    first = [shard * k // GROUP for k in range(count)]
    groups = max(-(-shard * (k + 1) // GROUP) - first[k] for k in range(count))
    return first, max(groups, 2)


def flat_rows(shard, count):
    first, groups = shard_groups(shard, count)
    return 16 * (first[-1] + groups)


def layer_pieces():
    square, vector_of = (D, D), (D,)
    return (
        (N_QUERY_W, square), (N_KEY_W, square), (N_VALUE_W, square), (N_OUTPUT_W, square), (N_UP_W, (D, FF)), (N_DOWN_W, (FF, D)),
        (N_QUERY_B, vector_of), (N_KEY_B, vector_of), (N_VALUE_B, vector_of), (N_OUTPUT_B, vector_of), (N_ATTN_GAIN, vector_of),
        (N_ATTN_SHIFT, vector_of), (N_UP_BIAS, (FF,)), (N_DOWN_BIAS, vector_of), (N_FFN_GAIN, vector_of), (N_FFN_SHIFT, vector_of),
        (N_REL_TABLE, (2 * SPAN, D)), (N_REL_GAIN, vector_of), (N_REL_SHIFT, vector_of),
    )


def matrix_rows():
    place, at = {}, 0
    for name, extent in layer_pieces():
        if len(extent) == 2:
            place[name] = (at // 128, extent[0], extent[1] // 128)
        else:
            place[name] = (at // 128, 1, extent[0] // 128)
        at += math.prod(extent)
    return place


MATRICES = (N_QUERY_W, N_KEY_W, N_VALUE_W, N_OUTPUT_W, N_UP_W, N_DOWN_W, N_REL_TABLE)
VECTORS = tuple(name for name, extent in layer_pieces() if len(extent) == 1)
FEED_FIRST = matrix_rows()[N_OUTPUT_W][0]
FEED_ROWS = matrix_rows()[N_QUERY_B][0] - FEED_FIRST
USED_ROWS = sum(rows * pieces for _, rows, pieces in matrix_rows().values())


def vector_rows():
    place, at = {}, 0
    for name in VECTORS:
        wide = matrix_rows()[name][2]
        place[name] = (at, wide)
        at += wide
    return place, -(-at // 8) * 8


SC = 1.0 / math.sqrt(3.0 * HEAD_DIM)
LOG2E = 1.4426950408889634
NT = (((1,), (1,)), ((), ()))
NN = (((1,), (0,)), ((), ()))
TN = (((0,), (0,)), ((), ()))


def dot(a, b, dims=NN):
    return lax.dot_general(a, b, dims, preferred_element_type=f32)


def iotas(rows, lanes):
    return lax.broadcasted_iota(jnp.int32, (rows, lanes), 0), lax.broadcasted_iota(jnp.int32, (rows, lanes), 1)


def tile(i):
    return pl.ds(pl.multiple_of(i * 128, 128), 128)


def window(i):
    return pl.ds(pl.multiple_of(i * 128, 128), NB * 128)


def wide_diagonal(columns):
    zero = jnp.zeros((64, 128), columns.dtype)
    return jnp.concatenate([jnp.concatenate([columns[:64], zero], axis=1), jnp.concatenate([zero, columns[64:]], axis=1)], axis=0)


def tall_diagonal(rows):
    lane = iotas(128, 128)[1]
    zero = jnp.zeros_like(rows)
    return jnp.concatenate([jnp.where(lane < 64, rows, zero), jnp.where(lane >= 64, rows, zero)], axis=0)


def own_heads(wide):
    return jnp.concatenate([wide[:64, :128], wide[64:, 128:]], axis=0)


def turn_rows(values, back):
    size = values.shape[0]
    lane = iotas(*values.shape)[1]
    for step in (64, 32, 16, 8, 4, 2, 1):
        moved = pltpu.roll(values, size - step if back else step, 0)
        values = jnp.where(lane & step != 0, moved, values)
    return values


def turn_lanes(values, first):
    return jnp.concatenate([pltpu.roll(values[8 * g : 8 * g + 8, :512], first + 8 * g, 1, stride=1, stride_axis=0) for g in range(16)], axis=0)


def stream_rows(load, up, fine):
    row, lane = iotas(8, 128)
    inner = [(step, lane & step != 0, row < step if not up else row >= 8 - step) for step in fine]
    masks = [lane & step != 0 for step in (8, 16, 32, 64)]
    turned = [None for _ in inner]
    past = [[] for _ in masks]
    extra = 15 + len(inner)
    order = list(range(64 - extra, 64)) + list(range(64)) if not up else list(reversed(list(range(64)) + list(range(extra))))
    for n, i in enumerate(order):
        value = load(i)
        for level, (step, mask, edge) in enumerate(inner):
            now = pltpu.roll(value, step if not up else 8 - step, 0)
            if turned[level] is not None:
                value = jnp.where(mask, jnp.where(edge, turned[level], now), value)
            turned[level] = now
        for level, mask in enumerate(masks):
            past[level].append(value)
            if len(past[level]) > 1 << level:
                value = jnp.where(mask, past[level].pop(0), value)
        if n >= extra:
            yield i, value


def att_fwd_body(nblk, qT_ref, k_ref, vT_ref, krt_ref, qrtT_ref, seg_ref, ctx_ref, p_ref, inv_ref, x_scr, bias_scr, s0, s1, z0, z1, t0, t1, m0, m1, hook=None):
    row, lane = iotas(128, 128)
    lane2 = iotas(128, 256)[1]
    lane512 = iotas(512, 256)[1]
    items, keys = PAIRS * nblk, nblk + 4

    def mk_bias(t, carry):
        sq = seg_ref[0:1, tile(t + 2)].astype(f32)
        for b in range(NB):
            sk = jnp.broadcast_to(seg_ref[0:1, tile(t + b)], (128, 128)).astype(f32).T
            ok = sk == sq
            if b == 0:
                ok = ok & (row >= lane)
            if b == NB - 1:
                ok = ok & (row <= lane)
            bias_scr[t, 128 * b : 128 * b + 128, :] = jnp.where(ok, 0.0, -1e30).astype(f32)
        return carry

    lax.fori_loop(0, nblk, mk_bias, 0)

    def keyside(p, J, slot):
        C = dot(tall_diagonal(k_ref[p, tile(J), :]), qrtT_ref[p])
        for h in range(2):
            Ch = C[128 * h : 128 * h + 128]
            R = turn_lanes(Ch, 0)
            x_scr[slot, h, :, 0:128] = jnp.where(lane > row, R[:, :128], Ch[:, 512:]).astype(bf)
            x_scr[slot, h, :, 128:512] = R[:, 128:].astype(bf)
            x_scr[slot, h, :, 512:640] = R[:, :128].astype(bf)

    def start(J, carry):
        keyside(0, J, J)
        return carry

    lax.fori_loop(0, keys, start, 0)

    def scores(n, s_scr, z_scr, t_scr, m_scr):
        n = jnp.minimum(n, items - 1)
        p, t = n // nblk, n % nblk
        base = (p % 2) * keys + t
        Q2 = wide_diagonal(qT_ref[p, :, tile(t)])
        odd = lane2 % 2 == 1
        zero = jnp.zeros_like(Q2)
        table = krt_ref[p]
        moved = krt_ref[PAIRS + p]
        Z = dot(jnp.concatenate([table, moved], axis=1), jnp.concatenate([jnp.where(odd, zero, Q2), jnp.where(odd, Q2, zero)], axis=0))
        ends = jnp.where(odd[:1], Z[2:3], Z[1:2])
        z_scr[...] = Z
        s_scr[...] = dot(k_ref[p, window(t), :], Q2)
        for h in range(2):
            cols = slice(128 * h, 128 * h + 128)

            def load(i):
                return z_scr[8 * i : 8 * i + 8, cols]

            end = ends[:, cols]
            top = None
            held = None
            for i, y in stream_rows(load, False, (2, 4)):
                if i % 2 == 0:
                    held = y
                    continue
                at, b = 8 * (i - 1), i // 16
                y = jnp.concatenate([held, y], axis=0)
                for block in (0, 4) if b == 0 else (b,):
                    r = at + 128 * (block - b)
                    rows = slice(r, r + 16)
                    inner = slice(at % 128, at % 128 + 16)
                    x = x_scr[base + block, h, inner, 128 * (4 - block) : 128 * (5 - block)].astype(f32)
                    part = y
                    if block == 0:
                        part = jnp.where(iotas(16, 128)[0] + at > iotas(16, 128)[1], y, end)
                    T = s_scr[rows, cols] + bias_scr[t, rows, :] + part + x
                    t_scr[rows, cols] = T
                    most = jnp.maximum(T[:8], T[8:])
                    top = most if top is None else jnp.maximum(top, most)
            m_scr[:, cols] = top

    def soft(n, t_scr, m_scr):
        n = jnp.clip(n, 0, items - 1)
        m = jnp.max(m_scr[...], axis=0, keepdims=True)
        total = None
        for i in range(40):
            e = jnp.exp2((t_scr[16 * i : 16 * i + 16, :] - m) * (SC * LOG2E))
            part = e[:8] + e[8:]
            total = part if total is None else total + part
            p_ref[n // nblk, n % nblk, 16 * i : 16 * i + 16, :] = e.astype(bf)
        inv_ref[n // nblk, n % nblk] = jnp.broadcast_to(1.0 / jnp.sum(total, axis=0, keepdims=True), (8, 256))

    def context(n):
        n = jnp.clip(n, 0, items - 1)
        p, t = n // nblk, n % nblk
        ctxT = own_heads(dot(vT_ref[p, :, window(t)], p_ref[p, t]) * inv_ref[p, t, 0:1, :])
        ctx_ref[p, tile(t), :] = ctxT.astype(bf).T

    half = nblk // 2
    per = keys // half

    def body(m, slot):
        context(2 * m - 2)
        soft(2 * m - 1, t1, m1)
        scores(2 * m, s0, z0, t0, m0)
        context(2 * m - 1)
        soft(2 * m, t0, m0)
        scores(2 * m + 1, s1, z1, t1, m1)
        p, first = jnp.minimum(m // half + 1, PAIRS - 1), per * (m % half)
        for i in range(per):
            keyside(p, first + i, slot + i)
        if hook is not None:
            hook(m)
        return jnp.where(slot + per == 2 * keys, 0, slot + per)

    lax.fori_loop(0, items // 2 + 1, body, jnp.int32(keys))


def unreversed(values, JR):
    high = values.astype(bf)
    low = (values - high.astype(f32)).astype(bf)
    both = dot(JR, jnp.concatenate([high, low], axis=1))
    return both[:, :128] + both[:, 128:]


def att_bwd_body(nblk, q_ref, kT_ref, kTr_ref, v_ref, krtT_ref, qrt_ref, qrtT_ref, dctxT_ref, e_ref, inv_ref, dq_ref, dkc_ref, dkp_ref, dv_ref, dkr_ref, dqr_ref,
                 gt_scr, dp_scr, gm_scr, gb0, gb1, gu0, gu1, e_scr, e_sem, hook):
    row, lane = iotas(128, 128)
    row16, lane16 = iotas(16, 256)
    JR = (row + lane == 127).astype(bf)
    zero = jnp.zeros((128, 128), bf)
    items, keys, half = PAIRS * nblk, nblk + 4, nblk // 2
    per = keys // half
    gt_scr[...] = jnp.zeros(gt_scr.shape, bf)
    gb1[...] = jnp.zeros(gb1.shape, bf)
    gu1[...] = jnp.zeros(gu1.shape, bf)
    for ref in (dkc_ref, dv_ref, dkr_ref, dqr_ref):
        ref[...] = jnp.zeros(ref.shape, f32)

    def kblocks(p, first, base):
        turned = [[], []]
        for i in range(per):
            for h in range(2):
                GT = gt_scr[base + first + i, h]
                Gm = jnp.concatenate([jnp.where(lane > row, GT[:, :128], GT[:, 512:]), GT[:, 128:512]], axis=1)
                turned[h].append(turn_lanes(dot(JR, Gm), 385).astype(bf))
        stacked = [jnp.concatenate(part, axis=0) for part in turned]
        dk = dot(jnp.concatenate(stacked, axis=1), qrt_ref[p])
        for i in range(per):
            dkp_ref[p, tile(first + i), :] = unreversed(dk[128 * i : 128 * i + 128], JR)
        span = pl.ds(pl.multiple_of(first * 128, 128), 128 * per)
        for h in range(2):
            heads = slice(64 * h, 64 * h + 64)
            dqr_ref[p, heads, 0:512] += dot(kTr_ref[p, heads, span], stacked[h])

    def upstream(n, slot, gb, gu, held):
        p, t = n // nblk, n % nblk
        D2 = wide_diagonal(dctxT_ref[p, :, tile(t)])
        inv = inv_ref[p, t, 0:1, :]
        dp_scr[...] = dot(v_ref[p, window(t), :], D2)
        total = None
        for i in range(40):
            rows = slice(16 * i, 16 * i + 16)
            w = e_scr[held, rows, :].astype(f32) * dp_scr[rows, :]
            part = w[:8] + w[8:]
            total = part if total is None else total + part
        less = jnp.sum(total, axis=0, keepdims=True) * inv * inv

        def grad(i):
            rows = slice(16 * i, 16 * i + 16)
            G = e_scr[held, rows, :].astype(f32) * (dp_scr[rows, :] * inv - less)
            Gb = G.astype(bf)
            gb[rows, :] = Gb
            b = i // 8
            for h in range(2):
                gt_scr[slot + b, h, 16 * (i % 8) : 16 * (i % 8) + 16, 128 * (4 - b) : 128 * (5 - b)] = Gb[:, 128 * h : 128 * h + 128]
            return G

        ends = None
        final = None
        for i in range(32):
            G = grad(i)
            if i < 8:
                at = row16 + 16 * i - lane16 % 128
                part = jnp.where(at == 0, G, 0.0)
                part = part[:8] + part[8:]
                ends = part if ends is None else ends + part
                other = grad(32 + i)
                part = jnp.where(at == 0, other, 0.0)
                part = part[:8] + part[8:]
                final = part if final is None else final + part
                G = jnp.where(at > 0, G, other)
            gm_scr[16 * i : 16 * i + 16, :] = G
        ends = jnp.sum(ends, axis=0, keepdims=True)
        final = jnp.sum(final, axis=0, keepdims=True)
        final = jnp.concatenate([jnp.broadcast_to(final[:, :128], (64, 128)), jnp.broadcast_to(final[:, 128:], (64, 128))], axis=0)
        dqr_ref[p, :, 512:640] += kT_ref[p, :, tile(t + 4)].astype(f32) * final
        dkc_ref[p, tile(t + 4), :] += (qrtT_ref[p, :, 512:640].astype(f32) * final).T
        dv_ref[p, window(t), :] += dot(e_scr[held], (D2.astype(f32) * inv).astype(bf).T)
        for h in range(2):
            cols = slice(128 * h, 128 * h + 128)
            held = None
            for i, y in stream_rows(lambda i: gm_scr[8 * i : 8 * i + 8, cols], True, (1, 2, 4)):
                if i == 0:
                    y = y + jnp.where(row[:8] == 1, ends[:, cols], 0.0)
                if i % 2 == 1:
                    held = y
                else:
                    gu[8 * i : 8 * i + 16, cols] = jnp.concatenate([y, held], axis=0).astype(bf)

    def downstream(n, gb, gu):
        n = jnp.maximum(n, 0)
        p, t = n // nblk, n % nblk
        dqT = own_heads(dot(kT_ref[p, :, window(t)], gb[...]) + dot(krtT_ref[p], gu[...]))
        dq_ref[p, tile(t), :] = (SC * dqT).astype(bf).T
        Qm = tall_diagonal(q_ref[p, tile(t), :])
        dkc_ref[p, window(t), :] += dot(gb[...], Qm)
        dkr_ref[p] += dot(gu[...], Qm)

    def fetch(m):
        source = e_ref.at[m // half, pl.ds(2 * (m % half), 2)]
        return pltpu.make_async_copy(source, e_scr.at[pl.ds(2 * (m % 2), 2)], e_sem.at[m % 2])

    def body(m, slot, late):
        p = m // half
        fetch(m).wait()
        pl.when(m + 1 < items // 2)(lambda: fetch(m + 1).start())
        if late:
            kblocks(p - 1, per * (m % half), (1 - p % 2) * keys)
        downstream(2 * m - 1, gb1, gu1)
        upstream(2 * m, slot, gb0, gu0, 2 * (m % 2))
        downstream(2 * m, gb0, gu0)
        upstream(2 * m + 1, slot + 1, gb1, gu1, 2 * (m % 2) + 1)
        hook(m)
        following = slot + 2
        following = jnp.where(following == nblk, keys, following)
        return jnp.where(following == keys + nblk, 0, following)

    fetch(jnp.int32(0)).start()
    slot = lax.fori_loop(0, half, lambda m, slot: body(m, slot, False), jnp.int32(0))
    lax.fori_loop(half, items // 2, lambda m, slot: body(m, slot, True), slot)
    downstream(items - 1, gb1, gu1)

    def last(i, carry):
        kblocks(PAIRS - 1, per * i, ((PAIRS - 1) % 2) * keys)
        return carry

    lax.fori_loop(0, half, last, 0)


def vector(vec_ref, name):
    at, wide = vector_rows()[0][name]
    return jnp.concatenate([vec_ref[at + i : at + i + 1, :] for i in range(wide)], axis=1)


def put_vector(vec_ref, name, value):
    at, wide = vector_rows()[0][name]
    for i in range(wide):
        vec_ref[at + i : at + i + 1, :] = value[:, 128 * i : 128 * i + 128]


def add_vector(vec_ref, name, value):
    at, wide = vector_rows()[0][name]
    for i in range(wide):
        vec_ref[at + i : at + i + 1, :] += value[:, 128 * i : 128 * i + 128]


def normalized(values):
    centered = values - jnp.mean(values, axis=1, keepdims=True)
    inverse = lax.rsqrt(jnp.mean(centered * centered, axis=1, keepdims=True) + EPSILON)
    return centered * inverse, inverse


def norm_back(upstream, gain, unit, inverse):
    scaled = upstream * gain
    mean = jnp.mean(scaled, axis=1, keepdims=True)
    along = jnp.mean(scaled * unit, axis=1, keepdims=True)
    return inverse * (scaled - mean - unit * along)


def column_sum(values):
    return jnp.sum(values, axis=0, keepdims=True)


def reversal():
    row = lax.broadcasted_iota(jnp.int32, (128, 128), 0)
    lane = lax.broadcasted_iota(jnp.int32, (128, 128), 1)
    return (row + lane == 127).astype(bf)


def reversed_rows(values, JR):
    blocks = values.shape[0] // 128
    return jnp.concatenate([dot(JR, values[128 * b : 128 * b + 128]).astype(bf) for b in reversed(range(blocks))], axis=0)


def project_body(x_ref, query_w, key_w, value_w, table_ref, vec_ref, q_ref, qT_ref, k_ref, kT_ref, kTr_ref, v_ref, vT_ref, krt_ref, krtT_ref, qrt_ref, qrtT_ref, pos_ref):
    tokens = q_ref.shape[1]
    JR = reversal()
    lane = iotas(512, 128)[1]
    unit, _ = normalized(table_ref[...].astype(f32))
    pos = (unit * vector(vec_ref, N_REL_GAIN) + vector(vec_ref, N_REL_SHIFT)).astype(bf)
    pos = pltpu.roll(reversed_rows(pos, JR).astype(f32), 1, 0).astype(bf)
    pos_ref[...] = pos
    keys = dot(pos, key_w[...]) + vector(vec_ref, N_KEY_B)
    moved = pltpu.roll(keys, 1, 0).astype(bf)
    keys = keys.astype(bf)
    queries = (dot(pos, query_w[...]) + vector(vec_ref, N_QUERY_B)).astype(bf)
    for p in range(PAIRS):
        cols = slice(128 * p, 128 * p + 128)
        krt_ref[p] = keys[:, cols]
        krt_ref[PAIRS + p] = moved[:, cols]
        krtT_ref[p] = keys[:, cols].T
        qrtT_ref[p, :, 0:512] = queries[:, cols].T
        qrtT_ref[p, :, 512:640] = jnp.broadcast_to(queries[1:2, cols], (128, 128)).T
        zero = jnp.zeros((512, 128), bf)
        qrt_ref[p, 0:512, :] = jnp.where(lane < 64, queries[:, cols], zero)
        qrt_ref[p, 512:1024, :] = jnp.where(lane < 64, zero, queries[:, cols])
    bias = {name: vector(vec_ref, name) for name in (N_QUERY_B, N_KEY_B, N_VALUE_B)}

    def chunk(i, carry):
        rows = pl.ds(pl.multiple_of(i * 256, 256), 256)
        x = x_ref[rows, :]
        y = (dot(x, key_w[...]) + bias[N_KEY_B]).astype(bf)
        w = (dot(x, value_w[...]) + bias[N_VALUE_B]).astype(bf)
        for p in range(PAIRS):
            cols = slice(128 * p, 128 * p + 128)
            k_ref[p, rows, :] = y[:, cols]
            turned = y[:, cols].T
            kT_ref[p, :, rows] = turned
            kTr_ref[p, :, rows] = jnp.concatenate([dot(turned[:, :128], JR), dot(turned[:, 128:], JR)], axis=1).astype(bf)
            v_ref[p, rows, :] = w[:, cols]
            vT_ref[p, :, rows] = w[:, cols].T
        return carry

    lax.fori_loop(0, x_ref.shape[0] // 256, chunk, 0)

    def own(i, carry):
        rows = pl.ds(pl.multiple_of(i * 256, 256), 256)
        x = x_ref[pl.ds(pl.multiple_of(i * 256 + SPAN, 256), 256), :]
        y = (dot(x, query_w[...]) + bias[N_QUERY_B]).astype(bf)
        for p in range(PAIRS):
            q_ref[p, rows, :] = y[:, 128 * p : 128 * p + 128]
            qT_ref[p, :, rows] = y[:, 128 * p : 128 * p + 128].T
        return carry

    lax.fori_loop(0, tokens // 256, own, 0)


SQRT_HALF = 0.7071067811865476
PHI_SCALE = 0.3989422804014327


def gelu_and_slope(u):
    cdf = 0.5 + 0.5 * lax.erf(u * SQRT_HALF)
    return u * cdf, cdf + u * (PHI_SCALE * jnp.exp(-0.5 * u * u))


def feed_body(x_ref, ctx_ref, og_ref, output_w, up_w, down_w, vec_ref, out_ref, dz1_ref, dctx_ref, wide, dvec_ref,
              ml_scr, dup_scr, act_scr, ddown_scr, dattn_scr, slope_scr):
    tokens = out_ref.shape[0]
    dvec_ref[...] = jnp.zeros(dvec_ref.shape, f32)
    vecs = {name: vector(vec_ref, name) for name in (N_OUTPUT_B, N_ATTN_GAIN, N_ATTN_SHIFT, N_UP_BIAS, N_DOWN_BIAS, N_FFN_GAIN, N_FFN_SHIFT)}
    C = 256

    def chunk(i, carry):
        rows = pl.ds(pl.multiple_of(i * C, C), C)
        h = x_ref[pl.ds(pl.multiple_of(i * C + SPAN, C), C), :].astype(f32)
        z1 = h + dot(jnp.concatenate([ctx_ref[p, rows, :] for p in range(PAIRS)], axis=1), output_w[...]) + vecs[N_OUTPUT_B]
        unit1, inv1 = normalized(z1)
        mid = unit1 * vecs[N_ATTN_GAIN] + vecs[N_ATTN_SHIFT]
        ml = mid.astype(bf)
        ml_scr[rows, :] = ml
        z2 = mid + vecs[N_DOWN_BIAS]
        for f in range(FF // 256):
            cols = slice(256 * f, 256 * f + 256)
            up = dot(ml, up_w[:, cols]) + vecs[N_UP_BIAS][:, cols]
            act, slope = gelu_and_slope(up)
            act_scr[rows, cols] = act.astype(bf)
            slope_scr[:, cols] = slope
        z2 = z2 + dot(act_scr[rows, :], down_w[...])
        unit2, inv2 = normalized(z2)
        out_ref[rows, :] = (unit2 * vecs[N_FFN_GAIN] + vecs[N_FFN_SHIFT]).astype(bf)
        dh = og_ref[rows, :].astype(f32)
        add_vector(dvec_ref, N_FFN_GAIN, column_sum(dh * unit2))
        add_vector(dvec_ref, N_FFN_SHIFT, column_sum(dh))
        dz2 = norm_back(dh, vecs[N_FFN_GAIN], unit2, inv2)
        ddown = dz2.astype(bf)
        ddown_scr[rows, :] = ddown
        add_vector(dvec_ref, N_DOWN_BIAS, column_sum(ddown.astype(f32)))
        for f in range(FF // 256):
            cols = slice(256 * f, 256 * f + 256)
            dup = (dot(ddown, down_w[cols, :], NT) * slope_scr[:, cols]).astype(bf)
            dup_scr[rows, cols] = dup
        add_vector(dvec_ref, N_UP_BIAS, column_sum(dup_scr[rows, :].astype(f32)))
        dmid = dz2 + dot(dup_scr[rows, :], up_w[...], NT)
        add_vector(dvec_ref, N_ATTN_GAIN, column_sum(dmid * unit1))
        add_vector(dvec_ref, N_ATTN_SHIFT, column_sum(dmid))
        dz1 = norm_back(dmid, vecs[N_ATTN_GAIN], unit1, inv1)
        dz1_ref[rows, :] = dz1
        dattn = dz1.astype(bf)
        dattn_scr[rows, :] = dattn
        add_vector(dvec_ref, N_OUTPUT_B, column_sum(dattn.astype(f32)))
        dctx = dot(dattn, output_w[...], NT).astype(bf)
        for p in range(PAIRS):
            dctx_ref[p, :, rows] = dctx[:, 128 * p : 128 * p + 128].T
        return carry

    lax.fori_loop(0, tokens // C, chunk, 0)
    place = matrix_rows()

    def put(name, first, rows, value):
        base, _, pieces = place[name]
        for c in range(value.shape[1] // 128):
            wide[pl.ds(base - FEED_FIRST + pieces * first[0] + first[1] + c, rows, stride=pieces), :] = value[:, 128 * c : 128 * c + 128]

    ctx = jnp.concatenate([ctx_ref[p] for p in range(PAIRS)], axis=1)
    put(N_OUTPUT_W, (0, 0), D, dot(ctx, dattn_scr[...], TN))
    for f in range(FF // 256):
        cols = slice(256 * f, 256 * f + 256)
        put(N_UP_W, (0, 2 * f), D, dot(ml_scr[...], dup_scr[:, cols], TN))
        put(N_DOWN_W, (256 * f, 0), 256, dot(act_scr[:, cols], ddown_scr[...], TN))


def split(values):
    high = values.astype(bf)
    return high, (values - high.astype(f32)).astype(bf)


def dot2(left, right, dims=NN):
    if left.dtype == f32:
        return sum(dot(part, right, dims) for part in split(left))
    return sum(dot(left, part, dims) for part in split(right))


def tail_local(dq_ref, x_ref, query_w, dx_ref, dwq_ref, dvec_ref):
    tokens = dx_ref.shape[0]
    dq = jnp.concatenate([dq_ref[p] for p in range(PAIRS)], axis=1)
    dx_ref[...] += dot(dq, query_w[...], NT)
    dwq_ref[...] = dot(x_ref[...], dq, TN)
    put_vector(dvec_ref, N_QUERY_B, column_sum(dq.astype(f32)))


def tail_table(dkr_ref, dqr_ref, pos_ref, table_ref, vec_ref, query_w, key_w, dwq_ref, dwk_ref, dtable_ref, dvec_ref):
    JR = reversal()
    second = iotas(512, 128)[0] == 1
    tabs = {N_KEY_B: jnp.concatenate([SC * dkr_ref[p] for p in range(PAIRS)], axis=1)}
    parts = []
    for p in range(PAIRS):
        part = dqr_ref[p].T
        parts.append(SC * (part[:512] + jnp.where(second, column_sum(part[512:]), 0.0)))
    tabs[N_QUERY_B] = jnp.concatenate(parts, axis=1)
    dpos = None
    for w, dw, name in ((key_w, dwk_ref, N_KEY_B), (query_w, dwq_ref, N_QUERY_B)):
        tab = tabs[name]
        if name == N_KEY_B:
            dw[...] = dot2(pos_ref[...], tab, TN)
            put_vector(dvec_ref, name, column_sum(tab))
        else:
            dw[...] += dot2(pos_ref[...], tab, TN)
            add_vector(dvec_ref, name, column_sum(tab))
        part = dot2(tab, w[...], NT)
        dpos = part if dpos is None else dpos + part
    table = jnp.concatenate([dot(JR, table_ref[128 * b : 128 * b + 128, :]) for b in reversed(range(4))], axis=0)
    unit, inverse = normalized(pltpu.roll(table, 1, 0))
    put_vector(dvec_ref, N_REL_GAIN, column_sum(dpos * unit))
    put_vector(dvec_ref, N_REL_SHIFT, column_sum(dpos))
    dpos = pltpu.roll(norm_back(dpos, vector(vec_ref, N_REL_GAIN), unit, inverse), 511, 0).astype(bf)
    for b in range(4):
        dtable_ref[128 * b : 128 * b + 128, :] = dot(JR, dpos[128 * (3 - b) : 128 * (4 - b)])


def tail_keys(dkc_ref, dkp_ref, dv_ref, halo_ref, x_ref, key_w, value_w, dx_ref, dwk_ref, dwv_ref, dvec_ref):
    tokens = dx_ref.shape[0]
    x = x_ref[...]
    for which, (ref, w, dw, name) in enumerate(((None, key_w, dwk_ref, N_KEY_B), (dv_ref, value_w, dwv_ref, N_VALUE_B))):
        pieces = []
        for p in range(PAIRS):
            middle = slice(SPAN, SPAN + tokens)
            own = SC * (dkc_ref[p, middle, :] + dkp_ref[p, middle, :]) if ref is None else ref[p, middle, :]
            edge = [halo_ref[side, which, p].astype(f32) for side in (0, 1)]
            pieces.append(jnp.concatenate([own[:SPAN] + edge[0], own[SPAN : tokens - SPAN], own[tokens - SPAN :] + edge[1]], axis=0).astype(bf))
        d = jnp.concatenate(pieces, axis=1)
        dx_ref[...] += dot(d, w[...], NT)
        if name == N_KEY_B:
            dw[...] += dot(x, d, TN)
            add_vector(dvec_ref, name, column_sum(d.astype(f32)))
        else:
            dw[...] = dot(x, d, TN)
            put_vector(dvec_ref, name, column_sum(d.astype(f32)))


def beside(grid, step):
    return {"seq": lax.axis_index("seq") + step, "row": lax.axis_index("row")}


def seq_edges(grid):
    s = lax.axis_index("seq")
    return s > 0, s < grid.seq - 1


def enter_all(grid, p, straight=False):
    sem = pltpu.get_barrier_semaphore()
    total = jnp.int32(0)
    before, after = seq_edges(grid)
    targets = [(grid.device(q), cond) for _, q, cond in neighbours_of(grid, p)]
    if straight:
        for d in range(2, grid.size["z"]):
            targets += [(grid.device(dict(p, z=p["z"] - d)), p["z"] - d >= 0), (grid.device(dict(p, z=p["z"] + d)), p["z"] + d < grid.size["z"])]
    targets += [(beside(grid, -1), before), (beside(grid, 1), after)]
    for device, cond in targets:
        guarded(cond, lambda device=device: pl.semaphore_signal(sem, inc=1, device_id=device, device_id_type=MESH))
        total = total + (1 if cond is None else cond.astype(jnp.int32))
    pl.semaphore_wait(sem, total)


def remote(source, target, send_sem, recv_sem, device):
    return pltpu.make_async_remote_copy(
        src_ref=source, dst_ref=target, send_sem=send_sem, recv_sem=recv_sem, device_id=device, device_id_type=MESH)


def assemble(grid, shard, slots, wide, first, final):
    for k in range(grid.count):
        low, high = shard * k // GROUP, -(-shard * (k + 1) // GROUP)
        shared = k + 1 < grid.count and shard * (k + 1) % GROUP != 0
        begin = max(first, low + (1 if k > 0 and shard * k % GROUP != 0 else 0))
        end = min(final, high - (1 if shared else 0))
        block = slots.at[grid.place(k)]
        if end > begin:
            wide[16 * (begin - first) : 16 * (end - first), :] = block[16 * (begin - low) : 16 * (end - low), :].astype(f32)
        if shared and first <= high - 1 < final:
            at = high - 1
            both_parts = block[16 * (at - low) : 16 * (at - low) + 16, :].astype(f32) + slots.at[grid.place(k + 1)][0:16, :].astype(f32)
            wide[16 * (at - first) : 16 * (at - first) + 16, :] = both_parts


def unpack(wide, first, outs):
    place = matrix_rows()
    for name, out in outs.items():
        base, rows, pieces = place[name]
        for c in range(pieces):
            out[:, 128 * c : 128 * c + 128] = wide[pl.ds(base - 16 * first + c, rows, stride=pieces), :].astype(bf)


VMEM = pl.BlockSpec(memory_space=pltpu.VMEM)
ANY = pl.BlockSpec(memory_space=pl.ANY)
FEED_FROM, FEED_TO = FEED_FIRST * 128, (FEED_FIRST + FEED_ROWS) * 128
LATE = (N_OUTPUT_W, N_UP_W, N_DOWN_W)


def projected(T):
    shape = jax.ShapeDtypeStruct
    E = T + 2 * SPAN
    natural = {N_Q: (T, 128), N_Q_TURNED: (128, T), N_K: (E, 128), N_K_TURNED: (128, E), N_K_TURNED_BACK: (128, E), N_V: (E, 128), N_V_TURNED: (128, E)}
    tables = {N_KRT: (512, 128), N_KRT_TURNED: (128, 512), N_QRT: (1024, 128), N_QRT_TURNED: (128, 640)}
    out = {name: shape((PAIRS,) + extent, bf) for name, extent in (natural | tables).items()}
    out[N_KRT] = shape((2 * PAIRS, 512, 128), bf)
    out[N_POS] = shape((512, D), bf)
    out[N_CTX] = shape((PAIRS, T, 128), bf)
    out[N_E] = shape((PAIRS, T // 128, 640, 256), bf)
    out[N_INV] = shape((PAIRS, T // 128, 8, 256), f32)
    return out


def front_outputs(T):
    shape = jax.ShapeDtypeStruct
    proj = projected(T)
    place = matrix_rows()
    out = {name: proj[name] for name in (N_Q, N_K_TURNED, N_K_TURNED_BACK, N_V, N_KRT_TURNED, N_QRT, N_QRT_TURNED, N_POS, N_E, N_INV)}
    for name in (N_QUERY_W, N_KEY_W, N_VALUE_W, N_REL_TABLE):
        out[name] = shape((place[name][1], 128 * place[name][2]), bf)
    out[N_VEC] = shape((vector_rows()[1], 128), f32)
    out[N_OUT] = shape((T, D), bf)
    out[N_DZ1] = shape((T, D), f32)
    out[N_DCTX_TURNED] = shape((PAIRS, 128, T), bf)
    out[N_DFLAT] = shape((FEED_ROWS, 128), bf)
    out[N_DVEC] = shape((vector_rows()[1], 128), f32)
    return out


def front_held(T):
    shape = jax.ShapeDtypeStruct
    proj = projected(T)
    place = matrix_rows()
    held = {name: proj[name] for name in (N_Q_TURNED, N_K, N_V_TURNED, N_KRT, N_CTX)}
    for name in LATE:
        held[name] = shape((place[name][1], 128 * place[name][2]), bf)
    held[N_X_EXT] = shape((T + 2 * SPAN, D), bf)
    held[N_SEG_EXT] = shape((8, T + 2 * SPAN), jnp.int32)
    return held


def shifted_block(values, shift):
    lane = iotas(*values.shape)[1]
    moved = pltpu.roll(values, shift % 128, 1)
    moved = jnp.where(lane < shift % 128, pltpu.roll(moved, 1, 0), moved)
    return pltpu.roll(moved, shift // 128, 0)


def middle_stages(grid, p, slots, send_sem, recv_sem, groups):
    top = grid.size["z"] - 1
    z, y, c, x = p["z"], p["y"], p["c"], p["x"]
    inner = pl.ds(1, top - 1)
    half = 16 * (groups // 2)
    halves = (pl.ds(0, half), pl.ds(half, 16 * groups - half))
    middle = lambda at: jnp.logical_and(at > 0, at < top)
    flips = {axis: dict(p, **{axis: 1 - p[axis]}) for axis in ("y", "c", "x")}

    def line(at, up):
        block = slots.at[at, y, c, x]
        q = dict(p, z=z + (1 if up else -1))
        return remote(block, block, send_sem.at[1 if up else 0, at], recv_sem.at[at], grid.device(q))

    def sends(distance):
        found = [(both([middle(z - distance), z < top]), line(z - distance, True))]
        found.append((both([middle(z + distance), z > 0]), line(z + distance, False)))
        return found

    def take(distance):
        for at in (z - distance, z + distance):
            pl.when(middle(at))(lambda at=at: line(at, True).wait_recv())

    def pass_on(distance):
        for cond, copy in sends(distance):
            pl.when(cond)(copy.start)

    def across(i, first):
        axis = ("y", "x")[i] if first else ("x", "y")[i]
        part = (y, c, x) if first else ((y, c, slice(None)) if axis == "y" else (slice(None), c, x))
        block = slots.at[(inner,) + part + (halves[i], slice(None))]
        at = top + 1 + 2 * i + (0 if first else 1)
        return remote(block, block, send_sem.at[i, top + 1 + (0 if first else 1)], recv_sem.at[at], grid.device(flips[axis]))

    def hand_over():
        block = slots.at[inner, :, c]
        return remote(block, block, send_sem.at[0, top + 3], recv_sem.at[top + 5], grid.device(flips["c"]))

    def begin():
        pass_on(0)

    def second():
        take(1)
        pass_on(1)

    def third():
        for distance in range(2, top):
            take(distance)
            if distance < top - 1:
                pass_on(distance)
        for i in (0, 1):
            across(i, True).start()

    def fourth():
        for i in (0, 1):
            across(i, True).wait_recv()
        for i in (0, 1):
            across(i, False).start()

    def fifth():
        for i in (0, 1):
            across(i, False).wait_recv()
        hand_over().start()

    def finish():
        hand_over().wait_recv()
        hand_over().wait_send()
        for i in (0, 1):
            across(i, True).wait_send()
            across(i, False).wait_send()
        for distance in range(top - 1):
            for cond, copy in sends(distance):
                pl.when(cond)(copy.wait_send)

    return [begin, second, third, fourth, fifth, finish]


def front_kernel(grid, shard, slot_ref, seg_ref, x_any, og_any, *refs):
    tokens = x_any.shape[0]
    blocks = tokens // 128
    outs, held = front_outputs(tokens), front_held(tokens)
    target = dict(zip(outs, refs))
    names = list(outs) + list(held)
    here = dict(zip(names, refs[len(outs) :]))
    slots, og_ref, local_sem, out_sem, send_sem, recv_sem, late_send, late_recv, halo_send, halo_recv = refs[len(outs) + len(names) :]
    p = grid.here()
    _, groups = shard_groups(shard, grid.count)
    before, after = seq_edges(grid)
    early = lambda o: jnp.logical_or(o["z"] == 0, o["z"] == grid.size["z"] - 1)
    x_ext, seg_ext = here[N_X_EXT], here[N_SEG_EXT]
    own = pltpu.make_async_copy(x_any, x_ext.at[pl.ds(SPAN, tokens), :], local_sem.at[0])
    own.start()
    og_load = pltpu.make_async_copy(og_any, og_ref, local_sem.at[1])
    og_load.start()
    if grid.split:
        k = grid.flat(p)
        slots[p["z"], p["y"], p["c"], p["x"]] = shifted_block(slot_ref[...], k * shard % GROUP).astype(bf)
    else:
        for k in range(grid.count):
            slots[grid.place(k)] = slot_ref[k]
    seg_ext[:, SPAN : SPAN + tokens] = jnp.broadcast_to(seg_ref[...] + 1, (8, tokens))
    enter_all(grid, p)
    own.wait()

    def halo_copies(side):
        step = -1 if side == 0 else 1
        take = pl.ds(SPAN, SPAN) if side == 0 else pl.ds(tokens, SPAN)
        land = pl.ds(tokens + SPAN, SPAN) if side == 0 else pl.ds(0, SPAN)
        return [
            remote(x_ext.at[take, :], x_ext.at[land, :], halo_send.at[side, 0], halo_recv.at[side, 0], beside(grid, step)),
            remote(seg_ext.at[:, take], seg_ext.at[:, land], halo_send.at[side, 1], halo_recv.at[side, 1], beside(grid, step)),
        ]

    def start(side):
        for copy in halo_copies(side):
            copy.start()

    def sent(side):
        for copy in halo_copies(side):
            copy.wait_send()

    def landed(side):
        for copy in halo_copies(side):
            copy.wait_recv()

    first_levels, first_partners, first_ends = ([[]], [], [])
    stages = [lambda: None]
    if grid.split:
        gather = Gather(grid, p, slots, send_sem, recv_sem, groups)
        first_levels, first_partners, first_ends = gather.plan(early, False, 0)
        stages = middle_stages(grid, p, slots, late_send, late_recv, groups)
    perform(first_levels[0])
    pl.when(before)(lambda: start(0))
    pl.when(after)(lambda: start(1))

    def clear(rows):
        x_ext[rows, :] = jnp.zeros((SPAN, D), bf)
        seg_ext[:, rows] = jnp.zeros((8, SPAN), jnp.int32)

    pl.when(jnp.logical_not(before))(lambda: clear(pl.ds(0, SPAN)))
    pl.when(jnp.logical_not(after))(lambda: clear(pl.ds(tokens + SPAN, SPAN)))
    for level in first_levels[1:]:
        perform(level)
    perform(first_partners)
    perform(first_ends)
    place = matrix_rows()
    feed_group, end_group = FEED_FIRST // 16, (FEED_FIRST + FEED_ROWS) // 16
    all_groups = flat_rows(shard, grid.count) // 16

    def first_part(wide):
        assemble(grid, shard, slots, wide, 0, feed_group)
        unpack(wide, 0, {name: here[name] for name in (N_QUERY_W, N_KEY_W, N_VALUE_W)})
        assemble(grid, shard, slots, wide, end_group, all_groups)
        unpack(wide, end_group, {N_REL_TABLE: here[N_REL_TABLE]})
        vec_at, vec_total = vector_rows()
        here[N_VEC][...] = jnp.zeros((vec_total, 128), f32)
        for name in VECTORS:
            base, _, pieces = place[name]
            at = base - 16 * end_group
            here[N_VEC][vec_at[name][0] : vec_at[name][0] + pieces, :] = wide[at : at + pieces, :]

    pl.run_scoped(first_part, pltpu.VMEM((16 * max(feed_group, all_groups - end_group), 128), f32))
    pl.when(before)(lambda: sent(0))
    pl.when(after)(lambda: sent(1))
    pl.when(after)(lambda: landed(0))
    pl.when(before)(lambda: landed(1))
    stages[0]()
    project_body(x_ext, *[here[n] for n in (N_QUERY_W, N_KEY_W, N_VALUE_W, N_REL_TABLE, N_VEC, N_Q, N_Q_TURNED, N_K, N_K_TURNED, N_K_TURNED_BACK, N_V, N_V_TURNED, N_KRT, N_KRT_TURNED, N_QRT, N_QRT_TURNED, N_POS)])

    def hook(m):
        for at, stage in zip((0, 2, 4, 8), stages[1:-1]):
            pl.when(m == at)(stage)

    def attend(*scratch):
        att_fwd_body(blocks, *[here[n] for n in (N_Q_TURNED, N_K, N_V_TURNED, N_KRT, N_QRT_TURNED, N_SEG_EXT, N_CTX, N_E, N_INV)], *scratch, hook)

    pl.run_scoped(attend, pltpu.VMEM((2 * (blocks + 4), 2, 128, 640), bf), pltpu.VMEM((blocks, 640, 128), f32), *FORWARD_SCRATCH)
    leaving = {name: pltpu.make_async_copy(here[name], target[name], out_sem.at[i]) for i, name in enumerate(outs)}
    finished = (N_OUT, N_DZ1, N_DCTX_TURNED, N_DFLAT, N_DVEC)
    for name in outs:
        if name not in finished:
            leaving[name].start()
    stages[-1]()

    def second_part(wide):
        assemble(grid, shard, slots, wide, feed_group, end_group)
        unpack(wide, feed_group, {name: here[name] for name in LATE})

    pl.run_scoped(second_part, pltpu.VMEM((FEED_ROWS, 128), f32))

    og_load.wait()

    def feed_part(wide, *scratch):
        feed_body(*[x_ext, here[N_CTX], og_ref] + [here[n] for n in LATE + (N_VEC, N_OUT, N_DZ1, N_DCTX_TURNED)], wide, here[N_DVEC], *scratch)
        here[N_DFLAT][...] = wide[...].astype(bf)

    pl.run_scoped(
        feed_part, pltpu.VMEM((FEED_ROWS, 128), f32), pltpu.VMEM((tokens, D), bf), pltpu.VMEM((tokens, FF), bf), pltpu.VMEM((tokens, FF), bf),
        pltpu.VMEM((tokens, D), bf), pltpu.VMEM((tokens, D), bf), pltpu.VMEM((256, FF), f32))
    for name in finished:
        leaving[name].start()
    for name in outs:
        leaving[name].wait()


FORWARD_SCRATCH = (
    [pltpu.VMEM((640, 256), f32)] * 2 + [pltpu.VMEM((512, 256), f32)] * 2 + [pltpu.VMEM((640, 256), f32)] * 2 + [pltpu.VMEM((8, 256), f32)] * 2
)


def front(grid, shard, slot, x, seg, out_grad):
    tokens = x.shape[0]
    _, groups = shard_groups(shard, grid.count)
    outs, held = front_outputs(tokens), front_held(tokens)
    if not grid.split:
        slot = lax.all_gather(slot, ("seq", "row"))
    results = pl.pallas_call(
        functools.partial(front_kernel, grid, shard),
        out_shape=list(outs.values()),
        in_specs=[VMEM, VMEM, ANY, ANY],
        out_specs=[ANY] * len(outs),
        scratch_shapes=[pltpu.VMEM(a.shape, a.dtype) for a in list(outs.values()) + list(held.values())]
        + [
            pltpu.VMEM((grid.size["z"], grid.size["y"], 2, grid.size["x"], 16 * groups, 128), bf),
            pltpu.VMEM((tokens, D), bf),
            pltpu.SemaphoreType.DMA((2,)),
            pltpu.SemaphoreType.DMA((len(outs),)),
            pltpu.SemaphoreType.DMA((count_sends(grid, groups, False) if grid.split else 1,)),
            pltpu.SemaphoreType.DMA((2, grid.count)),
            pltpu.SemaphoreType.DMA((2, grid.size["z"] + 3)),
            pltpu.SemaphoreType.DMA((grid.size["z"] + 5,)),
            pltpu.SemaphoreType.DMA((2, 2)),
            pltpu.SemaphoreType.DMA((2, 2)),
        ],
        compiler_params=pltpu.CompilerParams(collective_id=0, has_side_effects=True, vmem_limit_bytes=62 << 20),
    )(slot, seg, x, out_grad)
    return dict(zip(outs, results))


def back_scratch(grid, shard, tokens):
    _, groups = shard_groups(shard, grid.count)
    rows = flat_rows(shard, grid.count)
    names, half, blocks = 3 + grid.size["z"], (grid.count // 2 if grid.split else 1), tokens // 128
    square = pltpu.VMEM((D, D), bf)
    accumulator = pltpu.VMEM((PAIRS, tokens + 2 * SPAN, 128), f32)
    rim = pltpu.VMEM((2, 2, PAIRS, SPAN, 128), bf)
    return (
        [square, square, square, pltpu.VMEM((2 * SPAN, D), bf), pltpu.VMEM((512, D), bf), pltpu.VMEM((tokens, D), bf), pltpu.VMEM((tokens, D), f32)]
        + [pltpu.VMEM((PAIRS, tokens, 128), bf), accumulator, accumulator, accumulator, pltpu.VMEM((PAIRS, 512, 128), f32), pltpu.VMEM((PAIRS, 128, 640), f32)]
        + [pltpu.VMEM((2 * (blocks + 4), 2, 128, 640), bf), pltpu.VMEM((640, 256), f32), pltpu.VMEM((512, 256), f32)]
        + [pltpu.VMEM((640, 256), bf)] * 2 + [pltpu.VMEM((512, 256), bf)] * 2 + [pltpu.VMEM((4, 640, 256), bf), pltpu.SemaphoreType.DMA((2,))]
        + [pltpu.VMEM((D, D), f32)] * 3 + [pltpu.VMEM((2 * SPAN, D), f32), pltpu.VMEM((vector_rows()[1], 128), f32)]
        + [pltpu.VMEM((max(3 * D, rows - FEED_FIRST - FEED_ROWS), 128), f32), pltpu.VMEM((rows, 128), bf)]
        + [pltpu.VMEM((names, half, 16 * groups, 128), bf), pltpu.VMEM((16 * groups, 128), f32)]
        + [rim, rim, pltpu.SemaphoreType.DMA((8,)), pltpu.SemaphoreType.DMA((scatter_sends(grid, groups, True) + 48 if grid.split else 1,))]
        + [pltpu.SemaphoreType.DMA((2, names, half)), pltpu.SemaphoreType.DMA((2,)), pltpu.SemaphoreType.DMA((2,))]
    )


def back_kernel(grid, shard, q_ref, kT_ref, kTr_ref, v_ref, krtT_ref, qrt_ref, qrtT_ref, dctxT_ref, e_ref, inv_ref, vec_ref, dvec_in, *refs):
    sources, (dx_out, sum_ref) = refs[:8], refs[8:10]
    query_w, key_w, value_w, table_ref, pos_ref, x_ref, dx_ref = refs[10:17]
    dq, dkc, dkp, dv, dkr, dqr = refs[17:23]
    work = refs[23:32]
    dwq, dwk, dwv, dtable, dvec_ref, wide, flat, kids, total, halo_out, halo_in, load_sem, send_sem, recv_sem, halo_send, halo_recv = refs[32:]
    p = grid.here()
    tokens = dx_ref.shape[0]
    blocks = tokens // 128
    _, groups = shard_groups(shard, grid.count)
    before, after = seq_edges(grid)
    feed = pl.ds(FEED_FIRST, FEED_ROWS)
    targets = (flat.at[feed, :], query_w, key_w, value_w, table_ref, pos_ref, x_ref, dx_ref)
    loads = [pltpu.make_async_copy(source, target, load_sem.at[i]) for i, (source, target) in enumerate(zip(sources, targets))]
    for load in loads:
        load.start()
    enter_all(grid, p, True)
    first_row = lambda k: (k * shard // GROUP) * 16
    early = lambda k: jnp.logical_and(first_row(k) >= FEED_FIRST, first_row(k) + 16 * groups <= FEED_FIRST + FEED_ROWS)
    gifts, levels, ends, last_gifts, last_steps, last_ends = ([], [], [], [], [], [])
    if grid.split:
        scatter = lambda: Scatter(grid, p, flat, first_row, kids, total, send_sem, recv_sem, groups)
        gifts, levels, ends = scatter().plan(sum_ref, early, True, 0)
        last_gifts, last_steps, last_ends = scatter().plan_outer(sum_ref, lambda k: jnp.logical_not(early(k)), scatter_sends(grid, groups, True))
    loads[0].wait()
    perform(gifts)

    def hook(m):
        for i, level in enumerate(levels):
            pl.when(m == min(3 * i + 1, PAIRS * blocks // 2 - 1))(lambda level=level: perform(level))

    att_bwd_body(blocks, q_ref, kT_ref, kTr_ref, v_ref, krtT_ref, qrt_ref, qrtT_ref, dctxT_ref, e_ref, inv_ref, dq, dkc, dkp, dv, dkr, dqr, *work, hook)
    rims = (pl.ds(0, SPAN), pl.ds(tokens + SPAN, SPAN))
    for side in (0, 1):
        halo_out[side, 0] = (SC * (dkc[:, rims[side], :] + dkp[:, rims[side], :])).astype(bf)
        halo_out[side, 1] = dv[:, rims[side], :].astype(bf)

    def halo_copy(side):
        return remote(halo_out.at[side], halo_in.at[1 - side], halo_send.at[side], halo_recv.at[1 - side], beside(grid, -1 if side == 0 else 1))

    pl.when(before)(lambda: halo_copy(0).start())
    pl.when(after)(lambda: halo_copy(1).start())

    def clear(side):
        halo_in[side] = jnp.zeros(halo_in.shape[1:], bf)

    pl.when(jnp.logical_not(before))(lambda: clear(0))
    pl.when(jnp.logical_not(after))(lambda: clear(1))
    for load in loads[1:]:
        load.wait()
    dvec_ref[...] = dvec_in[...]
    tail_local(dq, x_ref, query_w, dx_ref, dwq, dvec_ref)
    tail_table(dkr, dqr, pos_ref, table_ref, vec_ref, query_w, key_w, dwq, dwk, dtable, dvec_ref)
    pl.when(before)(lambda: halo_copy(0).wait_send())
    pl.when(after)(lambda: halo_copy(1).wait_send())
    pl.when(before)(lambda: halo_copy(1).wait_recv())
    pl.when(after)(lambda: halo_copy(0).wait_recv())
    tail_keys(dkc, dkp, dv, halo_in, x_ref, key_w, value_w, dx_ref, dwk, dwv, dvec_ref)
    leave = pltpu.make_async_copy(dx_ref, dx_out, load_sem.at[0])
    leave.start()
    place = matrix_rows()
    vec_at, _ = vector_rows()
    final = FEED_FIRST + FEED_ROWS
    for name, ref in ((N_QUERY_W, dwq), (N_KEY_W, dwk), (N_VALUE_W, dwv)):
        base, rows, pieces = place[name]
        for c in range(pieces):
            wide[pl.ds(c, rows, stride=pieces), :] = ref[:, 128 * c : 128 * c + 128]
        flat[base : base + rows * pieces, :] = wide[0 : rows * pieces, :].astype(bf)
    rest = flat.shape[0] - final
    wide[0:rest, :] = jnp.zeros((rest, 128), f32)
    base, rows, pieces = place[N_REL_TABLE]
    for c in range(pieces):
        wide[pl.ds(base - final + c, rows, stride=pieces), :] = dtable[:, 128 * c : 128 * c + 128]
    for name in VECTORS:
        base, _, pieces = place[name]
        wide[base - final : base - final + pieces, :] = dvec_ref[vec_at[name][0] : vec_at[name][0] + pieces, :]
    flat[final:, :] = wide[0:rest, :].astype(bf)
    if not grid.split:
        sum_ref[...] = flat[...]
    perform(last_gifts)
    perform(last_steps)
    perform(ends)
    perform(last_ends)
    leave.wait()


def back(grid, shard, f, x):
    _, groups = shard_groups(shard, grid.count)
    tokens = x.shape[0]
    shape = jax.ShapeDtypeStruct
    leaving = shape((16 * groups, 128), f32) if grid.split else shape((flat_rows(shard, grid.count), 128), bf)
    dx, summed = pl.pallas_call(
        functools.partial(back_kernel, grid, shard),
        out_shape=[shape((tokens, D), f32), leaving],
        in_specs=[VMEM] * 8 + [ANY] + [VMEM] * 3 + [ANY] * 8,
        out_specs=[ANY, VMEM],
        scratch_shapes=back_scratch(grid, shard, tokens),
        compiler_params=pltpu.CompilerParams(collective_id=1, has_side_effects=True, vmem_limit_bytes=62 << 20),
    )(
        *[f[n] for n in (N_Q, N_K_TURNED, N_K_TURNED_BACK, N_V, N_KRT_TURNED, N_QRT, N_QRT_TURNED, N_DCTX_TURNED, N_E, N_INV, N_VEC, N_DVEC)],
        *[f[n] for n in (N_DFLAT, N_QUERY_W, N_KEY_W, N_VALUE_W, N_REL_TABLE, N_POS)], x, f[N_DZ1])
    if not grid.split:
        first, _ = shard_groups(shard, grid.count)
        pieces = jnp.concatenate([summed[16 * at : 16 * (at + groups)] for at in first], axis=0)
        summed = lax.psum_scatter(pieces.astype(f32), ("seq", "row"), scatter_dimension=0, tiled=True)
    return dx, summed


def on_device(layer_input, segment_ids, out_grad, weights, momentum, average):
    tokens_here = layer_input.shape[1]
    grid = Grid(lax.axis_size("seq"), lax.axis_size("row"))
    shard = weights.shape[0]
    _, groups = shard_groups(shard, grid.count)
    shift = (lax.axis_index("seq") * grid.row + lax.axis_index("row")) * shard % GROUP
    slot = jnp.pad(weights, (0, GROUP * groups - shard)).reshape(16 * groups, 128)
    if not grid.split:
        slot = lax.dynamic_update_slice(jnp.zeros((GROUP * groups,), bf), weights.astype(bf), (shift,)).reshape(16 * groups, 128)
    f = front(grid, shard, slot, layer_input[0], segment_ids, out_grad[0])
    block_output = f[N_OUT]
    dx, summed = back(grid, shard, f, layer_input[0])
    weight_grad = lax.dynamic_slice(summed.reshape(-1), (shift,), (shard,))
    all_tokens = tokens_here * grid.seq * layer_input.shape[0] * grid.row
    rate = 0.1 / math.sqrt(all_tokens)
    new_momentum = 0.5 * momentum + weight_grad
    new_weights = weights - rate * (weight_grad + 0.5 * new_momentum)
    new_average = 0.5 * average + 0.5 * new_weights
    return (
        block_output[None],
        dx[None],
        weight_grad,
        new_momentum,
        new_average,
        new_weights,
        new_weights.astype(jnp.bfloat16),
    )


def solution(mesh):
    flat = P(("seq", "row"))
    tokens = P("row", "seq", None)
    return jax.shard_map(
        on_device,
        mesh=mesh,
        in_specs=(tokens, P("row", "seq"), tokens, flat, flat, flat),
        out_specs=(tokens, tokens, flat, flat, flat, flat, flat),
        check_vma=False,
    )
```
